32 devices in a mesh: dp: 8 (over z, y), tensor: 4 (over x, core).
Axes of the slice: x: 2, y: 2, z: 4, core: 2. Of those that a mesh axis runs over, the one named last changes fastest.
Arguments:
- patches: bfloat16 [24576, 384], P(('dp', 'tensor')), may hold values from -6 to 6
- classes: bfloat16 [96, 384], P(('dp', 'tensor')), may hold values from -6 to 6
- group_size: int32 [32], P(('dp', 'tensor')), may hold values from 196 to 576, as said below
- image_count: int32 [32], P(('dp', 'tensor')), may hold values from 1 to 3, as said below
- self_entry: bfloat16 [384, 1152], P('dp', 'tensor'), may hold values from -0.3125 to 0.3125
- self_exit: bfloat16 [384, 384], P('dp', 'tensor'), may hold values from -1.25 to 1.25
- self_expand: bfloat16 [384, 1536], P('dp', 'tensor'), may hold values from -0.3125 to 0.3125
- self_reduce: bfloat16 [1536, 384], P('tensor', 'dp'), may hold values from -0.15625 to 0.15625
- self_vectors: float32 [10, 384], replicated, may hold values from -0.75 to 1.625
- self_talking: float32 [17, 8], replicated, may hold values from -0.7 to 1.9
- self_offset: float32 [1536], replicated, may hold values from -1.5 to 1.5
- class_entry: bfloat16 [384, 1152], P('dp', 'tensor'), may hold values from -0.3125 to 0.3125
- class_exit: bfloat16 [384, 384], P('dp', 'tensor'), may hold values from -1.25 to 1.25
- class_expand: bfloat16 [384, 1536], P('dp', 'tensor'), may hold values from -0.3125 to 0.3125
- class_reduce: bfloat16 [1536, 384], P('tensor', 'dp'), may hold values from -0.15625 to 0.15625
- class_vectors: float32 [10, 384], replicated, may hold values from -0.75 to 1.625
- class_offset: float32 [1536], replicated, may hold values from -1.5 to 1.5
- patch_cotangent: bfloat16 [24576, 384], P(('dp', 'tensor')), may hold values from -6 to 6
- class_cotangent: bfloat16 [96, 384], P(('dp', 'tensor')), may hold values from -6 to 6
Outputs:
- patch_result: bfloat16 [24576, 384], P(('dp', 'tensor'))
- class_result: bfloat16 [96, 384], P(('dp', 'tensor'))
- patch_grad: float32 [24576, 384], P(('dp', 'tensor'))
- class_grad: float32 [96, 384], P(('dp', 'tensor'))
- grad_self_entry: float32 [384, 1152], P('dp', 'tensor')
- grad_self_exit: float32 [384, 384], P('dp', 'tensor')
- grad_self_expand: float32 [384, 1536], P('dp', 'tensor')
- grad_self_reduce: float32 [1536, 384], P('tensor', 'dp')
- grad_self_vectors: float32 [10, 384], replicated
- grad_self_talking: float32 [17, 8], replicated
- grad_self_offset: float32 [1536], replicated
- grad_class_entry: float32 [384, 1152], P('dp', 'tensor')
- grad_class_exit: float32 [384, 384], P('dp', 'tensor')
- grad_class_expand: float32 [384, 1536], P('dp', 'tensor')
- grad_class_reduce: float32 [1536, 384], P('tensor', 'dp')
- grad_class_vectors: float32 [10, 384], replicated
- grad_class_offset: float32 [1536], replicated
The draws below stay inside these ranges and needn't reach their ends.
Inputs may be any that keep to these rules, and one draw needn't show every extreme that they name: `group_size`: each device holds images of one size only. `image_count`: images fill a device's first rows in order, image j on rows j * s to (j + 1) * s - 1 for its image size s; at most 768 // s images, and the rows after them are padding.
All inputs are finite; a program needn't handle non-finite values.
Results may differ from the reference program's by a relative error of at most 0.018.
Values may be sent and summed in bfloat16 or wider, within the bound.
A program may use at most 256 MiB of HBM per device.

```python
import jax
import jax.numpy as jnp
import numpy as np
from jax import lax

D = 384
HEADS = 8
FF = 1536
HEAD_DIM = 48
ROWS = 768
SMALL_SIZE = 196
BIG_SIZE = 576
NVEC = 10
IMG_DEV = 3
PATCHES = 24576
SLOTS = 96


KINDS = np.array([0, 1, 1, 1, 1, 2, 0, 1, 1, 2])


def image_layout(key):
    key = jax.random.fold_in(key, 101)
    devices = PATCHES // ROWS
    first_key, second_key = jax.random.split(key)
    large = jax.random.randint(first_key, (devices,), 0, 2)
    large = large.at[0].set(0).at[1].set(1)
    sizes = jnp.where(large == 1, BIG_SIZE, SMALL_SIZE).astype(jnp.int32)
    limits = ROWS // sizes
    counts = jnp.maximum(limits - jax.random.randint(second_key, (devices,), 0, 2), 1)
    counts = counts.at[0].set(limits[0])
    return (sizes, counts.astype(jnp.int32))


def draw_group_size(key, part):
    return image_layout(key)[0]


def draw_image_count(key, part):
    return image_layout(key)[1]


def vector_rows(noise, level):
    kinds = jnp.asarray(KINDS)[:, None]
    return jnp.where(kinds == 0, 1.0 + 0.25 * noise, jnp.where(kinds == 1, 0.3 * noise, level)).astype(jnp.float32)


def draw_self_vectors(key, part):
    key = jax.random.fold_in(key, 7)
    noise_key, level_key = jax.random.split(key)
    noise = jnp.clip(jax.random.normal(noise_key, (NVEC, D)), -2.5, 2.5)
    level = jax.random.uniform(level_key, (NVEC, D), minval=0.4, maxval=1.2)
    return vector_rows(noise, level)


def draw_class_vectors(key, part):
    key = jax.random.fold_in(key, 8)
    noise_key, level_key = jax.random.split(key)
    noise = jnp.clip(jax.random.normal(noise_key, (NVEC, D)), -2.5, 2.5)
    level = jax.random.uniform(level_key, (NVEC, D), minval=0.4, maxval=1.2)
    return vector_rows(noise, level)


def draw_self_talking(key, part):
    key = jax.random.fold_in(key, 9)
    noise_key, diagonal_key = jax.random.split(key)
    noise = jnp.clip(jax.random.normal(noise_key, (2 * HEADS + 1, HEADS)), -2.5, 2.5)
    diagonal = jax.random.uniform(diagonal_key, (2 * HEADS + 1, HEADS), minval=0.8, maxval=1.2)
    place = jnp.arange(2 * HEADS + 1)[:, None]
    column = jnp.arange(HEADS)[None, :]
    on_diagonal = (place % HEADS == column) & (place < 2 * HEADS)
    mixing = jnp.where(on_diagonal, diagonal, 0.0) + jnp.where(place < 2 * HEADS, 0.25 * noise, 0.004 * noise)
    return mixing.astype(jnp.float32)


def shard_levels(key, extent, cuts, least, largest):
    level, own = 1.0, jax.random.fold_in(key, 6)
    for position, shards_of in cuts:
        steps = jnp.exp(jax.random.uniform(jax.random.fold_in(own, position), (shards_of,), jnp.float32, least / len(cuts), largest / len(cuts)))
        level = level * jnp.repeat(steps, extent[position] // shards_of).reshape([-1 if axis == position else 1 for axis in range(len(extent))])
    return level


def bell_draw(stream_key, dims, scale, most, pieces=(), kind=jnp.bfloat16):
    drawn = jax.random.normal(stream_key, dims, jnp.float32) * scale
    if len(pieces) > 0:
        drawn = shard_levels(stream_key, dims, pieces, -0.22, 0.18) * drawn
    return jnp.clip(drawn, min=-most, max=most).astype(kind)


def setup_inputs(seed: int = 0) -> dict:
    streams_of = jax.random.split(jax.random.key(seed), 20)
    patches = bell_draw(streams_of[0], (PATCHES, D), 1.0, 6.0, ((0, 32),))
    classes = bell_draw(streams_of[1], (SLOTS, D), 1.0, 6.0, ((0, 32),))
    group_size = draw_group_size(jax.random.fold_in(streams_of[19], 71), 0)
    image_count = draw_image_count(jax.random.fold_in(streams_of[19], 71), 0)
    self_entry = bell_draw(streams_of[4], (D, 3 * D), D ** -0.5, 0.3125, ((0, 8), (1, 4)))
    self_exit = bell_draw(streams_of[5], (D, D), (D // 16) ** -0.5, 1.25, ((0, 8), (1, 4)))
    self_expand = bell_draw(streams_of[6], (D, FF), D ** -0.5, 0.3125, ((0, 8), (1, 4)))
    self_reduce = bell_draw(streams_of[7], (FF, D), FF ** -0.5, 0.15625, ((0, 4), (1, 8)))
    self_vectors = draw_self_vectors(jax.random.fold_in(streams_of[19], 71), 0)
    self_talking = draw_self_talking(jax.random.fold_in(streams_of[19], 71), 0)
    self_offset = bell_draw(streams_of[10], (FF,), 0.3, 1.5, (), jnp.float32)
    class_entry = bell_draw(streams_of[11], (D, 3 * D), D ** -0.5, 0.3125, ((0, 8), (1, 4)))
    class_exit = bell_draw(streams_of[12], (D, D), (D // 16) ** -0.5, 1.25, ((0, 8), (1, 4)))
    class_expand = bell_draw(streams_of[13], (D, FF), D ** -0.5, 0.3125, ((0, 8), (1, 4)))
    class_reduce = bell_draw(streams_of[14], (FF, D), FF ** -0.5, 0.15625, ((0, 4), (1, 8)))
    class_vectors = draw_class_vectors(jax.random.fold_in(streams_of[19], 71), 0)
    class_offset = bell_draw(streams_of[16], (FF,), 0.3, 1.5, (), jnp.float32)
    patch_cotangent = bell_draw(streams_of[17], (PATCHES, D), 1.0, 6.0, ((0, 32),))
    class_cotangent = bell_draw(streams_of[18], (SLOTS, D), 1.0, 6.0, ((0, 32),))
    return dict(patches=patches, classes=classes, group_size=group_size, image_count=image_count, self_entry=self_entry, self_exit=self_exit, self_expand=self_expand, self_reduce=self_reduce, self_vectors=self_vectors, self_talking=self_talking, self_offset=self_offset, class_entry=class_entry, class_exit=class_exit, class_expand=class_expand, class_reduce=class_reduce, class_vectors=class_vectors, class_offset=class_offset, patch_cotangent=patch_cotangent, class_cotangent=class_cotangent)


EPSILON = 1e-06
NEGATIVE = -1e+30
HIGH = lax.Precision.HIGHEST

@jax.custom_vjp
def low(v):
    return lax.optimization_barrier(v.astype(jnp.bfloat16)).astype(jnp.float32)

@jax.custom_vjp
def low_back(v):
    return v

def low_keep(v):
    return (low(v), None)

def low_pass(kept, grad):
    return (grad,)

def back_keep(v):
    return (v, None)

def back_low(kept, grad):
    return (low(grad),)
low.defvjp(low_keep, low_pass)
low_back.defvjp(back_keep, back_low)

def normalize(rows, gain, shift):
    mean = lax.optimization_barrier(jnp.mean(rows, -1, keepdims=True))
    centered = rows - mean
    spread = lax.optimization_barrier(jnp.mean(centered * centered, -1, keepdims=True))
    return centered * lax.rsqrt(spread + EPSILON) * gain + shift

def product(left, right):
    return jnp.dot(left, right, precision=HIGH)

def layout(size, count):
    place = jnp.arange(ROWS, dtype=jnp.int32)
    return (place // size, place < count * size)

def feed_forward(rows, vectors, expand, reduce_value, offset):
    normed = low(normalize(rows, vectors[6], vectors[7]))
    hidden = low_back(product(normed, expand) + offset)
    active = low(jax.nn.gelu(hidden, approximate=False))
    lifted = low_back(product(active, reduce_value) + vectors[8])
    return rows + vectors[9] * lifted

def self_block(rows, sizes, counts, entry, exit_weight, vectors, talking):
    scale = HEAD_DIM ** (-0.5)
    normed = low(normalize(rows, vectors[0], vectors[1]))
    bias = jnp.concatenate([vectors[2], jnp.zeros((D,), jnp.float32), vectors[3]])
    triple = low(low_back(product(normed, entry) + bias))
    per_device = triple.reshape(PATCHES // ROWS, ROWS, 3 * D)
    mix_pre = talking[:HEADS]
    mix_post = talking[HEADS:2 * HEADS]
    post_bias = talking[2 * HEADS]

    def attend(item):
        block, size, count = item
        segment, live = layout(size, count)
        place = jnp.arange(ROWS, dtype=jnp.int32)
        allowed = live[:, None] & live[None, :] & (segment[:, None] == segment[None, :]) | (place[:, None] == place[None, :])
        split = block.reshape(ROWS, 3, HEADS, HEAD_DIM)
        scores = jnp.einsum('qhe,khe->hqk', split[:, 0], split[:, 1], precision=HIGH) * scale
        scores = low_back(scores)
        mixed = jnp.einsum('gh,hqk->gqk', mix_pre, scores, precision=HIGH)
        mixed = jnp.where(allowed[None], mixed, NEGATIVE)
        top = lax.optimization_barrier(jnp.max(mixed, -1, keepdims=True))
        raised = jnp.exp(mixed - top)
        probs = raised / lax.optimization_barrier(jnp.sum(raised, -1, keepdims=True))
        posted = jnp.einsum('gh,hqk->gqk', mix_post, probs, precision=HIGH) + post_bias[:, None, None]
        weights = low(jnp.where(allowed[None], posted, 0.0))
        out = jnp.einsum('hqk,khe->qhe', weights, split[:, 2], precision=HIGH)
        return out.reshape(ROWS, D)
    outs = lax.map(jax.checkpoint(attend), (per_device, sizes, counts))
    attended = low(low_back(outs.reshape(PATCHES, D)))
    branch = low_back(product(attended, exit_weight) + vectors[4])
    return rows + vectors[5] * branch

def class_block(rows, classes, sizes, counts, entry, exit_weight, vectors):
    devices = PATCHES // ROWS
    scale = HEAD_DIM ** (-0.5)
    normed_rows = low(normalize(rows, vectors[0], vectors[1]))
    normed_class = low(normalize(classes, vectors[0], vectors[1]))
    pair_bias = jnp.concatenate([jnp.zeros((D,), jnp.float32), vectors[3]])
    queries = low(low_back(product(normed_class, entry[:, :D]) + vectors[2]))
    row_pairs = low(low_back(product(normed_rows, entry[:, D:]) + pair_bias))
    class_pairs = low(low_back(product(normed_class, entry[:, D:]) + pair_bias))
    queries = queries.reshape(devices, IMG_DEV, HEADS, HEAD_DIM)
    row_pairs = row_pairs.reshape(devices, ROWS, 2, HEADS, HEAD_DIM)
    class_pairs = class_pairs.reshape(devices, IMG_DEV, 2, HEADS, HEAD_DIM)
    place = jnp.arange(ROWS, dtype=jnp.int32)
    slot_ids = jnp.arange(IMG_DEV, dtype=jnp.int32)
    segment = place[None, :] // sizes[:, None]
    live = place[None, :] < (counts * sizes)[:, None]
    allowed = live[:, None, :] & (segment[:, None, :] == slot_ids[None, :, None])
    own = lax.optimization_barrier(jnp.sum(queries * class_pairs[:, :, 0], -1)) * scale
    others = jnp.einsum('dche,drhe->dhcr', queries, row_pairs[:, :, 0], precision=HIGH) * scale
    scores = low_back(jnp.concatenate([jnp.transpose(own, (0, 2, 1))[..., None], others], -1))
    allowed_all = jnp.concatenate([jnp.ones((devices, IMG_DEV, 1), dtype=bool), allowed], -1)[:, None]
    masked = jnp.where(allowed_all, scores, NEGATIVE)
    top = lax.optimization_barrier(jnp.max(masked, -1, keepdims=True))
    raised = jnp.exp(masked - top)
    probs = low(raised / lax.optimization_barrier(jnp.sum(raised, -1, keepdims=True)))
    own_part = jnp.transpose(probs[..., 0], (0, 2, 1))[..., None] * class_pairs[:, :, 1]
    other_part = jnp.einsum('dhcr,drhe->dche', probs[..., 1:], row_pairs[:, :, 1], precision=HIGH)
    attended = low(low_back((own_part + other_part).reshape(devices * IMG_DEV, D)))
    branch = low_back(product(attended, exit_weight) + vectors[4])
    return classes + vectors[5] * branch

def forward(values, sizes, counts):
    patches, classes, self_entry, self_exit, self_expand, self_reduce, self_vectors, self_talking, self_offset, class_entry, class_exit, class_expand, class_reduce, class_vectors, class_offset = values
    middle = self_block(patches, sizes, counts, self_entry, self_exit, self_vectors, self_talking)
    first = feed_forward(middle, self_vectors, self_expand, self_reduce, self_offset)
    class_middle = class_block(first, classes, sizes, counts, class_entry, class_exit, class_vectors)
    second = feed_forward(class_middle, class_vectors, class_expand, class_reduce, class_offset)
    return (first, second)

def reference(patches, classes, group_size, image_count, self_entry, self_exit, self_expand, self_reduce, self_vectors, self_talking, self_offset, class_entry, class_exit, class_expand, class_reduce, class_vectors, class_offset, patch_cotangent, class_cotangent):
    floats = (patches, classes, self_entry, self_exit, self_expand, self_reduce, self_vectors, self_talking, self_offset, class_entry, class_exit, class_expand, class_reduce, class_vectors, class_offset)
    floats = tuple((value.astype(jnp.float32) for value in floats))

    def run(*values):
        return forward(values, group_size, image_count)
    (first, second), pullback = jax.vjp(run, *floats)
    place = jnp.arange(ROWS, dtype=jnp.int32)
    live = (place[None, :] < (image_count * group_size)[:, None]).reshape(PATCHES, 1)
    live_cotangent = jnp.where(live, patch_cotangent.astype(jnp.float32), 0.0)
    grads = pullback((live_cotangent, class_cotangent.astype(jnp.float32)))
    return (first.astype(jnp.bfloat16), second.astype(jnp.bfloat16), grads[0], grads[1], grads[2], grads[3], grads[4], grads[5], grads[6], grads[7], grads[8], grads[9], grads[10], grads[11], grads[12], grads[13], grads[14])
```

```python
import functools

import jax
import jax.numpy as jnp
from jax import lax
from jax.experimental import pallas as pl
from jax.experimental.pallas import tpu as pltpu
from jax.sharding import PartitionSpec as P

HEADS = 8
EPSILON = 1e-06
NEGATIVE = -1e30
ROOT_HALF = 0.7071067811865476
ROOT_TWO_PI = 2.5066282746310002
WIDE = jnp.float32
LOW = jnp.bfloat16

WIDTH = 384
DEPTH = WIDTH // HEADS
ROWS = 768
FF = 1536
PARTS = 4
COLS = 3 * WIDTH // PARTS
TILE = 128
SPAN = HEADS * TILE
HALVES = (slice(0, SPAN // 2), slice(SPAN // 2, SPAN))
WIDE_HALVES = (slice(0, FF // 2), slice(FF // 2, FF))
SHARD = 48
DEPS = 4
STEPS = ROWS // TILE
TOGETHER = 1
KEYS = ROWS + 128
DENSE = 384
PAIRS = HEADS * 8


def nn(a, b):
    return lax.dot_general(a, b, (((1,), (0,)), ((), ())), preferred_element_type=WIDE)


def nt(a, b):
    return lax.dot_general(a, b, (((1,), (1,)), ((), ())), preferred_element_type=WIDE)


def iota(shape, dim):
    return lax.broadcasted_iota(jnp.int32, shape, dim)


def rows_at(i, size):
    return pl.ds(pl.multiple_of(i * size, size), size)


def normalize(x, gain, shift):
    mean = jnp.mean(x, -1, keepdims=True)
    centered = x - mean
    inverse = lax.rsqrt(jnp.mean(centered * centered, -1, keepdims=True) + EPSILON)
    unit = centered * inverse
    return unit * gain + shift, unit, inverse


def keep_stats(r, k, rows, x, inverse):
    r.stats[rows, 2 * k : 2 * k + 1] = jnp.mean(x, -1, keepdims=True)
    r.stats[rows, 2 * k + 1 : 2 * k + 2] = inverse


def unit_of(r, k, rows, x):
    inverse = r.stats[rows, 2 * k + 1 : 2 * k + 2]
    return (x - r.stats[rows, 2 * k : 2 * k + 1]) * inverse, inverse


def normalize_back(grad, gain, unit, inverse):
    scaled = grad * gain
    inner = jnp.mean(scaled * unit, -1, keepdims=True)
    return inverse * (scaled - jnp.mean(scaled, -1, keepdims=True) - unit * inner)


def by_head(x):
    return jnp.sum(x.reshape(HEADS, DEPTH, x.shape[-1]), 1)


def total(x):
    return jnp.sum(x, 0, keepdims=True)


def smooth(hidden):
    cdf = 0.5 * (1.0 + lax.erf(hidden * ROOT_HALF))
    slope = cdf + hidden * jnp.exp(-0.5 * hidden * hidden) * (1.0 / ROOT_TWO_PI)
    return (hidden * cdf).astype(LOW), slope.astype(LOW)


def each(count, together, step, points):
    def some(i, c):
        for k in range(together):

            def at(where):
                for key, todo in points.items():
                    t, place = divmod(key, 2)
                    if place == where and t % together == k:
                        pl.when(i == t // together)(todo)

            step(i * together + k, at)
        return c

    lax.fori_loop(0, count // together, some, 0)


class Refs:
    def __init__(self, **refs):
        self.__dict__.update(refs)


SCRATCH = dict(
    cols=((WIDTH, 128), WIDE),
    pad=((128, 128), WIDE),
    patches=((ROWS, WIDTH), LOW),
    cot=((ROWS, WIDTH), LOW),
    result=((ROWS, WIDTH), LOW),
    grad=((ROWS, WIDTH), WIDE),
    n1=((ROWS, WIDTH), LOW),
    stats=((ROWS, 128), WIDE),
    went=((3 * WIDTH, WIDTH), LOW),
    wout=((WIDTH, WIDTH), LOW),
    wback=((WIDTH, WIDTH), LOW),
    wfull=((WIDTH, 3 * WIDTH), LOW),
    qt=((WIDTH, ROWS), LOW),
    kext=((ROWS, 512), LOW),
    kt=((WIDTH, ROWS), LOW),
    vext=((ROWS, 512), LOW),
    vt=((WIDTH, ROWS), LOW),
    hot=((ROWS, 128), LOW),
    hott=((8, ROWS), WIDE),
    vsum=((WIDTH, 128), WIDE),
    gsum=((WIDTH, 128), WIDE),
    qm=((512, SPAN), LOW),
    qn=((WIDTH, SPAN), LOW),
    gm=((ROWS, SPAN), LOW),
    et=((STEPS, ROWS, SPAN), LOW),
    un=((STEPS, WIDTH, SPAN), LOW),
    linv=((STEPS, 1, SPAN), WIDE),
    attt=((WIDTH, ROWS), LOW),
    middle=((ROWS, WIDTH), WIDE),
    branch1=((ROWS, WIDTH), LOW),
    branch2=((ROWS, WIDTH), WIDE),
    n2t=((WIDTH, ROWS), LOW),
    act=((ROWS, FF), LOW),
    slope=((ROWS, FF), LOW),
    next=((KEYS, WIDTH), LOW),
    wout_c=((WIDTH, WIDTH), LOW),
    small8=((8, WIDTH), WIDE),
    cot8=((8, WIDTH), WIDE),
    both=((KEYS, 128), LOW),
    qkwv=((128, WIDTH), LOW),
    d1t=((WIDTH, ROWS), LOW),
    d2t=((WIDTH, ROWS), LOW),
    dot=((WIDTH, ROWS), LOW),
    gwout=((WIDTH, WIDTH), WIDE),
    offset=((1, FF), WIDE),
    dvt=((WIDTH, ROWS), WIDE),
    dkt=((WIDTH, ROWS), WIDE),
    accp=((HEADS, HEADS, TILE), WIDE),
    accq=((HEADS, HEADS, TILE), WIDE),
    dtr=((3 * WIDTH, ROWS), LOW),
)


def block_of(w, j):
    return w[j].reshape(WIDTH, w.shape[-1])


def whole_of(w):
    return w[...].reshape(WIDTH, FF)


def as_block(x):
    return x.reshape(DEPS, 2, SHARD, x.shape[-1])


def unpack_weights(wa, went, wout):
    for j in range(PARTS):
        block = block_of(wa, j).T
        went[COLS * j : COLS * (j + 1), :] = block[:COLS]
        wout[96 * j : 96 * (j + 1), :] = block[COLS:]

def columns(r):
    r.pad[...] = jnp.zeros((128, 128), WIDE)
    r.pad[0:8, 0:17] = r.talking[...]
    turned = r.pad[...]
    talk = turned.T
    turned = turned[0:8]
    moved = pltpu.roll(talk, 8, 1)[8:16]
    lane = iota((8, 128), 1)
    alone = jnp.sum(talk[8:16], 1, keepdims=True) + turned[:, 16:17]
    base = jnp.where(lane < 8, turned * DEPTH ** (-0.5), moved)
    base = jnp.where(lane == 16, turned, base)
    base = jnp.where(lane == 19, alone, base)
    turned = r.vec[0:8, :].T
    lane = iota((DEPTH, 128), 1)
    for h in range(HEADS):
        rows = slice(DEPTH * h, DEPTH * (h + 1))
        x = jnp.broadcast_to(base[h : h + 1], (DEPTH, 128))
        x = jnp.where(lane == 17, turned[rows, 2:3], x)
        r.cols[rows, :] = jnp.where(lane == 18, turned[rows, 3:4], x)


def masks(r):
    size, images = r.size[0], r.images[0]
    place = iota((ROWS, 128), 0)
    which = iota((ROWS, 128), 1)
    inside = (place >= which * size) & (place < which * size + size) & (which < images)
    r.hot[...] = jnp.where(inside, 1.0, 0.0).astype(LOW)
    r.kext[:, WIDTH:] = jnp.where(inside | (which >= 3), 0.0, NEGATIVE).astype(LOW)
    r.vext[:, WIDTH:] = jnp.where(which < 2, 1.0, 0.0).astype(LOW)
    place = iota((8, ROWS), 1)
    which = iota((8, ROWS), 0)
    inside = (place >= which * size) & (place < which * size + size) & (which < images)
    r.hott[...] = jnp.where(inside, 1.0, 0.0)


def norm_first(r):
    gain, shift = r.vec[0:1, :], r.vec[1:2, :]

    def norm_step(i, c):
        rows = rows_at(i, DENSE)
        x = r.patches[rows, :].astype(WIDE)
        normed, unit, inverse = normalize(x, gain, shift)
        r.n1[rows, :] = normed.astype(LOW)
        keep_stats(r, 0, rows, x, inverse)
        return c

    lax.fori_loop(0, ROWS // DENSE, norm_step, 0)


def project(r):
    unpack_weights(r.wa, r.went, r.wout)

    def step(i, c):
        rows = rows_at(i, DENSE)
        normed = r.n1[rows, :]
        turned = nt(r.went[...], normed)
        r.qt[:, rows] = (turned[0:WIDTH] + r.cols[:, 17:18]).astype(LOW)
        r.kt[:, rows] = turned[WIDTH : 2 * WIDTH].astype(LOW)
        r.vt[:, rows] = (turned[2 * WIDTH :] + r.cols[:, 18:19]).astype(LOW)
        both = nt(normed, r.went[WIDTH:, :])
        r.kext[rows, 0:WIDTH] = both[:, 0:WIDTH].astype(LOW)
        r.vext[rows, 0:WIDTH] = (both[:, WIDTH:] + r.vec[3:4, :]).astype(LOW)
        return c

    lax.fori_loop(0, ROWS // DENSE, step, 0)
    r.vsum[...] = nn(r.vt[...], r.hot[...])
    r.wback[...] = r.wout[...].T
    r.wfull[...] = r.went[...].T


def attend(r, points):
    def step(t, at):
        at(0)
        rows = rows_at(t, TILE)
        q = r.qt[:, rows].astype(WIDE)
        hot = r.hott[:, rows]
        hot_rows = jnp.concatenate([hot, jnp.zeros((120, TILE), WIDE)], 0).astype(LOW)
        for g in range(HEADS):
            r.qm[0:WIDTH, TILE * g : TILE * (g + 1)] = (q * r.cols[:, g : g + 1]).astype(LOW)
            r.qm[WIDTH:, TILE * g : TILE * (g + 1)] = hot_rows
        own = r.vt[:, rows].astype(WIDE)
        att = r.cols[:, 16:17] * (
            r.vsum[:, 0:1] * hot[0:1] + r.vsum[:, 1:2] * hot[1:2] + r.vsum[:, 2:3] * hot[2:3]
        )
        for half in HALVES:
            scores = nn(r.kext[...], r.qm[:, half])
            raised = jnp.exp(scores - jnp.max(scores, 0, keepdims=True))
            r.linv[t, :, half] = 1.0 / jnp.sum(raised, 0, keepdims=True)
            r.et[t, :, half] = raised.astype(LOW)
        at(1)
        for i, half in enumerate(HALVES):
            mean = nn(r.vt[...], r.et[t, :, half]) * r.linv[t, :, half]
            r.un[t, :, half] = mean.astype(LOW)
            for k in range(HEADS // 2):
                h = HEADS // 2 * i + k
                att = att + r.cols[:, 8 + h : 9 + h] * mean[:, TILE * k : TILE * (k + 1)]
        live = (hot[0:1] + hot[1:2] + hot[2:3]) > 0.5
        att = jnp.where(live, att, r.cols[:, 19:20] * own).astype(LOW)
        r.attt[:, rows] = att
        branch = nt(att.T, r.wout[...]) + r.vec[4:5, :]
        r.branch1[rows, :] = branch.astype(LOW)
        r.middle[rows, :] = r.patches[rows, :].astype(WIDE) + r.vec[5:6, :] * branch

    each(STEPS, TOGETHER, step, points)


def feed(r, points):
    def step(i, at):
        at(0)
        rows = rows_at(i, DENSE)
        middle = r.middle[rows, :]
        normed, unit, inverse = normalize(middle, r.vec[6:7, :], r.vec[7:8, :])
        keep_stats(r, 1, rows, middle, inverse)
        normed = normed.astype(LOW)
        r.n2t[:, rows] = normed.T
        hidden = [nn(normed, whole_of(r.we)[:, half]) + r.off[half].reshape(1, FF // 2) for half in WIDE_HALVES]
        for half, part in zip(WIDE_HALVES, hidden, strict=True):
            active, slope = smooth(part)
            r.act[rows, half] = active
            r.slope[rows, half] = slope
        at(1)
        lifted = nt(whole_of(r.wr), r.act[rows, :]).T
        branch = lifted + r.vec[8:9, :]
        r.branch2[rows, :] = branch
        first = middle + r.vec[9:10, :] * branch
        r.result[rows, :] = first.astype(LOW)
        normed, unit, inverse = normalize(first, r.vec_c[0:1, :], r.vec_c[1:2, :])
        r.next[rows, :] = normed.astype(LOW)
        keep_stats(r, 2, rows, first, inverse)

    each(ROWS // DENSE, 1, step, points)


def classes(r):
    v = lambda k: r.vec_c[k : k + 1, :]
    scale = DEPTH ** (-0.5)
    unpack_weights(r.wa_c, r.went, r.wout_c)
    wq, wk, wv = (r.went[WIDTH * k : WIDTH * (k + 1), :] for k in range(3))
    r.small8[...] = jnp.zeros((8, WIDTH), WIDE)
    r.cot8[...] = jnp.zeros((8, WIDTH), WIDE)
    r.small8[0:3, :] = r.classes[...].astype(WIDE)
    r.cot8[0:3, :] = r.class_cot[...].astype(WIDE)
    tokens = r.small8[...]
    normed, unit, inverse = normalize(tokens, v(0), v(1))
    low = normed.astype(LOW)
    valid = iota((128, WIDTH), 0) < 3
    r.next[ROWS:, :] = jnp.where(
        valid, jnp.concatenate([normed, jnp.zeros((120, WIDTH), WIDE)], 0), 0.0
    ).astype(LOW)
    head_of = iota((PAIRS, WIDTH), 1) // DEPTH
    own_head = head_of == iota((PAIRS, WIDTH), 0) // 8

    def spread(x):
        return jnp.where(own_head, jnp.concatenate([x] * HEADS, 0), 0.0)

    def gather_heads(x):
        x = jnp.where(own_head, x, 0.0)
        out = x[0:8]
        for h in range(1, HEADS):
            out = out + x[8 * h : 8 * (h + 1)]
        return out

    queries = (nt(low, wq) + v(2)).astype(LOW)
    qexp = spread(queries.astype(WIDE))
    qk = (nn(qexp.astype(LOW), wk) * scale).astype(LOW)
    keys = r.next[...]
    scores = nt(qk, keys)
    size, images = r.size[0], r.images[0]
    slot = iota((PAIRS, KEYS), 0) & 7
    place = iota((PAIRS, KEYS), 1)
    allowed = (place >= slot * size) & (place < slot * size + size) & (slot < images)
    allowed = allowed | (place == slot + ROWS)
    scores = jnp.where(allowed, scores, NEGATIVE)
    raised = jnp.exp(scores - jnp.max(scores, -1, keepdims=True))
    probs = raised / jnp.sum(raised, -1, keepdims=True)
    probs_low = probs.astype(LOW)
    mass = jnp.sum(probs_low.astype(WIDE), -1, keepdims=True)
    z = nn(probs_low, keys).astype(LOW)
    attended = gather_heads(nt(z, wv) + mass * v(3)).astype(LOW)
    branch = nt(attended, r.wout_c[...]) + v(4)
    middle = tokens + v(5) * branch
    normed2, unit2, inverse2 = normalize(middle, v(6), v(7))
    low2 = normed2.astype(LOW)
    expand, reduce = whole_of(r.we_c), whole_of(r.wr_c)
    hidden = nn(low2, expand) + r.off_c[...].reshape(1, FF)
    active, slope = smooth(hidden)
    lifted = nt(active, reduce)
    branch2 = lifted + v(8)
    second = middle + v(9) * branch2
    r.class_result[...] = second[0:3].astype(LOW)
    grad = r.cot8[...]
    grad_scale2 = total(grad * branch2)
    delta2 = (v(9) * grad).astype(LOW)
    grad_bias2 = total(delta2.astype(WIDE))
    low2_t, delta2_t = low2.astype(WIDE).T.astype(LOW), delta2.astype(WIDE).T.astype(LOW)
    grad_hidden = (nn(delta2, reduce) * slope.astype(WIDE)).astype(LOW)
    off = total(grad_hidden.astype(WIDE))
    for j in range(PARTS):
        r.early[0, 20 + j : 21 + j, :] = off[:, WIDTH * j : WIDTH * (j + 1)]
    back = nt(grad_hidden, expand)
    r.we_c[...] = as_block(nn(low2_t, grad_hidden).astype(LOW))
    r.wr_c[...] = as_block(nn(delta2_t, active).astype(LOW))
    grad_gain2, grad_shift2 = total(back * unit2), total(back)
    grad = grad + normalize_back(back, v(6), unit2, inverse2)
    grad_scale = total(grad * branch)
    delta = (v(5) * grad).astype(LOW)
    grad_bias = total(delta.astype(WIDE))
    gatt = nn(delta, r.wout_c[...]).astype(LOW)
    dexp = spread(gatt.astype(WIDE))
    wide_v = nn(dexp.astype(LOW), wv).astype(LOW)
    gp = nt(wide_v, keys)
    ds = (probs * (gp - jnp.sum(gp * probs, -1, keepdims=True))).astype(LOW)
    y = nn(ds, keys).astype(LOW)
    gq = (gather_heads(nt(y, wk)) * scale).astype(LOW)
    both = jnp.concatenate([ds.astype(WIDE), probs_low.astype(WIDE)], 0).T.astype(LOW)
    r.both[...] = both
    r.qkwv[...] = jnp.concatenate([qk, wide_v], 0)
    grad_normed = nn(both[ROWS:, :], r.qkwv[...])[0:8] + nn(gq, wq)
    r.class_grad[...] = (grad + normalize_back(grad_normed, v(0), unit, inverse))[0:3]
    valid8 = iota((8, WIDTH), 0) < 3
    grad_normed = jnp.where(valid8, grad_normed, 0.0)
    gq_t = gq.astype(WIDE).T.astype(LOW)
    grad_q = nn(gq_t, low)
    grad_k = nn((qexp * scale).T.astype(LOW), y)
    grad_v = nn(dexp.T.astype(LOW), z)
    grad_out = nn(delta.astype(WIDE).T.astype(LOW), attended)
    whole = jnp.concatenate([grad_q, grad_k, grad_v], 0)
    for j in range(PARTS):
        block = jnp.concatenate(
            [whole[COLS * j : COLS * (j + 1)], grad_out[96 * j : 96 * (j + 1)]], 0
        )
        r.wa_c[j] = as_block(block.T.astype(LOW))
    grad_vb = total(jnp.where(own_head, mass * dexp, 0.0))
    r.early[0, 10:20, :] = jnp.concatenate(
        [
            total(grad_normed * unit),
            total(grad_normed),
            total(gq.astype(WIDE)),
            grad_vb,
            grad_bias,
            grad_scale,
            grad_gain2,
            grad_shift2,
            grad_bias2,
            grad_scale2,
        ],
        0,
    )


def feed_back(r, points):
    size, images = r.size[0], r.images[0]
    r.early[0, 0:10, :] = jnp.zeros((10, WIDTH), WIDE)
    r.offset[...] = jnp.zeros((1, FF), WIDE)

    def add(k, x):
        r.early[0, k - 4 : k - 3, :] += total(x)

    def step(i, at):
        at(0)
        rows = rows_at(i, DENSE)
        branch2 = r.branch2[rows, :]
        unitc, inversec = unit_of(r, 2, rows, r.middle[rows, :] + r.vec[9:10, :] * branch2)
        dn = nn(r.both[rows, :], r.qkwv[...])
        add(14, dn * unitc)
        add(15, dn)
        grad = normalize_back(dn, r.vec_c[0:1, :], unitc, inversec)
        place = iota((DENSE, WIDTH), 0) + i * DENSE
        grad = grad + jnp.where(place < size * images, r.cot[rows, :].astype(WIDE), 0.0)
        add(9, grad * branch2)
        delta = (r.vec[9:10, :] * grad).astype(LOW)
        add(8, delta.astype(WIDE))
        r.d2t[:, rows] = delta.T
        grad_hidden = [
            (nn(delta, whole_of(r.wr)[:, half]) * r.slope[rows, half].astype(WIDE)).astype(LOW)
            for half in WIDE_HALVES
        ]
        for half, part in zip(WIDE_HALVES, grad_hidden, strict=True):
            r.slope[rows, half] = part
            r.offset[:, half] += total(part.astype(WIDE))
        at(1)
        back = nt(whole_of(r.we), r.slope[rows, :]).T
        unit, inverse = unit_of(r, 1, rows, r.middle[rows, :])
        add(6, back * unit)
        add(7, back)
        grad = grad + normalize_back(back, r.vec[6:7, :], unit, inverse)
        r.grad[rows, :] = grad
        add(5, grad * r.branch1[rows, :].astype(WIDE))
        delta = (r.vec[5:6, :] * grad).astype(LOW)
        add(4, delta.astype(WIDE))
        r.d1t[:, rows] = delta.T
        r.dot[:, rows] = nt(r.wback[...], delta).astype(LOW)

    each(ROWS // DENSE, 1, step, points)
    for half in WIDE_HALVES:
        r.we[:, :, :, half] = as_block(nn(r.n2t[...], r.slope[:, half]).astype(LOW))
        r.wr[:, :, :, half] = as_block(nn(r.d2t[...], r.act[:, half]).astype(LOW))
    for j in range(PARTS):
        r.early[0, 6 + j : 7 + j, :] = r.offset[:, WIDTH * j : WIDTH * (j + 1)]
    r.gwout[...] = nt(r.d1t[...], r.attt[...])


def attend_back(r, points):
    r.dvt[...] = jnp.zeros((WIDTH, ROWS), WIDE)
    r.dkt[...] = jnp.zeros((WIDTH, ROWS), WIDE)
    r.accp[...] = jnp.zeros((HEADS, HEADS, TILE), WIDE)
    r.accq[...] = jnp.zeros((HEADS, HEADS, TILE), WIDE)

    def step(t, at):
        at(0)
        rows = rows_at(t, TILE)
        grad = r.dot[:, rows].astype(WIDE)
        inverse = r.linv[t]
        place = iota((128, TILE), 0)
        for h in range(HEADS):
            part = slice(TILE * h, TILE * (h + 1))
            post = r.cols[:, 8 + h : 9 + h]
            w = grad * r.un[t, :, part].astype(WIDE)
            r.accp[h] += by_head(w)
            minus = -inverse[:, part] * total(post * w)
            high = minus.astype(LOW).astype(WIDE)
            r.qm[0:WIDTH, part] = (grad * post * inverse[:, part]).astype(LOW)
            extra = jnp.where(place == 0, high, jnp.where(place == 1, minus - high, 0.0))
            r.qm[WIDTH:, part] = extra.astype(LOW)
        q = r.qt[:, rows].astype(WIDE)
        for g in range(HEADS):
            r.qn[:, TILE * g : TILE * (g + 1)] = (q * r.cols[:, g : g + 1]).astype(LOW)
        for half in HALVES:
            gp = nn(r.vext[...], r.qm[:, half])
            r.gm[:, half] = (r.et[t, :, half].astype(WIDE) * gp).astype(LOW)
        r.dvt[...] += nt(r.qm[0:WIDTH, :], r.et[t])
        at(1)
        r.dkt[...] += nt(r.qn[...], r.gm[...])
        dq = jnp.zeros((WIDTH, TILE), WIDE)
        for i, half in enumerate(HALVES):
            y = nn(r.kt[...], r.gm[:, half])
            for k in range(HEADS // 2):
                g = HEADS // 2 * i + k
                part = y[:, TILE * k : TILE * (k + 1)]
                dq = dq + r.cols[:, g : g + 1] * part
                r.accq[g] += by_head(q * part)
        r.dtr[0:WIDTH, rows] = dq.astype(LOW)

    each(STEPS, TOGETHER, step, points)
    r.gsum[...] = nn(r.dot[...], r.hot[...])
    bias = r.cols[:, 16:17]
    for k in range(3):
        r.dvt[...] += (bias * r.gsum[:, k : k + 1]) * r.hott[k : k + 1, :]
    r.dtr[WIDTH : 2 * WIDTH, :] = r.dkt[...].astype(LOW)
    r.dtr[2 * WIDTH :, :] = r.dvt[...].astype(LOW)


def talking_back(r):
    lane = iota((HEADS, 128), 1)

    def lanes_sum(x):
        return jnp.sum(x, -1, keepdims=True)

    out = jnp.where(lane == 2 * HEADS, lanes_sum(by_head(r.gsum[...] * r.vsum[...])), 0.0)
    for h in range(HEADS):
        out = out + jnp.where(lane == h, lanes_sum(r.accq[h]) * DEPTH ** (-0.5), 0.0)
        out = out + jnp.where(lane == HEADS + h, lanes_sum(r.accp[h]), 0.0)
    r.late[0, :, WIDTH:] = out


def project_back_weights(r, part):
    rows = slice(128 * part, min(128 * part + 128, COLS))
    for j in range(PARTS):
        block = nn(r.dtr[COLS * j + rows.start : COLS * j + rows.stop, :], r.n1[...])
        if part == 2:
            block = jnp.concatenate([block, r.gwout[96 * j : 96 * (j + 1), :]], 0)
        block = block.T.astype(LOW).reshape(DEPS, 2, SHARD, 128)
        r.wa[j, :, :, :, 128 * part : 128 * part + 128] = block


def project_back(r):
    ones = jnp.ones((8, ROWS), LOW)
    r.late[0, 2:3, 0:WIDTH] = nt(ones, r.dtr[0:WIDTH, :])[0:1]
    r.late[0, 3:4, 0:WIDTH] = nt(ones, r.dtr[2 * WIDTH :, :])[0:1]

    def step(i, c):
        rows = rows_at(i, DENSE)
        back = nn(r.wfull[...], r.dtr[:, rows]).T
        unit, inverse = unit_of(r, 0, rows, r.patches[rows, :].astype(WIDE))
        r.late[0, 0:1, 0:WIDTH] += total(back * unit)
        r.late[0, 1:2, 0:WIDTH] += total(back)
        r.grad[rows, :] = r.grad[rows, :] + normalize_back(
            back, r.vec[0:1, :], unit, inverse
        )
        return c

    lax.fori_loop(0, ROWS // DENSE, step, 0)


MESH = pl.DeviceIdType.MESH
CHUNKS = ("a", "e", "r", "ac", "ec", "rc")
SHAPE = (PARTS, DEPS, 2, SHARD, WIDTH)
JOINED = (DEPS, 2, SHARD, PARTS * WIDTH)


class Place:
    def __init__(self, inner):
        self.inner = inner
        dp, tensor = lax.axis_index("dp"), lax.axis_index("tensor")
        self.rest = (lax.rem(dp, inner[0]), lax.rem(tensor, inner[1]))
        dp, tensor = dp // inner[0], tensor // inner[1]
        self.z, self.y = dp // 2, lax.rem(dp, 2)
        self.x, self.core = tensor // 2, lax.rem(tensor, 2)
        self.a = self.x + self.core * (self.y - self.x)
        self.b = self.y + self.core * (self.x - self.y)

    def xy(self, a, b):
        return a + self.core * (b - a), b + self.core * (a - b)

    def device(self, z, y, x, core):
        return (
            (z * 2 + y) * self.inner[0] + self.rest[0],
            (x * 2 + core) * self.inner[1] + self.rest[1],
        )

    def around(self, d):
        return lax.rem(self.z + d, DEPS)

    def z_peer(self, d):
        return self.device(self.around(d), self.y, self.x, self.core)

    def a_peer(self):
        x, y = self.xy(1 - self.a, self.b)
        return self.device(self.z, y, x, self.core)

    def b_peer(self):
        x, y = self.xy(self.a, 1 - self.b)
        return self.device(self.z, y, x, self.core)

    def x_peer(self):
        return self.device(self.z, self.y, 1 - self.x, self.core)

    def y_peer(self):
        return self.device(self.z, 1 - self.y, self.x, self.core)

    def plane_peer(self, a, b):
        x, y = self.xy(self.a + a * (1 - 2 * self.a), self.b + b * (1 - 2 * self.b))
        return self.device(self.z, y, x, self.core)

    def near(self, k):
        x = 1 - self.x if k & 4 else self.x
        y = 1 - self.y if k & 2 else self.y
        return self.device(self.z, y, x, 1 - self.core if k & 1 else self.core)

    def core_peer(self):
        return self.device(self.z, self.y, self.x, 1 - self.core)


def remote(src, dst, sems, k, device):
    return pltpu.make_async_remote_copy(
        src_ref=src,
        dst_ref=dst,
        send_sem=sems[0].at[k],
        recv_sem=sems[1].at[k],
        device_id=device,
        device_id_type=MESH,
    )


def part_of(w, j, z=slice(None), y=slice(None)):
    if len(w.shape) == 5:
        return w.at[j, z, y]
    return w.at[z, y, :, pl.ds(pl.multiple_of(j * WIDTH, 128), WIDTH)]


class Gather:
    def __init__(self, place, w, sems, base):
        self.p, self.w, self.sems, self.base = place, w, sems, base

    def copy(self, k, where, device):
        ref = part_of(self.w, *where)
        return remote(ref, ref, self.sems, self.base + k, device)

    def z_copies(self, back):
        p = self.p
        out = []
        for d in (1, 2, 3):
            z = p.around(DEPS - d) if back else p.z
            out.append(self.copy(d - 1, (p.x * 2 + p.core, z, p.y), p.z_peer(d)))
        return out

    def b_copies(self, back):
        p = self.p
        x, y = p.xy(p.a, 1 - p.b) if back else (p.x, p.y)
        return [self.copy(3, (x * 2 + p.core, slice(None), y), p.b_peer())]

    def a_copies(self, back):
        p = self.p
        a = 1 - p.a if back else p.a
        out = []
        for k, b in enumerate((p.b, 1 - p.b)):
            x, y = p.xy(a, b)
            out.append(self.copy(4 + k, (x * 2 + p.core, slice(None), y), p.a_peer()))
        return out

    def core_copies(self, back):
        p = self.p
        core = 1 - p.core if back else p.core
        return [self.copy(6 + x, (x * 2 + core,), p.core_peer()) for x in (0, 1)]

    def start(self, name):
        for copy in getattr(self, name + "_copies")(False):
            copy.start()

    def wait(self, name):
        for copy in getattr(self, name + "_copies")(True):
            copy.wait_recv()

    def drain(self):
        for name in ("z", "b", "a", "core"):
            for copy in getattr(self, name + "_copies")(False):
                copy.wait_send()


class QuickGather(Gather):
    def piece(self, a, b, back):
        p = self.p
        if back:
            a, b = p.a + a * (1 - 2 * p.a), p.b + b * (1 - 2 * p.b)
        else:
            a, b = p.a, p.b
        return p.xy(a, b)

    def plane_copy(self, q, d, back):
        p = self.p
        a, b = ((0, 1), (1, 0), (1, 1))[q]
        x, y = self.piece(a, b, back)
        where = (x * 2 + p.core, p.around(DEPS - d), y)
        return self.copy(3 + 4 * q + d, where, p.plane_peer(a, b))

    def core_copy(self, q, back):
        p = self.p
        a, b = ((0, 0), (0, 1), (1, 0), (1, 1))[q]
        x, y = self.piece(a, b, True)
        core = 1 - p.core if back else p.core
        return self.copy(15 + q, (x * 2 + core, slice(None), y), p.core_peer())

    def begin(self):
        for copy in self.z_copies(False):
            copy.start()
        for q in range(3):
            self.plane_copy(q, 0, False).start()

    def forward(self):
        for d, copy in zip((1, 2, 3), self.z_copies(True), strict=True):
            copy.wait_recv()
            for q in range(3):
                self.plane_copy(q, d, False).start()
        self.core_copy(0, False).start()

    def across(self):
        for q in range(3):
            for d in range(4):
                self.plane_copy(q, d, True).wait_recv()
            self.core_copy(1 + q, False).start()

    def end(self):
        for q in range(4):
            self.core_copy(q, True).wait_recv()

    def drain(self):
        for copy in self.z_copies(False):
            copy.wait_send()
        for q in range(3):
            for d in range(4):
                self.plane_copy(q, d, False).wait_send()
        for q in range(4):
            self.core_copy(q, False).wait_send()


class Scatter:
    def __init__(self, place, g, ins, sems, base):
        self.p, self.g, self.sems, self.base = place, g, sems, base
        self.c_in, self.a_in, self.b_in, self.z_in = ins

    def copies(self, name):
        p = self.p
        if name == "core":
            return [
                remote(part_of(self.g, x * 2 + 1 - p.core), self.c_in.at[x], self.sems, self.base + x, p.core_peer())
                for x in (0, 1)
            ]
        if name == "a":
            out = []
            for b in (0, 1):
                x, y = p.xy(1 - p.a, b)
                out.append(
                    remote(self.c_in.at[x, :, y], self.a_in.at[b], self.sems, self.base + 2 + b, p.a_peer())
                )
            return out
        if name == "b":
            return [remote(self.a_in.at[1 - p.b], self.b_in, self.sems, self.base + 4, p.b_peer())]
        return [
            remote(self.b_in.at[p.around(d)], self.z_in.at[d - 1], self.sems, self.base + 4 + d, p.z_peer(d))
            for d in (1, 2, 3)
        ]

    def start(self, name):
        for copy in self.copies(name):
            copy.start()

    def finish(self, name):
        p = self.p
        for copy in self.copies(name):
            copy.wait_recv()
        if name == "core":
            for x in (0, 1):
                self.c_in[x] += part_of(self.g, x * 2 + p.core)[...]
        elif name == "a":
            for b in (0, 1):
                x, y = p.xy(p.a, b)
                self.a_in[b] += self.c_in[x, :, y]
        elif name == "b":
            self.b_in[...] += self.a_in[p.b]

    def result(self):
        out = self.b_in[self.p.z].astype(WIDE)
        for d in range(3):
            out = out + self.z_in[d].astype(WIDE)
        return out

    def drain(self):
        for name in ("core", "a", "b", "z"):
            for copy in self.copies(name):
                copy.wait_send()


class QuickScatter(Scatter):
    def __init__(self, place, g, ins, sems, base, lane):
        super().__init__(place, g, ins, sems, base)
        self.lanes = pl.ds(lane, 128)

    def copies(self, name):
        p, base, lanes = self.p, self.base, self.lanes
        every = slice(None)
        out = []
        if name == "core":
            for x in (0, 1):
                src = self.g.at[x * 2 + 1 - p.core, :, :, :, lanes]
                dst = self.c_in.at[x, :, :, :, lanes]
                out.append(remote(src, dst, self.sems, base + x, p.core_peer()))
        elif name == "a":
            for q, (a, b) in enumerate(((0, 1), (1, 0), (1, 1))):
                x, y = p.xy(p.a + a * (1 - 2 * p.a), p.b + b * (1 - 2 * p.b))
                src = self.c_in.at[x, :, y, :, lanes]
                dst = self.a_in.at[q, :, :, lanes]
                out.append(remote(src, dst, self.sems, base + 2 + q, p.plane_peer(a, b)))
        elif name == "z":
            for d in (1, 2, 3):
                src = self.b_in.at[p.around(d), :, lanes]
                dst = self.z_in.at[d - 1, :, lanes]
                out.append(remote(src, dst, self.sems, base + 4 + d, p.z_peer(d)))
        return out

    def finish(self, name):
        p, lanes = self.p, self.lanes
        for copy in self.copies(name):
            copy.wait_recv()
        if name == "core":
            for x in (0, 1):
                self.c_in[x, :, :, :, lanes] += self.g[x * 2 + p.core, :, :, :, lanes]
        elif name == "a":
            mine = self.c_in[p.x, :, p.y, :, lanes].astype(WIDE)
            for q in range(3):
                mine = mine + self.a_in[q, :, :, lanes].astype(WIDE)
            self.b_in[:, :, lanes] = mine.astype(LOW)

    def result(self):
        out = self.b_in[self.p.z, :, self.lanes].astype(WIDE)
        for d in range(3):
            out = out + self.z_in[d, :, self.lanes].astype(WIDE)
        return out


class SlowTotal:
    def __init__(self, place, own, got, sems, base):
        self.p, self.own, self.got, self.sems, self.base = place, own, got, sems, base

    def copies(self, k):
        p = self.p
        if k < 3:
            device = (p.core_peer, p.x_peer, p.y_peer)[k]()
            return [remote(self.own.at[k], self.got.at[k], self.sems, self.base + k, device)]
        return [
            remote(self.own.at[3], self.got.at[3 + d], self.sems, self.base + 2 + d, p.z_peer(d))
            for d in (1, 2, 3)
        ]

    def start(self, k):
        for copy in self.copies(k):
            copy.start()

    def finish(self, k):
        p = self.p
        for copy in self.copies(k):
            copy.wait_recv()
        if k < 3:
            self.own[k + 1] = self.own[k] + self.got[k]
            return None
        self.got[3] = self.own[3]
        out = None
        for z in range(DEPS):
            part = self.got[3 + lax.rem(p.z - z + DEPS, DEPS)]
            out = part if z == 0 else out + part
        return out

    def drain(self):
        for k in range(4):
            for copy in self.copies(k):
                copy.wait_send()


class Total:
    def __init__(self, place, own, got, sems, base):
        self.p, self.own, self.got, self.sems, self.base = place, own, got, sems, base

    def copies(self, k):
        p = self.p
        if k == 0:
            return [
                remote(self.own.at[0], self.got.at[n], self.sems, self.base + n, p.near(n))
                for n in range(1, 8)
            ]
        return [
            remote(self.own.at[1], self.got.at[8 + d], self.sems, self.base + 7 + d, p.z_peer(d))
            for d in (1, 2, 3)
        ]

    def start(self, k):
        for copy in self.copies(k):
            copy.start()

    def finish(self, k):
        p = self.p
        for copy in self.copies(k):
            copy.wait_recv()
        self.got[8 * k] = self.own[k]
        out = None
        if k == 0:
            for n in range(8):
                x = 1 - p.x if n & 4 else p.x
                y = 1 - p.y if n & 2 else p.y
                core = 1 - p.core if n & 1 else p.core
                part = self.got[x * 4 + y * 2 + core]
                out = part if n == 0 else out + part
            self.own[1] = out
            return None
        for z in range(DEPS):
            part = self.got[8 + lax.rem(p.z - z + DEPS, DEPS)]
            out = part if z == 0 else out + part
        return out

    def drain(self):
        for k in range(2):
            for copy in self.copies(k):
                copy.wait_send()


INPUTS = ("size", "images", "patches_in", "cot_in", "classes", "class_cot")
INPUTS += ("entry", "exit", "expand", "reduce", "entry_c", "exit_c", "expand_c", "reduce_c")
INPUTS += ("vec", "talking", "off", "vec_c", "off_c")
OUTPUTS = dict(
    patch_result=((ROWS, WIDTH), LOW),
    patch_grad=((ROWS, WIDTH), WIDE),
    class_result=((3, WIDTH), LOW),
    class_grad=((3, WIDTH), WIDE),
    blocks=((6, SHARD, WIDTH), WIDE),
    rows_early=((24, WIDTH), WIDE),
    rows_late=((8, 512), WIDE),
)
COMM = {n: (SHAPE, LOW) for n in ("wa", "wa_c")}
COMM |= {n: (JOINED, LOW) for n in ("we", "wr", "we_c", "wr_c")}
COMM |= dict(
    early=((4, 24, WIDTH), WIDE),
    early_in=((7, 24, WIDTH), WIDE),
    late=((2, 8, 512), WIDE),
    late_in=((12, 8, 512), WIDE),
)
for _k in CHUNKS:
    COMM["c_in_" + _k] = ((2, DEPS, 2, SHARD, WIDTH), LOW)
    COMM["a_in_" + _k] = ((3 if _k == "a" else 2, DEPS, SHARD, WIDTH), LOW)
    COMM["b_in_" + _k] = ((DEPS, SHARD, WIDTH), LOW)
    COMM["z_in_" + _k] = ((3, SHARD, WIDTH), LOW)
SEMS = dict(g_send=59, g_recv=59, s_send=64, s_recv=64, t_send=17, t_recv=17, out=2, into=2)


def enter(p):
    barrier = pltpu.get_barrier_semaphore()
    peers = [p.z_peer(d) for d in (1, 2, 3)] + [p.near(n) for n in range(1, 8)]
    for peer in peers:
        pl.semaphore_signal(barrier, inc=1, device_id=peer, device_id_type=MESH)
    pl.semaphore_wait(barrier, len(peers))


def layer_kernel(inner, *refs):
    r = Refs(**dict(zip([*INPUTS, *OUTPUTS, *SCRATCH, *COMM, *SEMS], refs, strict=True)))
    p = Place(inner)
    mine = p.x * 2 + p.core
    weights = dict(a=r.wa, e=r.we, r=r.wr, ac=r.wa_c, ec=r.we_c, rc=r.wr_c)
    grads = weights
    first = QuickGather(p, r.wa, (r.g_send, r.g_recv), 40)
    gathers, scatters = {}, {}
    for i, k in enumerate(CHUNKS):
        if k != "a":
            gathers[k] = Gather(p, weights[k], (r.g_send, r.g_recv), 8 * (i - 1))
        ins = [getattr(r, n + "_in_" + k) for n in ("c", "a", "b", "z")]
        if k == "a":
            last = [QuickScatter(p, r.wa, ins, (r.s_send, r.s_recv), 40 + 8 * n, 128 * n) for n in range(3)]
        else:
            scatters[k] = Scatter(p, grads[k], ins, (r.s_send, r.s_recv), 8 * (i - 1))
    early = SlowTotal(p, r.early, r.early_in, (r.t_send, r.t_recv), 0)
    late = Total(p, r.late, r.late_in, (r.t_send, r.t_recv), 6)

    def go(*moves):
        def todo():
            for k, old, new in moves:
                if old:
                    gathers[k].wait(old)
                if new:
                    gathers[k].start(new)

        return todo

    def back(*moves):
        def todo():
            for k, old, new in moves:
                what = scatters.get(k) or early
                if old is not None:
                    what.finish(old)
                if new is not None:
                    what.start(new)

        return todo

    r.wa[mine, p.z, p.y] = jnp.concatenate([r.entry[...], r.exit[...]], 1)
    load = [
        pltpu.make_async_copy(r.patches_in, r.patches, r.into.at[0]),
        pltpu.make_async_copy(r.cot_in, r.cot, r.into.at[1]),
    ]
    load[0].start()
    load[1].start()
    enter(p)
    first.begin()
    part_of(r.we, mine, p.z, p.y)[...] = r.expand[...]
    part_of(r.wr, mine, p.z, p.y)[...] = r.reduce[...]
    r.wa_c[mine, p.z, p.y] = jnp.concatenate([r.entry_c[...], r.exit_c[...]], 1)
    part_of(r.we_c, mine, p.z, p.y)[...] = r.expand_c[...]
    part_of(r.wr_c, mine, p.z, p.y)[...] = r.reduce_c[...]
    columns(r)
    first.forward()
    gathers["e"].start("z")
    gathers["r"].start("z")
    masks(r)
    load[0].wait()
    norm_first(r)
    r.early[0] = jnp.zeros((24, WIDTH), WIDE)
    r.late[0] = jnp.zeros((8, 512), WIDE)
    first.across()
    first.end()
    go(("e", "z", "b"), ("ac", None, "z"))()
    project(r)
    attend(r, gather_points(go))
    gathers["e"].wait("core")
    gathers["r"].wait("core")
    feed(r, feed_points(go))
    out_result = pltpu.make_async_copy(r.result, r.patch_result, r.out.at[0])
    out_result.start()
    go(("rc", "a", "core"))()
    for k in ("ac", "ec", "rc"):
        gathers[k].wait("core")
    first.drain()
    for k in CHUNKS[1:]:
        gathers[k].drain()
    load[1].wait()
    classes(r)
    for k in ("ac", "ec", "rc"):
        scatters[k].start("core")
    feed_back(r, feed_back_points(back))
    scatters["e"].start("core")
    scatters["r"].start("core")
    attend_back(r, attend_back_points(back))
    for n in range(3):
        project_back_weights(r, n)
        last[n].start("core")
    for n in range(3):
        last[n].finish("core")
        last[n].start("a")
    talking_back(r)
    project_back(r)
    late.start(0)
    out_grad = pltpu.make_async_copy(r.grad, r.patch_grad, r.out.at[1])
    out_grad.start()
    for i, k in enumerate(CHUNKS):
        if k != "a":
            scatters[k].finish("z")
            r.blocks[i] = scatters[k].result()
    r.rows_early[...] = early.finish(3)
    last[0].finish("a")
    last[0].start("z")
    late.finish(0)
    late.start(1)
    for n in (1, 2):
        last[n].finish("a")
        last[n].start("z")
    r.rows_late[...] = late.finish(1)
    for n in range(3):
        last[n].finish("z")
        r.blocks[0, :, 128 * n : 128 * n + 128] = last[n].result()
    out_result.wait()
    out_grad.wait()
    for k in CHUNKS[1:]:
        scatters[k].drain()
    for k in last:
        k.drain()
    early.drain()
    late.drain()


def gather_points(go):
    return {
        0: go(("r", "z", "b")),
        1: go(("e", "b", "a"), ("ec", None, "z")),
        3: go(("r", "b", "a")),
        4: go(("ac", "z", "b")),
        5: go(("e", "a", "core")),
        6: go(("ac", "b", "a"), ("rc", None, "z")),
        7: go(("r", "a", "core"), ("ec", "z", "b")),
        9: go(("rc", "z", "b")),
        10: go(("ec", "b", "a"), ("ac", "a", "core")),
    }


def feed_points(go):
    return {0: go(("rc", "b", "a")), 2: go(("ec", "a", "core"))}


def feed_back_points(back):
    return {
        1: back(("ac", "core", "a")),
        2: back(("ec", "core", "a")),
    }


def attend_back_points(back):
    return {
        0: back(("ac", "a", "b"), ("rc", "core", "a")),
        1: back(("ec", "a", "b"), ("early", None, 0)),
        2: back(("e", "core", "a")),
        3: back(("rc", "a", "b"), ("ac", "b", "z")),
        4: back(("r", "core", "a"), ("ec", "b", "z"), ("early", 0, 1)),
        5: back(("e", "a", "b")),
        6: back(("rc", "b", "z")),
        7: back(("e", "b", "z"), ("early", 1, 2)),
        8: back(("r", "a", "b")),
        9: back(("early", 2, 3)),
        10: back(("r", "b", "z")),
    }


def finish_kernel(*refs):
    r = Refs(**dict(zip([*(n + "_in" for n in OUTPUTS), *FINAL], refs, strict=True)))
    r.patch_result[...] = r.patch_result_in[...]
    r.patch_grad[...] = r.patch_grad_in[...]
    r.class_result[...] = r.class_result_in[...]
    r.class_grad[...] = r.class_grad_in[...]
    for i, c in ((0, ""), (3, "_c")):
        getattr(r, "g_entry" + c)[...] = r.blocks_in[i, :, 0:COLS]
        getattr(r, "g_exit" + c)[...] = r.blocks_in[i, :, COLS:]
        getattr(r, "g_expand" + c)[...] = r.blocks_in[i + 1]
        getattr(r, "g_reduce" + c)[...] = r.blocks_in[i + 2]
    r.g_vec[0:4, :] = r.rows_late_in[0:4, 0:WIDTH]
    r.g_vec[4:10, :] = r.rows_early_in[0:6, :]
    r.g_vec_c[...] = r.rows_early_in[10:20, :]
    for j in range(PARTS):
        part = slice(WIDTH * j, WIDTH * (j + 1))
        r.g_off[part] = r.rows_early_in[6 + j : 7 + j, :].reshape(WIDTH)
        r.g_off_c[part] = r.rows_early_in[20 + j : 21 + j, :].reshape(WIDTH)
    talk = r.rows_late_in[:, WIDTH:]
    turned = jnp.concatenate([talk, jnp.zeros((120, 128), WIDE)], 0).T
    lane = iota((8, 128), 1)
    moved = pltpu.roll(turned[8:16], 8, 1)
    r.g_talking[...] = jnp.where((lane >= 8) & (lane < 16), moved, talk)[:, 0:17]


FINAL = dict(
    patch_result=((ROWS, WIDTH), LOW),
    class_result=((3, WIDTH), LOW),
    patch_grad=((ROWS, WIDTH), WIDE),
    class_grad=((3, WIDTH), WIDE),
    g_entry=((SHARD, COLS), WIDE),
    g_exit=((SHARD, 96), WIDE),
    g_expand=((SHARD, WIDTH), WIDE),
    g_reduce=((SHARD, WIDTH), WIDE),
    g_vec=((10, WIDTH), WIDE),
    g_talking=((8, 17), WIDE),
    g_off=((FF,), WIDE),
    g_entry_c=((SHARD, COLS), WIDE),
    g_exit_c=((SHARD, 96), WIDE),
    g_expand_c=((SHARD, WIDTH), WIDE),
    g_reduce_c=((SHARD, WIDTH), WIDE),
    g_vec_c=((10, WIDTH), WIDE),
    g_off_c=((FF,), WIDE),
)


def layers(inner, *args):
    smem = pl.BlockSpec(memory_space=pltpu.SMEM)
    vmem = pl.BlockSpec(memory_space=pltpu.VMEM)
    hbm = pl.BlockSpec(memory_space=pl.ANY)
    sems = [pltpu.SemaphoreType.DMA((n,)) for n in SEMS.values()]
    mid = pl.pallas_call(
        functools.partial(layer_kernel, inner),
        out_shape=[jax.ShapeDtypeStruct(*s) for s in OUTPUTS.values()],
        in_specs=[smem, smem, hbm, hbm] + [vmem] * (len(INPUTS) - 4),
        out_specs=[hbm, hbm] + [vmem] * (len(OUTPUTS) - 2),
        scratch_shapes=[pltpu.VMEM(*s) for s in (SCRATCH | COMM).values()] + sems,
        compiler_params=pltpu.CompilerParams(
            vmem_limit_bytes=63 * 2**20, collective_id=0, has_side_effects=True
        ),
    )(*args)
    out = pl.pallas_call(
        finish_kernel,
        out_shape=[jax.ShapeDtypeStruct(*s) for s in FINAL.values()],
        in_specs=[vmem] * len(OUTPUTS),
        out_specs=[vmem] * len(FINAL),
    )(*mid)
    return dict(zip(FINAL, out, strict=True))


def groups(axis, inner):
    return [[inner * k + i for i in range(inner)] for k in range(lax.axis_size(axis) // inner)]


def widen(x, inner, dims):
    for axis, n, dim in zip(("dp", "tensor"), inner, dims, strict=True):
        if n > 1:
            x = lax.all_gather(x, axis, axis=dim, tiled=True, axis_index_groups=groups(axis, n))
    return x


def narrow(x, inner, dims):
    for axis, n, dim in zip(("dp", "tensor"), inner, dims, strict=True):
        if n > 1:
            x = lax.psum_scatter(
                x, axis, scatter_dimension=dim, tiled=True, axis_index_groups=groups(axis, n)
            )
    return x


def whole(x, inner):
    for axis, n in zip(("dp", "tensor"), inner, strict=True):
        if n > 1:
            x = lax.psum(x, axis, axis_index_groups=groups(axis, n))
    return x


KINDS = ((0, 1),) * 4


def local(
    patches,
    classes,
    group_size,
    image_count,
    self_entry,
    self_exit,
    self_expand,
    self_reduce,
    self_vectors,
    self_talking,
    self_offset,
    class_entry,
    class_exit,
    class_expand,
    class_reduce,
    class_vectors,
    class_offset,
    patch_cotangent,
    class_cotangent,
):
    inner = (lax.axis_size("dp") // 8, lax.axis_size("tensor") // 4)
    weights = [
        widen(w, inner, dims)
        for w, dims in zip(
            (
                self_entry,
                self_exit,
                self_expand,
                self_reduce.T,
                class_entry,
                class_exit,
                class_expand,
                class_reduce.T,
            ),
            KINDS * 2,
            strict=True,
        )
    ]
    out = layers(
        inner,
        group_size,
        image_count,
        patches,
        patch_cotangent,
        classes,
        class_cotangent,
        *weights,
        self_vectors,
        self_talking.T,
        self_offset,
        class_vectors,
        class_offset,
    )
    names = ("entry", "exit", "expand", "reduce")
    own = [narrow(out["g_" + n], inner, dims) for n, dims in zip(names, KINDS, strict=True)]
    own_c = [narrow(out["g_" + n + "_c"], inner, dims) for n, dims in zip(names, KINDS, strict=True)]
    return (
        out["patch_result"],
        out["class_result"],
        out["patch_grad"],
        out["class_grad"],
        *own[:3],
        own[3].T,
        whole(out["g_vec"], inner),
        whole(out["g_talking"], inner).T,
        whole(out["g_off"], inner),
        *own_c[:3],
        own_c[3].T,
        whole(out["g_vec_c"], inner),
        whole(out["g_off_c"], inner),
    )


def solution(mesh):
    both = P(("dp", "tensor"), None)
    weights = (P("dp", "tensor"), P("dp", "tensor"), P("dp", "tensor"), P("tensor", "dp"))
    return jax.shard_map(
        local,
        mesh=mesh,
        in_specs=(
            both,
            both,
            P(("dp", "tensor")),
            P(("dp", "tensor")),
            *weights,
            P(),
            P(),
            P(),
            *weights,
            P(),
            P(),
            both,
            both,
        ),
        out_specs=(both, both, both, both, *weights, P(), P(), P(), *weights, P(), P()),
        check_vma=False,
    )
```

```python
import functools

import jax
import jax.numpy as jnp
from jax import lax
from jax.experimental import pallas as pl
from jax.experimental.pallas import tpu as pltpu
from jax.sharding import PartitionSpec as P

HEADS = 8
EPSILON = 1e-06
NEGATIVE = -1e30
ROOT_HALF = 0.7071067811865476
ROOT_TWO_PI = 2.5066282746310002
WIDE = jnp.float32
LOW = jnp.bfloat16

WIDTH = 384
DEPTH = WIDTH // HEADS
ROWS = 768
FF = 1536
PARTS = 4
COLS = 3 * WIDTH // PARTS
TILE = 128
SPAN = HEADS * TILE
HALVES = (slice(0, SPAN // 2), slice(SPAN // 2, SPAN))
WIDE_HALVES = (slice(0, FF // 2), slice(FF // 2, FF))
SHARD = 48
DEPS = 4
STEPS = ROWS // TILE
TOGETHER = 1
KEYS = ROWS + 128
DENSE = 384
PAIRS = HEADS * 8


def nn(a, b):
    return lax.dot_general(a, b, (((1,), (0,)), ((), ())), preferred_element_type=WIDE)


def nt(a, b):
    return lax.dot_general(a, b, (((1,), (1,)), ((), ())), preferred_element_type=WIDE)


def iota(shape, dim):
    return lax.broadcasted_iota(jnp.int32, shape, dim)


def rows_at(i, size):
    if isinstance(i, int):
        return slice(i * size, (i + 1) * size)
    return pl.ds(pl.multiple_of(i * size, size), size)


def normalize(x, gain, shift):
    mean = jnp.mean(x, -1, keepdims=True)
    centered = x - mean
    inverse = lax.rsqrt(jnp.mean(centered * centered, -1, keepdims=True) + EPSILON)
    unit = centered * inverse
    return unit * gain + shift, unit, inverse


def keep_stats(r, k, rows, x, inverse):
    r.stats[rows, 2 * k : 2 * k + 1] = jnp.mean(x, -1, keepdims=True)
    r.stats[rows, 2 * k + 1 : 2 * k + 2] = inverse


def unit_of(r, k, rows, x):
    inverse = r.stats[rows, 2 * k + 1 : 2 * k + 2]
    return (x - r.stats[rows, 2 * k : 2 * k + 1]) * inverse, inverse


def normalize_back(grad, gain, unit, inverse):
    scaled = grad * gain
    inner = jnp.mean(scaled * unit, -1, keepdims=True)
    return inverse * (scaled - jnp.mean(scaled, -1, keepdims=True) - unit * inner)


def by_head(x):
    return jnp.sum(x.reshape(HEADS, DEPTH, x.shape[-1]), 1)


def total(x):
    return jnp.sum(x, 0, keepdims=True)


def smooth(hidden):
    cdf = 0.5 * (1.0 + lax.erf(hidden * ROOT_HALF))
    slope = cdf + hidden * jnp.exp(-0.5 * hidden * hidden) * (1.0 / ROOT_TWO_PI)
    return (hidden * cdf).astype(LOW), slope.astype(LOW)


def each(count, together, step, points):
    def some(i, c):
        for k in range(together):

            def at(where):
                for key, todo in points.items():
                    if isinstance(key, str):
                        continue
                    t, place = divmod(key, 2)
                    if place == where and t % together == k:
                        pl.when(i == t // together)(todo)

            step(i * together + k, at)
        return c

    lax.fori_loop(0, count // together, some, 0)


class Refs:
    def __init__(self, **refs):
        self.__dict__.update(refs)


SCRATCH = dict(
    cols=((WIDTH, 128), WIDE),
    pad=((128, 128), WIDE),
    patches=((ROWS, WIDTH), LOW),
    cot=((ROWS, WIDTH), LOW),
    result=((ROWS, WIDTH), LOW),
    n1=((ROWS, WIDTH), LOW),
    stats=((ROWS, 128), WIDE),
    went=((3 * WIDTH, WIDTH), LOW),
    wout=((WIDTH, WIDTH), LOW),
    wback=((WIDTH, WIDTH), LOW),
    wfull=((WIDTH, 3 * WIDTH), LOW),
    qt=((WIDTH, ROWS), LOW),
    kext=((ROWS, 512), LOW),
    kt=((WIDTH, ROWS), LOW),
    vext=((ROWS, 512), LOW),
    vt=((WIDTH, ROWS), LOW),
    hot=((ROWS, 128), LOW),
    hott=((8, ROWS), WIDE),
    vsum=((WIDTH, 128), WIDE),
    gsum=((WIDTH, 128), WIDE),
    qm=((512, SPAN), LOW),
    qn=((WIDTH, SPAN), LOW),
    et=((STEPS + 1, ROWS, SPAN), LOW),
    un=((STEPS, WIDTH, SPAN), LOW),
    linv=((STEPS, 1, SPAN), WIDE),
    attt=((WIDTH, ROWS), LOW),
    middle=((ROWS, WIDTH), WIDE),
    branch1=((ROWS, WIDTH), LOW),
    branch2=((ROWS, WIDTH), WIDE),
    n2t=((WIDTH, ROWS), LOW),
    act=((ROWS, FF), LOW),
    slope=((ROWS, FF), LOW),
    next=((KEYS, WIDTH), LOW),
    wout_c=((WIDTH, WIDTH), LOW),
    small8=((8, WIDTH), WIDE),
    cot8=((8, WIDTH), WIDE),
    both=((KEYS, 128), LOW),
    qkwv=((128, WIDTH), LOW),
    d1t=((WIDTH, ROWS), LOW),
    d2t=((WIDTH, ROWS), LOW),
    dot=((WIDTH, ROWS), LOW),
    gwout=((WIDTH, WIDTH), WIDE),
    sums=((8, WIDTH), WIDE),
    offset=((1, FF), WIDE),
    dvt=((WIDTH, ROWS), WIDE),
    dkt=((WIDTH, ROWS), WIDE),
    accp=((HEADS, HEADS, TILE), WIDE),
    accq=((HEADS, HEADS, TILE), WIDE),
    dtr=((3 * WIDTH, ROWS), LOW),
)


def block_of(w, j):
    return w[j].reshape(WIDTH, w.shape[-1])


def whole_of(w):
    return w[...].reshape(WIDTH, FF)


def as_block(x):
    return x.reshape(DEPS, 2, SHARD, x.shape[-1])


def unpack_weights(wa, went, wout):
    for j in range(PARTS):
        block = block_of(wa, j).T
        went[COLS * j : COLS * (j + 1), :] = block[:COLS]
        wout[96 * j : 96 * (j + 1), :] = block[COLS:]

def columns(r):
    r.pad[...] = jnp.zeros((128, 128), WIDE)
    r.pad[0:8, 0:17] = r.talking[...]
    turned = r.pad[...]
    talk = turned.T
    turned = turned[0:8]
    moved = pltpu.roll(talk, 8, 1)[8:16]
    lane = iota((8, 128), 1)
    alone = jnp.sum(talk[8:16], 1, keepdims=True) + turned[:, 16:17]
    base = jnp.where(lane < 8, turned * DEPTH ** (-0.5), moved)
    base = jnp.where(lane == 16, turned, base)
    base = jnp.where(lane == 19, alone, base)
    turned = r.vec[0:8, :].T
    lane = iota((DEPTH, 128), 1)
    for h in range(HEADS):
        rows = slice(DEPTH * h, DEPTH * (h + 1))
        x = jnp.broadcast_to(base[h : h + 1], (DEPTH, 128))
        x = jnp.where(lane == 17, turned[rows, 2:3], x)
        r.cols[rows, :] = jnp.where(lane == 18, turned[rows, 3:4], x)


def masks(r):
    size, images = r.size[0], r.images[0]
    place = iota((ROWS, 128), 0)
    which = iota((ROWS, 128), 1)
    inside = (place >= which * size) & (place < which * size + size) & (which < images)
    r.hot[...] = jnp.where(inside, 1.0, 0.0).astype(LOW)
    r.kext[:, WIDTH:] = jnp.where(inside | (which >= 3), 0.0, NEGATIVE).astype(LOW)
    r.vext[:, WIDTH:] = jnp.where(which < 2, 1.0, 0.0).astype(LOW)
    place = iota((8, ROWS), 1)
    which = iota((8, ROWS), 0)
    inside = (place >= which * size) & (place < which * size + size) & (which < images)
    r.hott[...] = jnp.where(inside, 1.0, 0.0)


def norm_first(r):
    gain, shift = r.vec[0:1, :], r.vec[1:2, :]

    def norm_step(i, c):
        rows = rows_at(i, DENSE)
        x = r.patches[rows, :].astype(WIDE)
        normed, unit, inverse = normalize(x, gain, shift)
        r.n1[rows, :] = normed.astype(LOW)
        keep_stats(r, 0, rows, x, inverse)
        return c

    lax.fori_loop(0, ROWS // DENSE, norm_step, 0)


def project(r):
    unpack_weights(r.wa, r.went, r.wout)

    def step(i, c):
        rows = rows_at(i, DENSE)
        normed = r.n1[rows, :]
        turned = nt(r.went[...], normed)
        r.qt[:, rows] = (turned[0:WIDTH] + r.cols[:, 17:18]).astype(LOW)
        r.kt[:, rows] = turned[WIDTH : 2 * WIDTH].astype(LOW)
        r.vt[:, rows] = (turned[2 * WIDTH :] + r.cols[:, 18:19]).astype(LOW)
        both = nt(normed, r.went[WIDTH:, :])
        r.kext[rows, 0:WIDTH] = both[:, 0:WIDTH].astype(LOW)
        r.vext[rows, 0:WIDTH] = (both[:, WIDTH:] + r.vec[3:4, :]).astype(LOW)
        return c

    lax.fori_loop(0, ROWS // DENSE, step, 0)
    r.vsum[...] = nn(r.vt[...], r.hot[...])
    r.wback[...] = r.wout[...].T
    r.wfull[:, 0:WIDTH] = r.went[0:WIDTH, :].T
    r.wfull[:, WIDTH : 2 * WIDTH] = r.went[2 * WIDTH :, :].T
    r.wfull[:, 2 * WIDTH :] = r.went[WIDTH : 2 * WIDTH, :].T


def attend(r, points):
    def step(t, at):
        at(0)
        rows = rows_at(t, TILE)
        q = r.qt[:, rows].astype(WIDE)
        hot = r.hott[:, rows]
        hot_rows = jnp.concatenate([hot, jnp.zeros((120, TILE), WIDE)], 0).astype(LOW)
        for g in range(HEADS):
            r.qm[0:WIDTH, TILE * g : TILE * (g + 1)] = (q * r.cols[:, g : g + 1]).astype(LOW)
            r.qm[WIDTH:, TILE * g : TILE * (g + 1)] = hot_rows
        own = r.vt[:, rows].astype(WIDE)
        att = r.cols[:, 16:17] * (
            r.vsum[:, 0:1] * hot[0:1] + r.vsum[:, 1:2] * hot[1:2] + r.vsum[:, 2:3] * hot[2:3]
        )
        for half in HALVES:
            scores = nn(r.kext[...], r.qm[:, half])
            raised = jnp.exp(scores - jnp.max(scores, 0, keepdims=True))
            r.linv[t, :, half] = 1.0 / jnp.sum(raised, 0, keepdims=True)
            r.et[t + 1, :, half] = raised.astype(LOW)
        at(1)
        for i, half in enumerate(HALVES):
            mean = nn(r.vt[...], r.et[t + 1, :, half]) * r.linv[t, :, half]
            r.un[t, :, half] = mean.astype(LOW)
            for k in range(HEADS // 2):
                h = HEADS // 2 * i + k
                att = att + r.cols[:, 8 + h : 9 + h] * mean[:, TILE * k : TILE * (k + 1)]
        live = (hot[0:1] + hot[1:2] + hot[2:3]) > 0.5
        att = jnp.where(live, att, r.cols[:, 19:20] * own).astype(LOW)
        r.attt[:, rows] = att
        branch = nt(att.T, r.wout[...]) + r.vec[4:5, :]
        r.branch1[rows, :] = branch.astype(LOW)
        r.middle[rows, :] = r.patches[rows, :].astype(WIDE) + r.vec[5:6, :] * branch

    each(STEPS, TOGETHER, step, points)


def feed(r, points):
    def step(i, at):
        at(0)
        rows = rows_at(i, DENSE)
        middle = r.middle[rows, :]
        normed, unit, inverse = normalize(middle, r.vec[6:7, :], r.vec[7:8, :])
        keep_stats(r, 1, rows, middle, inverse)
        normed = normed.astype(LOW)
        r.n2t[:, rows] = normed.T
        hidden = [nn(normed, whole_of(r.we)[:, half]) + r.off[half].reshape(1, FF // 2) for half in WIDE_HALVES]
        for half, part in zip(WIDE_HALVES, hidden, strict=True):
            active, slope = smooth(part)
            r.act[rows, half] = active
            r.slope[rows, half] = slope
        at(1)
        lifted = nt(whole_of(r.wr), r.act[rows, :]).T
        branch = lifted + r.vec[8:9, :]
        r.branch2[rows, :] = branch
        first = middle + r.vec[9:10, :] * branch
        r.result[rows, :] = first.astype(LOW)
        normed, unit, inverse = normalize(first, r.vec_c[0:1, :], r.vec_c[1:2, :])
        r.next[rows, :] = normed.astype(LOW)
        keep_stats(r, 2, rows, first, inverse)

    each(ROWS // DENSE, 1, step, points)


def classes(r, points):
    v = lambda k: r.vec_c[k : k + 1, :]
    scale = DEPTH ** (-0.5)
    points[0]()
    unpack_weights(r.wa_c, r.went, r.wout_c)
    wq, wk, wv = (r.went[WIDTH * k : WIDTH * (k + 1), :] for k in range(3))
    r.small8[...] = jnp.zeros((8, WIDTH), WIDE)
    r.cot8[...] = jnp.zeros((8, WIDTH), WIDE)
    r.small8[0:3, :] = r.classes[...].astype(WIDE)
    r.cot8[0:3, :] = r.class_cot[...].astype(WIDE)
    tokens = r.small8[...]
    normed, unit, inverse = normalize(tokens, v(0), v(1))
    low = normed.astype(LOW)
    valid = iota((128, WIDTH), 0) < 3
    r.next[ROWS:, :] = jnp.where(
        valid, jnp.concatenate([normed, jnp.zeros((120, WIDTH), WIDE)], 0), 0.0
    ).astype(LOW)
    head_of = iota((PAIRS, WIDTH), 1) // DEPTH
    own_head = head_of == iota((PAIRS, WIDTH), 0) // 8

    def spread(x):
        return jnp.where(own_head, jnp.concatenate([x] * HEADS, 0), 0.0)

    def gather_heads(x):
        x = jnp.where(own_head, x, 0.0)
        out = x[0:8]
        for h in range(1, HEADS):
            out = out + x[8 * h : 8 * (h + 1)]
        return out

    queries = (nt(low, wq) + v(2)).astype(LOW)
    qexp = spread(queries.astype(WIDE))
    qk = (nn(qexp.astype(LOW), wk) * scale).astype(LOW)
    keys = r.next[...]
    scores = nt(qk, keys)
    size, images = r.size[0], r.images[0]
    slot = iota((PAIRS, KEYS), 0) & 7
    place = iota((PAIRS, KEYS), 1)
    allowed = (place >= slot * size) & (place < slot * size + size) & (slot < images)
    allowed = allowed | (place == slot + ROWS)
    scores = jnp.where(allowed, scores, NEGATIVE)
    raised = jnp.exp(scores - jnp.max(scores, -1, keepdims=True))
    probs = raised / jnp.sum(raised, -1, keepdims=True)
    probs_low = probs.astype(LOW)
    mass = jnp.sum(probs_low.astype(WIDE), -1, keepdims=True)
    z = nn(probs_low, keys).astype(LOW)
    attended = gather_heads(nt(z, wv) + mass * v(3)).astype(LOW)
    branch = nt(attended, r.wout_c[...]) + v(4)
    middle = tokens + v(5) * branch
    normed2, unit2, inverse2 = normalize(middle, v(6), v(7))
    low2 = normed2.astype(LOW)
    grad = r.cot8[...]
    delta2 = (v(9) * grad).astype(LOW)
    points[2](jnp.concatenate([low2.astype(WIDE), delta2.astype(WIDE)], 0).astype(LOW))
    points[1]()
    expand, reduce = whole_of(r.we_c), whole_of(r.wr_c)
    hidden = nn(low2, expand) + r.off_c[...].reshape(1, FF)
    active, slope = smooth(hidden)
    lifted = nt(active, reduce)
    branch2 = lifted + v(8)
    second = middle + v(9) * branch2
    r.class_result[...] = second[0:3].astype(LOW)
    grad_scale2 = total(grad * branch2)
    grad_bias2 = total(delta2.astype(WIDE))
    grad_hidden = (nn(delta2, reduce) * slope.astype(WIDE)).astype(LOW)
    off = total(grad_hidden.astype(WIDE))
    for j in range(PARTS):
        r.early[0, 20 + j : 21 + j, :] = off[:, WIDTH * j : WIDTH * (j + 1)]
    back = nt(grad_hidden, expand)
    grad_gain2, grad_shift2 = total(back * unit2), total(back)
    grad = grad + normalize_back(back, v(6), unit2, inverse2)
    grad_scale = total(grad * branch)
    delta = (v(5) * grad).astype(LOW)
    grad_bias = total(delta.astype(WIDE))
    gatt = nn(delta, r.wout_c[...]).astype(LOW)
    dexp = spread(gatt.astype(WIDE))
    wide_v = nn(dexp.astype(LOW), wv).astype(LOW)
    gp = nt(wide_v, keys)
    ds = (probs * (gp - jnp.sum(gp * probs, -1, keepdims=True))).astype(LOW)
    y = nn(ds, keys).astype(LOW)
    gq = (gather_heads(nt(y, wk)) * scale).astype(LOW)
    both = jnp.concatenate([ds.astype(WIDE), probs_low.astype(WIDE)], 0).T.astype(LOW)
    r.both[...] = both
    r.qkwv[...] = jnp.concatenate([qk, wide_v], 0)
    grad_normed = nn(both[ROWS:, :], r.qkwv[...])[0:8] + nn(gq, wq)
    r.class_grad[...] = (grad + normalize_back(grad_normed, v(0), unit, inverse))[0:3]
    valid8 = iota((8, WIDTH), 0) < 3
    grad_normed = jnp.where(valid8, grad_normed, 0.0)
    gq_t = gq.astype(WIDE).T.astype(LOW)
    grad_q = nn(gq_t, low)
    grad_k = nn((qexp * scale).T.astype(LOW), y)
    grad_v = nn(dexp.T.astype(LOW), z)
    grad_out = nn(delta.astype(WIDE).T.astype(LOW), attended)
    whole = jnp.concatenate([grad_q, grad_k, grad_v], 0)
    for j in range(PARTS):
        block = jnp.concatenate(
            [whole[COLS * j : COLS * (j + 1)], grad_out[96 * j : 96 * (j + 1)]], 0
        )
        r.wa_c[j] = as_block(block.T.astype(LOW))
    grad_vb = total(jnp.where(own_head, mass * dexp, 0.0))
    r.early[0, 10:20, :] = jnp.concatenate(
        [
            total(grad_normed * unit),
            total(grad_normed),
            total(gq.astype(WIDE)),
            grad_vb,
            grad_bias,
            grad_scale,
            grad_gain2,
            grad_shift2,
            grad_bias2,
            grad_scale2,
        ],
        0,
    )


def class_weights(r, p):
    rows = r.wf[...].astype(WIDE).reshape(32, 16, WIDTH)
    normed, delta = (rows[:, k : k + 8].reshape(256, WIDTH) for k in (0, 8))
    for k, x in enumerate((normed, delta)):
        r.turned[k] = x.T.astype(LOW).reshape(DEPS, 2, SHARD, 256)
    part = p.x * 2 + p.core
    offset = r.off_c[0:WIDTH]
    for j in range(1, PARTS):
        offset = jnp.where(part == j, r.off_c[WIDTH * j : WIDTH * (j + 1)], offset)
    expand = part_of(r.we_c, part)[...].reshape(WIDTH, WIDTH)
    reduce = part_of(r.wr_c, part)[...].reshape(WIDTH, WIDTH)
    hidden = nn(normed.astype(LOW), expand) + offset.reshape(1, WIDTH)
    active, slope = smooth(hidden)
    grad_hidden = (nn(delta.astype(LOW), reduce) * slope.astype(WIDE)).astype(LOW)
    r.blocks[4] = nn(r.turned[0, p.z, p.y], grad_hidden)
    r.blocks[5] = nn(r.turned[1, p.z, p.y], active)


def feed_back(r, points):
    size, images = r.size[0], r.images[0]
    r.early[0, 0:10, :] = jnp.zeros((10, WIDTH), WIDE)
    r.offset[...] = jnp.zeros((1, FF), WIDE)

    def add(k, x):
        r.early[0, k - 4 : k - 3, :] += total(x)

    def step(i, at):
        at(0)
        rows = rows_at(i, DENSE)
        branch2 = r.branch2[rows, :]
        unitc, inversec = unit_of(r, 2, rows, r.middle[rows, :] + r.vec[9:10, :] * branch2)
        dn = nn(r.both[rows, :], r.qkwv[...])
        add(14, dn * unitc)
        add(15, dn)
        grad = normalize_back(dn, r.vec_c[0:1, :], unitc, inversec)
        place = iota((DENSE, WIDTH), 0) + i * DENSE
        grad = grad + jnp.where(place < size * images, r.cot[rows, :].astype(WIDE), 0.0)
        add(9, grad * branch2)
        delta = (r.vec[9:10, :] * grad).astype(LOW)
        add(8, delta.astype(WIDE))
        r.d2t[:, rows] = delta.T
        grad_hidden = [
            (nn(delta, whole_of(r.wr)[:, half]) * r.slope[rows, half].astype(WIDE)).astype(LOW)
            for half in WIDE_HALVES
        ]
        for half, part in zip(WIDE_HALVES, grad_hidden, strict=True):
            r.slope[rows, half] = part
            r.offset[:, half] += total(part.astype(WIDE))
        at(1)
        back = nt(whole_of(r.we), r.slope[rows, :]).T
        unit, inverse = unit_of(r, 1, rows, r.middle[rows, :])
        add(6, back * unit)
        add(7, back)
        grad = grad + normalize_back(back, r.vec[6:7, :], unit, inverse)
        r.middle[rows, :] = grad
        add(5, grad * r.branch1[rows, :].astype(WIDE))
        delta = (r.vec[5:6, :] * grad).astype(LOW)
        add(4, delta.astype(WIDE))
        r.d1t[:, rows] = delta.T
        r.dot[:, rows] = nt(r.wback[...], delta).astype(LOW)

    each(ROWS // DENSE, 1, step, points)
    for half in WIDE_HALVES:
        r.we[:, :, :, half] = as_block(nn(r.n2t[...], r.slope[:, half]).astype(LOW))
    points["expand"]()
    for half in WIDE_HALVES:
        r.wr[:, :, :, half] = as_block(nn(r.d2t[...], r.act[:, half]).astype(LOW))
    points["reduce"]()
    for j in range(PARTS):
        r.early[0, 6 + j : 7 + j, :] = r.offset[:, WIDTH * j : WIDTH * (j + 1)]
    r.gwout[...] = nt(r.d1t[...], r.attt[...])


def attend_back(r, points):
    r.dvt[...] = jnp.zeros((WIDTH, ROWS), WIDE)
    r.accp[...] = jnp.zeros((HEADS, HEADS, TILE), WIDE)
    r.accq[...] = jnp.zeros((HEADS, HEADS, TILE), WIDE)

    def step(t, at):
        at(0)
        rows = rows_at(t, TILE)
        grad = r.dot[:, rows].astype(WIDE)
        inverse = r.linv[t]
        place = iota((128, TILE), 0)
        for h in range(HEADS):
            part = slice(TILE * h, TILE * (h + 1))
            post = r.cols[:, 8 + h : 9 + h]
            w = grad * r.un[t, :, part].astype(WIDE)
            r.accp[h] += by_head(w)
            minus = -inverse[:, part] * total(post * w)
            high = minus.astype(LOW).astype(WIDE)
            r.qm[0:WIDTH, part] = (grad * post * inverse[:, part]).astype(LOW)
            extra = jnp.where(place == 0, high, jnp.where(place == 1, minus - high, 0.0))
            r.qm[WIDTH:, part] = extra.astype(LOW)
        q = r.qt[:, rows].astype(WIDE)
        for half in HALVES:
            gp = nn(r.vext[...], r.qm[:, half])
            r.et[t, :, half] = (r.et[t + 1, :, half].astype(WIDE) * gp).astype(LOW)
        r.dvt[...] += nt(r.qm[0:WIDTH, :], r.et[t + 1])
        at(1)
        dq = jnp.zeros((WIDTH, TILE), WIDE)
        for i, half in enumerate(HALVES):
            y = nn(r.kt[...], r.et[t, :, half])
            for k in range(HEADS // 2):
                g = HEADS // 2 * i + k
                part = y[:, TILE * k : TILE * (k + 1)]
                dq = dq + r.cols[:, g : g + 1] * part
                r.accq[g] += by_head(q * part)
        r.dtr[0:WIDTH, rows] = dq.astype(LOW)

    each(STEPS, TOGETHER, step, points)
    r.gsum[...] = nn(r.dot[...], r.hot[...])
    bias = r.cols[:, 16:17]
    for k in range(3):
        r.dvt[...] += (bias * r.gsum[:, k : k + 1]) * r.hott[k : k + 1, :]
    r.dtr[WIDTH : 2 * WIDTH, :] = r.dvt[...].astype(LOW)


def keys_back(r, points):
    for t in range(STEPS):
        if t in points:
            points[t]()
        q = r.qt[:, rows_at(t, TILE)].astype(WIDE)
        mixed = r.qn if t % 2 else r.qm
        for g in range(HEADS):
            mixed[0:WIDTH, TILE * g : TILE * (g + 1)] = (q * r.cols[:, g : g + 1]).astype(LOW)
        part = nt(mixed[0:WIDTH, :], r.et[t])
        r.dkt[...] = part if t == 0 else r.dkt[...] + part
    r.dtr[2 * WIDTH :, :] = r.dkt[...].astype(LOW)


def talking_back(r):
    lane = iota((HEADS, 128), 1)

    def lanes_sum(x):
        return jnp.sum(x, -1, keepdims=True)

    out = jnp.where(lane == 2 * HEADS, lanes_sum(by_head(r.gsum[...] * r.vsum[...])), 0.0)
    for h in range(HEADS):
        out = out + jnp.where(lane == h, lanes_sum(r.accq[h]) * DEPTH ** (-0.5), 0.0)
        out = out + jnp.where(lane == HEADS + h, lanes_sum(r.accp[h]), 0.0)
    r.mid[0, :, WIDTH:] = out


def store_grads(r, j, part, rows):
    lanes = rows.shape[0]
    block = rows.T.astype(LOW).reshape(DEPS, 2, SHARD, lanes)
    r.wa[j, :, :, :, 128 * part : 128 * part + lanes] = block


def weights_early(r):
    whole = nn(r.dtr[0 : 2 * WIDTH, :], r.n1[...])
    query, value = whole[0:WIDTH], whole[WIDTH:]
    gwout = r.gwout
    store_grads(r, 0, 0, jnp.concatenate([query[0:288], gwout[0:96, :]], 0))
    store_grads(r, 1, 0, jnp.concatenate([query[288:], gwout[96:128, :]], 0))
    store_grads(r, 2, 0, jnp.concatenate([value[0:96], gwout[192:224, :]], 0))
    store_grads(r, 3, 0, jnp.concatenate([value[96:], gwout[288:, :]], 0))


def weights_late(r):
    keys = nn(r.dtr[2 * WIDTH :, :], r.n1[...])
    store_grads(r, 1, 1, jnp.concatenate([r.gwout[128:192, :], keys[0:192]], 0))
    store_grads(r, 2, 1, jnp.concatenate([r.gwout[224:288, :], keys[192:]], 0))


def project_back_start(r):
    ones = jnp.ones((8, ROWS), LOW)
    r.mid[0, 0:1, 0:WIDTH] = nt(ones, r.dtr[0:WIDTH, :])[0:1]
    r.mid[0, 1:2, 0:WIDTH] = nt(ones, r.dtr[WIDTH : 2 * WIDTH, :])[0:1]
    r.dvt[...] = nn(r.wfull[:, 0 : 2 * WIDTH], r.dtr[0 : 2 * WIDTH, :])


def project_back(r):
    r.sums[...] = jnp.zeros((8, WIDTH), WIDE)

    def step(i, c):
        rows = rows_at(i, DENSE)
        back = (r.dvt[:, rows] + nn(r.wfull[:, 2 * WIDTH :], r.dtr[2 * WIDTH :, rows])).T
        unit, inverse = unit_of(r, 0, rows, r.patches[rows, :].astype(WIDE))
        r.sums[0:1, :] += total(back * unit)
        r.sums[1:2, :] += total(back)
        r.middle[rows, :] = r.middle[rows, :] + normalize_back(
            back, r.vec[0:1, :], unit, inverse
        )
        return c

    lax.fori_loop(0, ROWS // DENSE, step, 0)
    for k in range(2):
        for n in range(3):
            r.late[0, 3 * k + n : 3 * k + n + 1, :] = r.sums[k : k + 1, 128 * n : 128 * n + 128]


MESH = pl.DeviceIdType.MESH
CHUNKS = ("a", "e", "r", "ac", "ec", "rc")
SHAPE = (PARTS, DEPS, 2, SHARD, WIDTH)
JOINED = (DEPS, 2, SHARD, PARTS * WIDTH)


class Place:
    def __init__(self, inner):
        self.inner = inner
        dp, tensor = lax.axis_index("dp"), lax.axis_index("tensor")
        self.rest = (lax.rem(dp, inner[0]), lax.rem(tensor, inner[1]))
        dp, tensor = dp // inner[0], tensor // inner[1]
        self.z, self.y = dp // 2, lax.rem(dp, 2)
        self.x, self.core = tensor // 2, lax.rem(tensor, 2)
        self.a = self.x + self.core * (self.y - self.x)
        self.b = self.y + self.core * (self.x - self.y)

    def xy(self, a, b):
        return a + self.core * (b - a), b + self.core * (a - b)

    def device(self, z, y, x, core):
        return (
            (z * 2 + y) * self.inner[0] + self.rest[0],
            (x * 2 + core) * self.inner[1] + self.rest[1],
        )

    def around(self, d):
        return lax.rem(self.z + d, DEPS)

    def z_peer(self, d):
        return self.device(self.around(d), self.y, self.x, self.core)

    def a_peer(self):
        x, y = self.xy(1 - self.a, self.b)
        return self.device(self.z, y, x, self.core)

    def b_peer(self):
        x, y = self.xy(self.a, 1 - self.b)
        return self.device(self.z, y, x, self.core)

    def x_peer(self):
        return self.device(self.z, self.y, 1 - self.x, self.core)

    def y_peer(self):
        return self.device(self.z, 1 - self.y, self.x, self.core)

    def plane_peer(self, a, b):
        x, y = self.xy(self.a + a * (1 - 2 * self.a), self.b + b * (1 - 2 * self.b))
        return self.device(self.z, y, x, self.core)

    def near(self, k):
        x = 1 - self.x if k & 4 else self.x
        y = 1 - self.y if k & 2 else self.y
        return self.device(self.z, y, x, 1 - self.core if k & 1 else self.core)

    def core_peer(self):
        return self.device(self.z, self.y, self.x, 1 - self.core)


def remote(src, dst, sems, k, device):
    return pltpu.make_async_remote_copy(
        src_ref=src,
        dst_ref=dst,
        send_sem=sems[0].at[k],
        recv_sem=sems[1].at[k],
        device_id=device,
        device_id_type=MESH,
    )


def part_of(w, j, z=slice(None), y=slice(None)):
    if len(w.shape) == 5:
        return w.at[j, z, y]
    return w.at[z, y, :, pl.ds(pl.multiple_of(j * WIDTH, 128), WIDTH)]


class Gather:
    def __init__(self, place, w, sems, base):
        self.p, self.w, self.sems, self.base = place, w, sems, base

    def copy(self, k, where, device):
        ref = part_of(self.w, *where)
        return remote(ref, ref, self.sems, self.base + k, device)

    def z_copies(self, back):
        p = self.p
        out = []
        for d in (1, 2, 3):
            z = p.around(DEPS - d) if back else p.z
            out.append(self.copy(d - 1, (p.x * 2 + p.core, z, p.y), p.z_peer(d)))
        return out

    def b_copies(self, back):
        p = self.p
        x, y = p.xy(p.a, 1 - p.b) if back else (p.x, p.y)
        return [self.copy(3, (x * 2 + p.core, slice(None), y), p.b_peer())]

    def a_copies(self, back):
        p = self.p
        a = 1 - p.a if back else p.a
        out = []
        for k, b in enumerate((p.b, 1 - p.b)):
            x, y = p.xy(a, b)
            out.append(self.copy(4 + k, (x * 2 + p.core, slice(None), y), p.a_peer()))
        return out

    def core_copies(self, back):
        p = self.p
        core = 1 - p.core if back else p.core
        return [self.copy(6 + x, (x * 2 + core,), p.core_peer()) for x in (0, 1)]

    def start(self, name):
        for copy in getattr(self, name + "_copies")(False):
            copy.start()

    def wait(self, name):
        for copy in getattr(self, name + "_copies")(True):
            copy.wait_recv()

    def drain(self):
        for name in ("z", "b", "a", "core"):
            for copy in getattr(self, name + "_copies")(False):
                copy.wait_send()


class QuickGather(Gather):
    def piece(self, a, b, back):
        p = self.p
        if back:
            a, b = p.a + a * (1 - 2 * p.a), p.b + b * (1 - 2 * p.b)
        else:
            a, b = p.a, p.b
        return p.xy(a, b)

    def plane_copy(self, q, d, back):
        p = self.p
        a, b = ((0, 1), (1, 0), (1, 1))[q]
        x, y = self.piece(a, b, back)
        where = (x * 2 + p.core, p.around(DEPS - d), y)
        return self.copy(3 + 4 * q + d, where, p.plane_peer(a, b))

    def core_copy(self, q, back):
        p = self.p
        a, b = ((0, 0), (0, 1), (1, 0), (1, 1))[q]
        x, y = self.piece(a, b, True)
        core = 1 - p.core if back else p.core
        return self.copy(15 + q, (x * 2 + core, slice(None), y), p.core_peer())

    def begin(self):
        for copy in self.z_copies(False):
            copy.start()
        for q in range(3):
            self.plane_copy(q, 0, False).start()

    def forward(self):
        for d, copy in zip((1, 2, 3), self.z_copies(True), strict=True):
            copy.wait_recv()
            for q in range(3):
                self.plane_copy(q, d, False).start()
        self.core_copy(0, False).start()

    def across(self):
        for q in range(3):
            for d in range(4):
                self.plane_copy(q, d, True).wait_recv()
            self.core_copy(1 + q, False).start()

    def end(self):
        for q in range(4):
            self.core_copy(q, True).wait_recv()

    def drain(self):
        for copy in self.z_copies(False):
            copy.wait_send()
        for q in range(3):
            for d in range(4):
                self.plane_copy(q, d, False).wait_send()
        for q in range(4):
            self.core_copy(q, False).wait_send()


class Scatter:
    def __init__(self, place, g, ins, sems, base):
        self.p, self.g, self.sems, self.base = place, g, sems, base
        self.c_in, self.a_in, self.b_in, self.z_in = ins

    def copies(self, name):
        p = self.p
        if name == "core":
            return [
                remote(part_of(self.g, x * 2 + 1 - p.core), self.c_in.at[x], self.sems, self.base + x, p.core_peer())
                for x in (0, 1)
            ]
        if name == "a":
            out = []
            for b in (0, 1):
                x, y = p.xy(1 - p.a, b)
                out.append(
                    remote(self.c_in.at[x, :, y], self.a_in.at[b], self.sems, self.base + 2 + b, p.a_peer())
                )
            return out
        if name == "b":
            return [remote(self.a_in.at[1 - p.b], self.b_in, self.sems, self.base + 4, p.b_peer())]
        return [
            remote(self.b_in.at[p.around(d)], self.z_in.at[d - 1], self.sems, self.base + 4 + d, p.z_peer(d))
            for d in (1, 2, 3)
        ]

    def start(self, name):
        for copy in self.copies(name):
            copy.start()

    def finish(self, name):
        p = self.p
        for copy in self.copies(name):
            copy.wait_recv()
        if name == "core":
            for x in (0, 1):
                self.c_in[x] += part_of(self.g, x * 2 + p.core)[...]
        elif name == "a":
            for b in (0, 1):
                x, y = p.xy(p.a, b)
                self.a_in[b] += self.c_in[x, :, y]
        elif name == "b":
            self.b_in[...] += self.a_in[p.b]

    def result(self):
        out = self.b_in[self.p.z].astype(WIDE)
        for d in range(3):
            out = out + self.z_in[d].astype(WIDE)
        return out

    def drain(self):
        for name in ("core", "a", "b", "z"):
            for copy in self.copies(name):
                copy.wait_send()


class QuickScatter(Scatter):
    def __init__(self, place, g, ins, sems, base, lane):
        super().__init__(place, g, ins, sems, base)
        self.lanes = pl.ds(lane, 128)

    def copies(self, name):
        p, base, lanes = self.p, self.base, self.lanes
        every = slice(None)
        out = []
        if name == "core":
            for x in (0, 1):
                src = self.g.at[x * 2 + 1 - p.core, :, :, :, lanes]
                dst = self.c_in.at[x, :, :, :, lanes]
                out.append(remote(src, dst, self.sems, base + x, p.core_peer()))
        elif name == "a":
            for q, (a, b) in enumerate(((0, 1), (1, 0), (1, 1))):
                x, y = p.xy(p.a + a * (1 - 2 * p.a), p.b + b * (1 - 2 * p.b))
                src = self.c_in.at[x, :, y, :, lanes]
                dst = self.a_in.at[q, :, :, lanes]
                out.append(remote(src, dst, self.sems, base + 2 + q, p.plane_peer(a, b)))
        elif name == "z":
            for d in (1, 2, 3):
                src = self.b_in.at[p.around(d), :, lanes]
                dst = self.z_in.at[d - 1, :, lanes]
                out.append(remote(src, dst, self.sems, base + 4 + d, p.z_peer(d)))
        return out

    def finish(self, name):
        p, lanes = self.p, self.lanes
        for copy in self.copies(name):
            copy.wait_recv()
        if name == "core":
            for x in (0, 1):
                self.c_in[x, :, :, :, lanes] += self.g[x * 2 + p.core, :, :, :, lanes]
        elif name == "a":
            mine = self.c_in[p.x, :, p.y, :, lanes].astype(WIDE)
            for q in range(3):
                mine = mine + self.a_in[q, :, :, lanes].astype(WIDE)
            self.b_in[:, :, lanes] = mine.astype(LOW)

    def result(self):
        out = self.b_in[self.p.z, :, self.lanes].astype(WIDE)
        for d in range(3):
            out = out + self.z_in[d, :, self.lanes].astype(WIDE)
        return out


class PartScatter(QuickScatter):
    def __init__(self, place, g, ins, sems, base, owner):
        super().__init__(place, g, ins, sems, base, 128)
        self.lanes = pl.ds(128, 256)
        self.owner = owner

    def core_copy(self, back):
        p = self.p
        x = self.owner if back else 1 - self.owner
        src = self.g.at[x * 2 + 1 - p.core, :, :, :, self.lanes]
        return remote(src, self.c_in.at[x, :, :, :, self.lanes], self.sems, self.base, p.core_peer())

    def plane_copy(self, k):
        p = self.p
        y = 1 - p.y if k & 1 else p.y
        src = self.c_in.at[self.owner, :, y, :, self.lanes]
        dst = self.a_in.at[k - 1, :, :, self.lanes]
        peer = (None, p.y_peer, p.x_peer, lambda: p.plane_peer(1, 1))[k]()
        return remote(src, dst, self.sems, self.base + k, peer)

    def owned(self, todo):
        pl.when(self.p.x == self.owner)(todo)

    def others(self, todo):
        pl.when(self.p.x != self.owner)(todo)

    def start(self, name):
        if name == "core":
            self.core_copy(False).start()
        elif name == "a":
            self.owned(lambda: self.plane_copy(1).start())

            def both():
                self.plane_copy(2).start()
                self.plane_copy(3).start()

            self.others(both)
        else:
            self.owned(lambda: QuickScatter.start(self, name))

    def finish(self, name):
        p, lanes = self.p, self.lanes
        if name == "core":
            self.core_copy(True).wait_recv()
            self.c_in[self.owner, :, :, :, lanes] += self.g[self.owner * 2 + p.core, :, :, :, lanes]
            return

        def todo():
            if name == "z":
                QuickScatter.finish(self, name)
                return
            for k in (1, 2, 3):
                self.plane_copy(k).wait_recv()
            mine = self.c_in[self.owner, :, p.y, :, lanes].astype(WIDE)
            for q in range(3):
                mine = mine + self.a_in[q, :, :, lanes].astype(WIDE)
            self.b_in[:, :, lanes] = mine.astype(LOW)

        self.owned(todo)

    def drain(self):
        self.core_copy(False).wait_send()

        def owned():
            self.plane_copy(1).wait_send()
            for copy in self.copies("z"):
                copy.wait_send()

        def others():
            self.plane_copy(2).wait_send()
            self.plane_copy(3).wait_send()

        self.owned(owned)
        self.others(others)


class SlowTotal:
    def __init__(self, place, own, got, sems, base):
        self.p, self.own, self.got, self.sems, self.base = place, own, got, sems, base

    def copies(self, k):
        p = self.p
        if k < 3:
            device = (p.core_peer, p.x_peer, p.y_peer)[k]()
            return [remote(self.own.at[k], self.got.at[k], self.sems, self.base + k, device)]
        return [
            remote(self.own.at[3], self.got.at[3 + d], self.sems, self.base + 2 + d, p.z_peer(d))
            for d in (1, 2, 3)
        ]

    def start(self, k):
        for copy in self.copies(k):
            copy.start()

    def finish(self, k):
        p = self.p
        for copy in self.copies(k):
            copy.wait_recv()
        if k < 3:
            self.own[k + 1] = self.own[k] + self.got[k]
            return None
        self.got[3] = self.own[3]
        out = None
        for z in range(DEPS):
            part = self.got[3 + lax.rem(p.z - z + DEPS, DEPS)]
            out = part if z == 0 else out + part
        return out

    def drain(self):
        for k in range(4):
            for copy in self.copies(k):
                copy.wait_send()


class Total:
    def __init__(self, place, own, got, sems, base):
        self.p, self.own, self.got, self.sems, self.base = place, own, got, sems, base

    def copies(self, k):
        p = self.p
        if k == 0:
            return [
                remote(self.own.at[0], self.got.at[n], self.sems, self.base + n, p.near(n))
                for n in range(1, 8)
            ]
        return [
            remote(self.own.at[1], self.got.at[8 + d], self.sems, self.base + 7 + d, p.z_peer(d))
            for d in (1, 2, 3)
        ]

    def start(self, k):
        for copy in self.copies(k):
            copy.start()

    def finish(self, k):
        p = self.p
        for copy in self.copies(k):
            copy.wait_recv()
        self.got[8 * k] = self.own[k]
        out = None
        if k == 0:
            for n in range(8):
                x = 1 - p.x if n & 4 else p.x
                y = 1 - p.y if n & 2 else p.y
                core = 1 - p.core if n & 1 else p.core
                part = self.got[x * 4 + y * 2 + core]
                out = part if n == 0 else out + part
            self.own[1] = out
            return None
        for z in range(DEPS):
            part = self.got[8 + lax.rem(p.z - z + DEPS, DEPS)]
            out = part if z == 0 else out + part
        return out

    def drain(self):
        for k in range(2):
            for copy in self.copies(k):
                copy.wait_send()


INPUTS = ("size", "images", "patches_in", "cot_in", "classes", "class_cot")
INPUTS += ("entry", "exit", "expand", "reduce", "entry_c", "exit_c", "expand_c", "reduce_c")
INPUTS += ("vec", "talking", "off", "vec_c", "off_c")
OUTPUTS = dict(
    patch_result=((ROWS, WIDTH), LOW),
    patch_grad=((ROWS, WIDTH), WIDE),
    class_result=((3, WIDTH), LOW),
    class_grad=((3, WIDTH), WIDE),
    blocks=((6, SHARD, WIDTH), WIDE),
    rows_early=((24, WIDTH), WIDE),
    rows_mid=((8, 512), WIDE),
    rows_late=((8, 128), WIDE),
)
COMM = {n: (SHAPE, LOW) for n in ("wa", "wa_c")}
COMM |= {n: (JOINED, LOW) for n in ("we", "wr", "we_c", "wr_c")}
COMM |= dict(
    wf=((PARTS, DEPS, 2, 16, WIDTH), LOW),
    turned=((2, DEPS, 2, SHARD, 256), LOW),
    early=((4, 24, WIDTH), WIDE),
    early_in=((7, 24, WIDTH), WIDE),
    mid=((2, 8, 512), WIDE),
    mid_in=((12, 8, 512), WIDE),
    late=((2, 8, 128), WIDE),
    late_in=((12, 8, 128), WIDE),
)
for _k in ("a", "e", "r", "ac"):
    COMM["c_in_" + _k] = ((2, DEPS, 2, SHARD, WIDTH), LOW)
    COMM["a_in_" + _k] = ((3 if _k == "a" else 2, DEPS, SHARD, WIDTH), LOW)
    COMM["b_in_" + _k] = ((DEPS, SHARD, WIDTH), LOW)
    COMM["z_in_" + _k] = ((3, SHARD, WIDTH), LOW)
SEMS = dict(g_send=67, g_recv=67, s_send=64, s_recv=64, t_send=28, t_recv=28, out=2, into=2)


def greet(p):
    barrier = pltpu.get_barrier_semaphore()
    peers = [p.z_peer(d) for d in (1, 2, 3)] + [p.near(n) for n in range(1, 8)]
    for peer in peers:
        pl.semaphore_signal(barrier, inc=1, device_id=peer, device_id_type=MESH)
    return lambda: pl.semaphore_wait(barrier, len(peers))


def layer_kernel(inner, *refs):
    r = Refs(**dict(zip([*INPUTS, *OUTPUTS, *SCRATCH, *COMM, *SEMS], refs, strict=True)))
    p = Place(inner)
    mine = p.x * 2 + p.core
    weights = dict(a=r.wa, e=r.we, r=r.wr, ac=r.wa_c, ec=r.we_c, rc=r.wr_c)
    grads = weights
    first = QuickGather(p, r.wa, (r.g_send, r.g_recv), 40)
    gathers, scatters = {}, {}
    for i, k in enumerate(CHUNKS):
        if k != "a":
            gathers[k] = Gather(p, weights[k], (r.g_send, r.g_recv), 8 * (i - 1))
        if k in ("ec", "rc"):
            continue
        ins = [getattr(r, n + "_in_" + k) for n in ("c", "a", "b", "z")]
        if k == "a":
            sems = (r.s_send, r.s_recv)
            last = [
                QuickScatter(p, r.wa, ins, sems, 40, 0),
                PartScatter(p, r.wa, ins, sems, 48, p.core),
                PartScatter(p, r.wa, ins, sems, 56, 1 - p.core),
            ]
        else:
            scatters[k] = Scatter(p, grads[k], ins, (r.s_send, r.s_recv), 8 * (i - 1))
    gathers["cf"] = Gather(p, r.wf, (r.g_send, r.g_recv), 59)
    early = SlowTotal(p, r.early, r.early_in, (r.t_send, r.t_recv), 0)
    mid = Total(p, r.mid, r.mid_in, (r.t_send, r.t_recv), 6)
    late = Total(p, r.late, r.late_in, (r.t_send, r.t_recv), 17)

    def go(*moves):
        def todo():
            for k, old, new in moves:
                if old:
                    gathers[k].wait(old)
                if new:
                    gathers[k].start(new)

        return todo

    def back(*moves):
        def todo():
            for k, old, new in moves:
                if k == "cf":
                    go((k, old, new))()
                    continue
                what = scatters.get(k) or early
                if old is not None:
                    what.finish(old)
                if new is not None:
                    what.start(new)

        return todo

    enter = greet(p)
    r.wa[mine, p.z, p.y] = jnp.concatenate([r.entry[...], r.exit[...]], 1)
    load = [
        pltpu.make_async_copy(r.patches_in, r.patches, r.into.at[0]),
        pltpu.make_async_copy(r.cot_in, r.cot, r.into.at[1]),
    ]
    load[0].start()
    load[1].start()
    enter()
    first.begin()
    part_of(r.we, mine, p.z, p.y)[...] = r.expand[...]
    part_of(r.wr, mine, p.z, p.y)[...] = r.reduce[...]
    r.wa_c[mine, p.z, p.y] = jnp.concatenate([r.entry_c[...], r.exit_c[...]], 1)
    part_of(r.we_c, mine, p.z, p.y)[...] = r.expand_c[...]
    part_of(r.wr_c, mine, p.z, p.y)[...] = r.reduce_c[...]
    columns(r)
    first.forward()
    go(("e", None, "z"), ("r", None, "z"))()
    masks(r)
    load[0].wait()
    norm_first(r)
    r.early[0] = jnp.zeros((24, WIDTH), WIDE)
    r.mid[0] = jnp.zeros((8, 512), WIDE)
    r.late[0] = jnp.zeros((8, 128), WIDE)
    first.across()
    first.end()
    go(("e", "z", "b"), ("ac", None, "z"), ("ec", None, "z"), ("rc", None, "z"), ("r", "z", "b"))()
    project(r)
    attend(r, gather_points(go))
    gathers["e"].wait("core")
    gathers["r"].wait("core")
    feed(r, feed_points(go))
    out_result = pltpu.make_async_copy(r.result, r.patch_result, r.out.at[0])
    out_result.start()
    def begin_class():
        gathers["ac"].wait("core")
        load[1].wait()

    def begin_feed():
        gathers["rc"].wait("a")
        gathers["rc"].start("core")
        gathers["ec"].wait("core")
        gathers["rc"].wait("core")
        for k in ("a", *CHUNKS[1:]):
            (first if k == "a" else gathers[k]).drain()

    def share(rows):
        r.wf[mine, p.z, p.y] = rows
        gathers["cf"].start("z")

    classes(r, (begin_class, begin_feed, share))
    scatters["ac"].start("core")
    ready = {n: functools.partial(scatters[n[0]].start, "core") for n in ("expand", "reduce")}
    feed_back(r, feed_back_points(back) | ready)
    attend_back(r, attend_back_points(back))
    weights_early(r)
    last[0].start("core")
    last[1].start("core")
    talking_back(r)
    project_back_start(r)
    mid.start(0)
    keys_back(r, keys_points(last, mid, back))
    weights_late(r)
    last[2].start("core")
    project_back(r)
    last[2].finish("core")
    last[2].start("a")
    late.start(0)
    out_grad = pltpu.make_async_copy(r.middle, r.patch_grad, r.out.at[1])
    out_grad.start()
    for n in (0, 1):
        last[n].finish("a")
        last[n].start("z")
    gathers["cf"].wait("core")
    class_weights(r, p)
    for i, k in ((1, "e"), (2, "r"), (3, "ac")):
        scatters[k].finish("z")
        r.blocks[i] = scatters[k].result()
    r.rows_early[...] = early.finish(3)
    late.finish(0)
    late.start(1)
    r.rows_mid[...] = mid.finish(1)
    last[2].finish("a")
    last[2].start("z")
    r.rows_late[...] = late.finish(1)
    for n in range(3):
        last[n].finish("z")
    r.blocks[0, :, 0:128] = last[0].result()
    r.blocks[0, :, 128:] = last[1].result()
    out_result.wait()
    out_grad.wait()
    for k in ("e", "r", "ac"):
        scatters[k].drain()
    gathers["cf"].drain()
    for k in last:
        k.drain()
    early.drain()
    mid.drain()
    late.drain()


def gather_points(go):
    return {
        0: go(("e", "b", "a")),
        2: go(("ac", "z", "b")),
        3: go(("r", "b", "a")),
        5: go(("e", "a", "core"), ("ec", "z", "b")),
        6: go(("ac", "b", "a")),
        8: go(("r", "a", "core"), ("rc", "z", "b")),
        9: go(("ec", "b", "a")),
        11: go(("ac", "a", "core")),
    }


def feed_points(go):
    return {0: go(("rc", "b", "a")), 2: go(("ec", "a", "core"))}


def keys_points(last, mid, back):
    def core(n):
        def todo():
            last[n].finish("core")
            last[n].start("a")

        return todo

    def middle():
        mid.finish(0)
        mid.start(1)

    return {0: core(0), 1: core(1), 4: middle}


def feed_back_points(back):
    return {
        0: back(("cf", "z", "b")),
        2: back(("cf", "b", "a"), ("ac", "core", "a")),
    }


def attend_back_points(back):
    return {
        0: back(("cf", "a", "core")),
        2: back(("ac", "a", "b"), ("e", "core", "a")),
        4: back(("r", "core", "a"), ("ac", "b", "z"), ("early", None, 0)),
        6: back(("e", "a", "b"), ("early", 0, 1)),
        8: back(("r", "a", "b"), ("e", "b", "z"), ("early", 1, 2)),
        10: back(("r", "b", "z"), ("early", 2, 3)),
    }


def finish_kernel(inner, *refs):
    r = Refs(**dict(zip([*(n + "_in" for n in OUTPUTS), *FINAL], refs, strict=True)))
    r.patch_result[...] = r.patch_result_in[...]
    r.patch_grad[...] = r.patch_grad_in[...]
    r.class_result[...] = r.class_result_in[...]
    r.class_grad[...] = r.class_grad_in[...]
    r.g_entry_c[...] = r.blocks_in[3, :, 0:COLS]
    r.g_exit_c[...] = r.blocks_in[3, :, COLS:]
    part = lax.axis_index("tensor") // inner[1]
    block = r.blocks_in[0]
    one, two, three = block[:, 0:96], block[:, 96:192], block[:, 192:]
    outer = (part == 0) | (part == 3)
    inside = jnp.where(
        part == 1, jnp.concatenate([one, three], 1), jnp.concatenate([three, one], 1)
    )
    r.g_entry[...] = jnp.where(outer, block[:, 0:COLS], inside)
    r.g_exit[...] = jnp.where(outer, block[:, COLS:], two)
    for i, c in ((0, ""), (3, "_c")):
        getattr(r, "g_expand" + c)[...] = r.blocks_in[i + 1]
        getattr(r, "g_reduce" + c)[...] = r.blocks_in[i + 2]
    for k in range(2):
        for n in range(3):
            r.g_vec[k : k + 1, 128 * n : 128 * n + 128] = r.rows_late_in[3 * k + n : 3 * k + n + 1, :]
    r.g_vec[2:4, :] = r.rows_mid_in[0:2, 0:WIDTH]
    r.g_vec[4:10, :] = r.rows_early_in[0:6, :]
    r.g_vec_c[...] = r.rows_early_in[10:20, :]
    for j in range(PARTS):
        part = slice(WIDTH * j, WIDTH * (j + 1))
        r.g_off[part] = r.rows_early_in[6 + j : 7 + j, :].reshape(WIDTH)
        r.g_off_c[part] = r.rows_early_in[20 + j : 21 + j, :].reshape(WIDTH)
    talk = r.rows_mid_in[:, WIDTH:]
    turned = jnp.concatenate([talk, jnp.zeros((120, 128), WIDE)], 0).T
    lane = iota((8, 128), 1)
    moved = pltpu.roll(turned[8:16], 8, 1)
    r.g_talking[...] = jnp.where((lane >= 8) & (lane < 16), moved, talk)[:, 0:17]


FINAL = dict(
    patch_result=((ROWS, WIDTH), LOW),
    class_result=((3, WIDTH), LOW),
    patch_grad=((ROWS, WIDTH), WIDE),
    class_grad=((3, WIDTH), WIDE),
    g_entry=((SHARD, COLS), WIDE),
    g_exit=((SHARD, 96), WIDE),
    g_expand=((SHARD, WIDTH), WIDE),
    g_reduce=((SHARD, WIDTH), WIDE),
    g_vec=((10, WIDTH), WIDE),
    g_talking=((8, 17), WIDE),
    g_off=((FF,), WIDE),
    g_entry_c=((SHARD, COLS), WIDE),
    g_exit_c=((SHARD, 96), WIDE),
    g_expand_c=((SHARD, WIDTH), WIDE),
    g_reduce_c=((SHARD, WIDTH), WIDE),
    g_vec_c=((10, WIDTH), WIDE),
    g_off_c=((FF,), WIDE),
)


def layers(inner, *args):
    smem = pl.BlockSpec(memory_space=pltpu.SMEM)
    vmem = pl.BlockSpec(memory_space=pltpu.VMEM)
    hbm = pl.BlockSpec(memory_space=pl.ANY)
    sems = [pltpu.SemaphoreType.DMA((n,)) for n in SEMS.values()]
    mid = pl.pallas_call(
        functools.partial(layer_kernel, inner),
        out_shape=[jax.ShapeDtypeStruct(*s) for s in OUTPUTS.values()],
        in_specs=[smem, smem, hbm, hbm] + [vmem] * (len(INPUTS) - 4),
        out_specs=[hbm, hbm] + [vmem] * (len(OUTPUTS) - 2),
        scratch_shapes=[pltpu.VMEM(*s) for s in (SCRATCH | COMM).values()] + sems,
        compiler_params=pltpu.CompilerParams(
            vmem_limit_bytes=63 * 2**20, collective_id=0, has_side_effects=True
        ),
    )(*args)
    out = pl.pallas_call(
        functools.partial(finish_kernel, inner),
        out_shape=[jax.ShapeDtypeStruct(*s) for s in FINAL.values()],
        in_specs=[vmem] * len(OUTPUTS),
        out_specs=[vmem] * len(FINAL),
    )(*mid)
    return dict(zip(FINAL, out, strict=True))


def groups(axis, inner):
    return [[inner * k + i for i in range(inner)] for k in range(lax.axis_size(axis) // inner)]


def widen(x, inner, dims):
    for axis, n, dim in zip(("dp", "tensor"), inner, dims, strict=True):
        if n > 1:
            x = lax.all_gather(x, axis, axis=dim, tiled=True, axis_index_groups=groups(axis, n))
    return x


def narrow(x, inner, dims):
    for axis, n, dim in zip(("dp", "tensor"), inner, dims, strict=True):
        if n > 1:
            x = lax.psum_scatter(
                x, axis, scatter_dimension=dim, tiled=True, axis_index_groups=groups(axis, n)
            )
    return x


def whole(x, inner):
    for axis, n in zip(("dp", "tensor"), inner, strict=True):
        if n > 1:
            x = lax.psum(x, axis, axis_index_groups=groups(axis, n))
    return x


KINDS = ((0, 1),) * 4


def local(
    patches,
    classes,
    group_size,
    image_count,
    self_entry,
    self_exit,
    self_expand,
    self_reduce,
    self_vectors,
    self_talking,
    self_offset,
    class_entry,
    class_exit,
    class_expand,
    class_reduce,
    class_vectors,
    class_offset,
    patch_cotangent,
    class_cotangent,
):
    inner = (lax.axis_size("dp") // 8, lax.axis_size("tensor") // 4)
    weights = [
        widen(w, inner, dims)
        for w, dims in zip(
            (
                self_entry,
                self_exit,
                self_expand,
                self_reduce.T,
                class_entry,
                class_exit,
                class_expand,
                class_reduce.T,
            ),
            KINDS * 2,
            strict=True,
        )
    ]
    out = layers(
        inner,
        group_size,
        image_count,
        patches,
        patch_cotangent,
        classes,
        class_cotangent,
        *weights,
        self_vectors,
        self_talking.T,
        self_offset,
        class_vectors,
        class_offset,
    )
    names = ("entry", "exit", "expand", "reduce")
    own = [narrow(out["g_" + n], inner, dims) for n, dims in zip(names, KINDS, strict=True)]
    own_c = [narrow(out["g_" + n + "_c"], inner, dims) for n, dims in zip(names, KINDS, strict=True)]
    return (
        out["patch_result"],
        out["class_result"],
        out["patch_grad"],
        out["class_grad"],
        *own[:3],
        own[3].T,
        whole(out["g_vec"], inner),
        whole(out["g_talking"], inner).T,
        whole(out["g_off"], inner),
        *own_c[:3],
        own_c[3].T,
        whole(out["g_vec_c"], inner),
        whole(out["g_off_c"], inner),
    )


def solution(mesh):
    both = P(("dp", "tensor"), None)
    weights = (P("dp", "tensor"), P("dp", "tensor"), P("dp", "tensor"), P("tensor", "dp"))
    return jax.shard_map(
        local,
        mesh=mesh,
        in_specs=(
            both,
            both,
            P(("dp", "tensor")),
            P(("dp", "tensor")),
            *weights,
            P(),
            P(),
            P(),
            *weights,
            P(),
            P(),
            both,
            both,
        ),
        out_specs=(both, both, both, both, *weights, P(), P(), P(), *weights, P(), P()),
        check_vma=False,
    )
```

```python
import functools

import jax
import jax.numpy as jnp
from jax import lax
from jax.experimental import pallas as pl
from jax.experimental.pallas import tpu as pltpu
from jax.sharding import PartitionSpec as P

HEADS = 8
EPSILON = 1e-06
NEGATIVE = -1e30
ROOT_HALF = 0.7071067811865476
ROOT_TWO_PI = 2.5066282746310002
WIDE = jnp.float32
LOW = jnp.bfloat16

WIDTH = 384
DEPTH = WIDTH // HEADS
ROWS = 768
FF = 1536
PARTS = 4
COLS = 3 * WIDTH // PARTS
TILE = 128
SPAN = HEADS * TILE
HALVES = (slice(0, SPAN // 2), slice(SPAN // 2, SPAN))
WIDE_HALVES = (slice(0, FF // 2), slice(FF // 2, FF))
SHARD = 48
DEPS = 4
STEPS = ROWS // TILE
TOGETHER = 1
KEYS = ROWS + 128
DENSE = 384
PAIRS = HEADS * 8


def nn(a, b):
    return lax.dot_general(a, b, (((1,), (0,)), ((), ())), preferred_element_type=WIDE)


def nt(a, b):
    return lax.dot_general(a, b, (((1,), (1,)), ((), ())), preferred_element_type=WIDE)


def iota(shape, dim):
    return lax.broadcasted_iota(jnp.int32, shape, dim)


def rows_at(i, size):
    if isinstance(i, int):
        return slice(i * size, (i + 1) * size)
    return pl.ds(pl.multiple_of(i * size, size), size)


def normalize(x, gain, shift):
    mean = jnp.mean(x, -1, keepdims=True)
    centered = x - mean
    inverse = lax.rsqrt(jnp.mean(centered * centered, -1, keepdims=True) + EPSILON)
    unit = centered * inverse
    return unit * gain + shift, unit, inverse


def keep_stats(r, k, rows, x, inverse):
    r.stats[rows, 2 * k : 2 * k + 1] = jnp.mean(x, -1, keepdims=True)
    r.stats[rows, 2 * k + 1 : 2 * k + 2] = inverse


def unit_of(r, k, rows, x):
    inverse = r.stats[rows, 2 * k + 1 : 2 * k + 2]
    return (x - r.stats[rows, 2 * k : 2 * k + 1]) * inverse, inverse


def normalize_back(grad, gain, unit, inverse):
    scaled = grad * gain
    inner = jnp.mean(scaled * unit, -1, keepdims=True)
    return inverse * (scaled - jnp.mean(scaled, -1, keepdims=True) - unit * inner)


def by_head(x):
    return jnp.sum(x.reshape(HEADS, DEPTH, x.shape[-1]), 1)


def total(x):
    return jnp.sum(x, 0, keepdims=True)


def smooth(hidden):
    cdf = 0.5 * (1.0 + lax.erf(hidden * ROOT_HALF))
    slope = cdf + hidden * jnp.exp(-0.5 * hidden * hidden) * (1.0 / ROOT_TWO_PI)
    return (hidden * cdf).astype(LOW), slope.astype(LOW)


def each(count, together, step, points):
    def some(i, c):
        for k in range(together):

            def at(where):
                for key, todo in points.items():
                    if isinstance(key, str):
                        continue
                    t, place = divmod(key, 2)
                    if place == where and t % together == k:
                        pl.when(i == t // together)(todo)

            step(i * together + k, at)
        return c

    lax.fori_loop(0, count // together, some, 0)


class Refs:
    def __init__(self, **refs):
        self.__dict__.update(refs)


SCRATCH = dict(
    cols=((WIDTH, 128), WIDE),
    pad=((128, 128), WIDE),
    patches=((ROWS, WIDTH), LOW),
    cot=((ROWS, WIDTH), LOW),
    result=((ROWS, WIDTH), LOW),
    n1=((ROWS, WIDTH), LOW),
    stats=((ROWS, 128), WIDE),
    went=((3 * WIDTH, WIDTH), LOW),
    wout=((WIDTH, WIDTH), LOW),
    wback=((WIDTH, WIDTH), LOW),
    wfull=((WIDTH, 3 * WIDTH), LOW),
    qt=((WIDTH, ROWS), LOW),
    kext=((ROWS, 512), LOW),
    kt=((WIDTH, ROWS), LOW),
    vext=((ROWS, 512), LOW),
    vt=((WIDTH, ROWS), LOW),
    hot=((ROWS, 128), LOW),
    hott=((8, ROWS), WIDE),
    vsum=((WIDTH, 128), WIDE),
    gsum=((WIDTH, 128), WIDE),
    qm=((512, SPAN), LOW),
    qn=((WIDTH, SPAN), LOW),
    et=((STEPS + 1, ROWS, SPAN), LOW),
    un=((STEPS, WIDTH, SPAN), LOW),
    linv=((STEPS, 1, SPAN), WIDE),
    attt=((WIDTH, ROWS), LOW),
    middle=((ROWS, WIDTH), WIDE),
    branch1=((ROWS, WIDTH), LOW),
    branch2=((ROWS, WIDTH), WIDE),
    n2t=((WIDTH, ROWS), LOW),
    act=((ROWS, FF), LOW),
    slope=((ROWS, FF), LOW),
    next=((KEYS, WIDTH), LOW),
    wout_c=((WIDTH, WIDTH), LOW),
    small8=((8, WIDTH), WIDE),
    cot8=((8, WIDTH), WIDE),
    both=((KEYS, 128), LOW),
    qkwv=((128, WIDTH), LOW),
    d1t=((WIDTH, ROWS), LOW),
    d2t=((WIDTH, ROWS), LOW),
    dot=((WIDTH, ROWS), LOW),
    gwout=((WIDTH, WIDTH), WIDE),
    sums=((8, WIDTH), WIDE),
    offset=((1, FF), WIDE),
    dvt=((WIDTH, ROWS), WIDE),
    dkt=((WIDTH, ROWS), WIDE),
    accp=((HEADS, HEADS, TILE), WIDE),
    accq=((HEADS, HEADS, TILE), WIDE),
    dtr=((3 * WIDTH, ROWS), LOW),
)


def block_of(w, j):
    return w[j].reshape(WIDTH, w.shape[-1])


def whole_of(w):
    return w[...].reshape(WIDTH, FF)


def as_block(x):
    return x.reshape(DEPS, 2, SHARD, x.shape[-1])


def unpack_weights(wa, went, wout):
    for j in range(PARTS):
        block = block_of(wa, j).T
        went[COLS * j : COLS * (j + 1), :] = block[:COLS]
        wout[96 * j : 96 * (j + 1), :] = block[COLS:]

def columns(r):
    r.pad[...] = jnp.zeros((128, 128), WIDE)
    r.pad[0:8, 0:17] = r.talking[...]
    turned = r.pad[...]
    talk = turned.T
    turned = turned[0:8]
    moved = pltpu.roll(talk, 8, 1)[8:16]
    lane = iota((8, 128), 1)
    alone = jnp.sum(talk[8:16], 1, keepdims=True) + turned[:, 16:17]
    base = jnp.where(lane < 8, turned * DEPTH ** (-0.5), moved)
    base = jnp.where(lane == 16, turned, base)
    base = jnp.where(lane == 19, alone, base)
    turned = r.vec[0:8, :].T
    lane = iota((DEPTH, 128), 1)
    for h in range(HEADS):
        rows = slice(DEPTH * h, DEPTH * (h + 1))
        x = jnp.broadcast_to(base[h : h + 1], (DEPTH, 128))
        x = jnp.where(lane == 17, turned[rows, 2:3], x)
        r.cols[rows, :] = jnp.where(lane == 18, turned[rows, 3:4], x)


def masks(r):
    size, images = r.size[0], r.images[0]
    place = iota((ROWS, 128), 0)
    which = iota((ROWS, 128), 1)
    inside = (place >= which * size) & (place < which * size + size) & (which < images)
    r.hot[...] = jnp.where(inside, 1.0, 0.0).astype(LOW)
    r.kext[:, WIDTH:] = jnp.where(inside | (which >= 3), 0.0, NEGATIVE).astype(LOW)
    r.vext[:, WIDTH:] = jnp.where(which < 2, 1.0, 0.0).astype(LOW)
    place = iota((8, ROWS), 1)
    which = iota((8, ROWS), 0)
    inside = (place >= which * size) & (place < which * size + size) & (which < images)
    r.hott[...] = jnp.where(inside, 1.0, 0.0)


def norm_first(r):
    gain, shift = r.vec[0:1, :], r.vec[1:2, :]

    def norm_step(i, c):
        rows = rows_at(i, DENSE)
        x = r.patches[rows, :].astype(WIDE)
        normed, unit, inverse = normalize(x, gain, shift)
        r.n1[rows, :] = normed.astype(LOW)
        keep_stats(r, 0, rows, x, inverse)
        return c

    lax.fori_loop(0, ROWS // DENSE, norm_step, 0)


def project(r):
    unpack_weights(r.wa, r.went, r.wout)

    def step(i, c):
        rows = rows_at(i, DENSE)
        normed = r.n1[rows, :]
        turned = nt(r.went[...], normed)
        r.qt[:, rows] = (turned[0:WIDTH] + r.cols[:, 17:18]).astype(LOW)
        r.kt[:, rows] = turned[WIDTH : 2 * WIDTH].astype(LOW)
        r.vt[:, rows] = (turned[2 * WIDTH :] + r.cols[:, 18:19]).astype(LOW)
        both = nt(normed, r.went[WIDTH:, :])
        r.kext[rows, 0:WIDTH] = both[:, 0:WIDTH].astype(LOW)
        r.vext[rows, 0:WIDTH] = (both[:, WIDTH:] + r.vec[3:4, :]).astype(LOW)
        return c

    lax.fori_loop(0, ROWS // DENSE, step, 0)
    r.vsum[...] = nn(r.vt[...], r.hot[...])
    r.wback[...] = r.wout[...].T
    r.wfull[:, 0:WIDTH] = r.went[0:WIDTH, :].T
    r.wfull[:, WIDTH : 2 * WIDTH] = r.went[2 * WIDTH :, :].T
    r.wfull[:, 2 * WIDTH :] = r.went[WIDTH : 2 * WIDTH, :].T


def attend(r, points):
    def step(t, at):
        at(0)
        rows = rows_at(t, TILE)
        q = r.qt[:, rows].astype(WIDE)
        hot = r.hott[:, rows]
        hot_rows = jnp.concatenate([hot, jnp.zeros((120, TILE), WIDE)], 0).astype(LOW)
        for g in range(HEADS):
            r.qm[0:WIDTH, TILE * g : TILE * (g + 1)] = (q * r.cols[:, g : g + 1]).astype(LOW)
            r.qm[WIDTH:, TILE * g : TILE * (g + 1)] = hot_rows
        own = r.vt[:, rows].astype(WIDE)
        att = r.cols[:, 16:17] * (
            r.vsum[:, 0:1] * hot[0:1] + r.vsum[:, 1:2] * hot[1:2] + r.vsum[:, 2:3] * hot[2:3]
        )
        for half in HALVES:
            scores = nn(r.kext[...], r.qm[:, half])
            raised = jnp.exp(scores - jnp.max(scores, 0, keepdims=True))
            r.linv[t, :, half] = 1.0 / jnp.sum(raised, 0, keepdims=True)
            r.et[t + 1, :, half] = raised.astype(LOW)
        at(1)
        for i, half in enumerate(HALVES):
            mean = nn(r.vt[...], r.et[t + 1, :, half]) * r.linv[t, :, half]
            r.un[t, :, half] = mean.astype(LOW)
            for k in range(HEADS // 2):
                h = HEADS // 2 * i + k
                att = att + r.cols[:, 8 + h : 9 + h] * mean[:, TILE * k : TILE * (k + 1)]
        live = (hot[0:1] + hot[1:2] + hot[2:3]) > 0.5
        att = jnp.where(live, att, r.cols[:, 19:20] * own).astype(LOW)
        r.attt[:, rows] = att
        branch = nt(att.T, r.wout[...]) + r.vec[4:5, :]
        r.branch1[rows, :] = branch.astype(LOW)
        r.middle[rows, :] = r.patches[rows, :].astype(WIDE) + r.vec[5:6, :] * branch

    each(STEPS, TOGETHER, step, points)


def feed(r, points):
    def step(i, at):
        at(0)
        rows = rows_at(i, DENSE)
        middle = r.middle[rows, :]
        normed, unit, inverse = normalize(middle, r.vec[6:7, :], r.vec[7:8, :])
        keep_stats(r, 1, rows, middle, inverse)
        normed = normed.astype(LOW)
        r.n2t[:, rows] = normed.T
        hidden = [nn(normed, whole_of(r.we)[:, half]) + r.off[half].reshape(1, FF // 2) for half in WIDE_HALVES]
        for half, part in zip(WIDE_HALVES, hidden, strict=True):
            active, slope = smooth(part)
            r.act[rows, half] = active
            r.slope[rows, half] = slope
        at(1)
        lifted = nt(whole_of(r.wr), r.act[rows, :]).T
        branch = lifted + r.vec[8:9, :]
        r.branch2[rows, :] = branch
        first = middle + r.vec[9:10, :] * branch
        r.result[rows, :] = first.astype(LOW)
        normed, unit, inverse = normalize(first, r.vec_c[0:1, :], r.vec_c[1:2, :])
        r.next[rows, :] = normed.astype(LOW)
        keep_stats(r, 2, rows, first, inverse)

    each(ROWS // DENSE, 1, step, points)


def classes(r, points):
    v = lambda k: r.vec_c[k : k + 1, :]
    scale = DEPTH ** (-0.5)
    points[0]()
    unpack_weights(r.wa_c, r.went, r.wout_c)
    wq, wk, wv = (r.went[WIDTH * k : WIDTH * (k + 1), :] for k in range(3))
    r.small8[...] = jnp.zeros((8, WIDTH), WIDE)
    r.cot8[...] = jnp.zeros((8, WIDTH), WIDE)
    r.small8[0:3, :] = r.classes[...].astype(WIDE)
    r.cot8[0:3, :] = r.class_cot[...].astype(WIDE)
    tokens = r.small8[...]
    normed, unit, inverse = normalize(tokens, v(0), v(1))
    low = normed.astype(LOW)
    valid = iota((128, WIDTH), 0) < 3
    r.next[ROWS:, :] = jnp.where(
        valid, jnp.concatenate([normed, jnp.zeros((120, WIDTH), WIDE)], 0), 0.0
    ).astype(LOW)
    head_of = iota((PAIRS, WIDTH), 1) // DEPTH
    own_head = head_of == iota((PAIRS, WIDTH), 0) // 8

    def spread(x):
        return jnp.where(own_head, jnp.concatenate([x] * HEADS, 0), 0.0)

    def gather_heads(x):
        x = jnp.where(own_head, x, 0.0)
        out = x[0:8]
        for h in range(1, HEADS):
            out = out + x[8 * h : 8 * (h + 1)]
        return out

    queries = (nt(low, wq) + v(2)).astype(LOW)
    qexp = spread(queries.astype(WIDE))
    qk = (nn(qexp.astype(LOW), wk) * scale).astype(LOW)
    keys = r.next[...]
    points[3]()
    scores = nt(qk, keys)
    size, images = r.size[0], r.images[0]
    slot = iota((PAIRS, KEYS), 0) & 7
    place = iota((PAIRS, KEYS), 1)
    allowed = (place >= slot * size) & (place < slot * size + size) & (slot < images)
    allowed = allowed | (place == slot + ROWS)
    scores = jnp.where(allowed, scores, NEGATIVE)
    raised = jnp.exp(scores - jnp.max(scores, -1, keepdims=True))
    probs = raised / jnp.sum(raised, -1, keepdims=True)
    probs_low = probs.astype(LOW)
    mass = jnp.sum(probs_low.astype(WIDE), -1, keepdims=True)
    z = nn(probs_low, keys).astype(LOW)
    attended = gather_heads(nt(z, wv) + mass * v(3)).astype(LOW)
    branch = nt(attended, r.wout_c[...]) + v(4)
    middle = tokens + v(5) * branch
    normed2, unit2, inverse2 = normalize(middle, v(6), v(7))
    low2 = normed2.astype(LOW)
    grad = r.cot8[...]
    delta2 = (v(9) * grad).astype(LOW)
    points[2](jnp.concatenate([low2.astype(WIDE), delta2.astype(WIDE)], 0).astype(LOW))
    points[1]()
    expand = whole_of(r.we_c)
    hidden = nn(low2, expand) + r.off_c[...].reshape(1, FF)
    active, slope = smooth(hidden)
    points[4]()
    reduce = whole_of(r.wr_c)
    lifted = nt(active, reduce)
    branch2 = lifted + v(8)
    second = middle + v(9) * branch2
    r.class_result[...] = second[0:3].astype(LOW)
    grad_scale2 = total(grad * branch2)
    grad_bias2 = total(delta2.astype(WIDE))
    grad_hidden = (nn(delta2, reduce) * slope.astype(WIDE)).astype(LOW)
    off = total(grad_hidden.astype(WIDE))
    for j in range(PARTS):
        r.early[0, 20 + j : 21 + j, :] = off[:, WIDTH * j : WIDTH * (j + 1)]
    back = nt(grad_hidden, expand)
    grad_gain2, grad_shift2 = total(back * unit2), total(back)
    grad = grad + normalize_back(back, v(6), unit2, inverse2)
    grad_scale = total(grad * branch)
    delta = (v(5) * grad).astype(LOW)
    grad_bias = total(delta.astype(WIDE))
    gatt = nn(delta, r.wout_c[...]).astype(LOW)
    dexp = spread(gatt.astype(WIDE))
    wide_v = nn(dexp.astype(LOW), wv).astype(LOW)
    gp = nt(wide_v, keys)
    ds = (probs * (gp - jnp.sum(gp * probs, -1, keepdims=True))).astype(LOW)
    y = nn(ds, keys).astype(LOW)
    gq = (gather_heads(nt(y, wk)) * scale).astype(LOW)
    both = jnp.concatenate([ds.astype(WIDE), probs_low.astype(WIDE)], 0).T.astype(LOW)
    r.both[...] = both
    r.qkwv[...] = jnp.concatenate([qk, wide_v], 0)
    grad_normed = nn(both[ROWS:, :], r.qkwv[...])[0:8] + nn(gq, wq)
    r.class_grad[...] = (grad + normalize_back(grad_normed, v(0), unit, inverse))[0:3]
    valid8 = iota((8, WIDTH), 0) < 3
    grad_normed = jnp.where(valid8, grad_normed, 0.0)
    gq_t = gq.astype(WIDE).T.astype(LOW)
    grad_q = nn(gq_t, low)
    grad_k = nn((qexp * scale).T.astype(LOW), y)
    grad_v = nn(dexp.T.astype(LOW), z)
    grad_out = nn(delta.astype(WIDE).T.astype(LOW), attended)
    whole = jnp.concatenate([grad_q, grad_k, grad_v], 0)
    for j in range(PARTS):
        block = jnp.concatenate(
            [whole[COLS * j : COLS * (j + 1)], grad_out[96 * j : 96 * (j + 1)]], 0
        )
        r.wa_c[j] = as_block(block.T.astype(LOW))
    grad_vb = total(jnp.where(own_head, mass * dexp, 0.0))
    r.early[0, 10:20, :] = jnp.concatenate(
        [
            total(grad_normed * unit),
            total(grad_normed),
            total(gq.astype(WIDE)),
            grad_vb,
            grad_bias,
            grad_scale,
            grad_gain2,
            grad_shift2,
            grad_bias2,
            grad_scale2,
        ],
        0,
    )


def class_weights(r, p):
    rows = r.wf[...].astype(WIDE).reshape(32, 16, WIDTH)
    normed, delta = (rows[:, k : k + 8].reshape(256, WIDTH) for k in (0, 8))
    for k, x in enumerate((normed, delta)):
        r.turned[k] = x.T.astype(LOW).reshape(DEPS, 2, SHARD, 256)
    part = p.x * 2 + p.core
    offset = r.off_c[0:WIDTH]
    for j in range(1, PARTS):
        offset = jnp.where(part == j, r.off_c[WIDTH * j : WIDTH * (j + 1)], offset)
    expand = part_of(r.we_c, part)[...].reshape(WIDTH, WIDTH)
    reduce = part_of(r.wr_c, part)[...].reshape(WIDTH, WIDTH)
    hidden = nn(normed.astype(LOW), expand) + offset.reshape(1, WIDTH)
    active, slope = smooth(hidden)
    grad_hidden = (nn(delta.astype(LOW), reduce) * slope.astype(WIDE)).astype(LOW)
    r.blocks[4] = nn(r.turned[0, p.z, p.y], grad_hidden)
    r.blocks[5] = nn(r.turned[1, p.z, p.y], active)


def feed_back(r, points):
    size, images = r.size[0], r.images[0]
    r.early[0, 0:10, :] = jnp.zeros((10, WIDTH), WIDE)
    r.offset[...] = jnp.zeros((1, FF), WIDE)

    def add(k, x):
        r.early[0, k - 4 : k - 3, :] += total(x)

    def step(i, at):
        at(0)
        rows = rows_at(i, DENSE)
        branch2 = r.branch2[rows, :]
        unitc, inversec = unit_of(r, 2, rows, r.middle[rows, :] + r.vec[9:10, :] * branch2)
        dn = nn(r.both[rows, :], r.qkwv[...])
        add(14, dn * unitc)
        add(15, dn)
        grad = normalize_back(dn, r.vec_c[0:1, :], unitc, inversec)
        place = iota((DENSE, WIDTH), 0) + i * DENSE
        grad = grad + jnp.where(place < size * images, r.cot[rows, :].astype(WIDE), 0.0)
        add(9, grad * branch2)
        delta = (r.vec[9:10, :] * grad).astype(LOW)
        add(8, delta.astype(WIDE))
        r.d2t[:, rows] = delta.T
        grad_hidden = [
            (nn(delta, whole_of(r.wr)[:, half]) * r.slope[rows, half].astype(WIDE)).astype(LOW)
            for half in WIDE_HALVES
        ]
        for half, part in zip(WIDE_HALVES, grad_hidden, strict=True):
            r.slope[rows, half] = part
            r.offset[:, half] += total(part.astype(WIDE))
        at(1)
        back = nt(whole_of(r.we), r.slope[rows, :]).T
        unit, inverse = unit_of(r, 1, rows, r.middle[rows, :])
        add(6, back * unit)
        add(7, back)
        grad = grad + normalize_back(back, r.vec[6:7, :], unit, inverse)
        r.middle[rows, :] = grad
        add(5, grad * r.branch1[rows, :].astype(WIDE))
        delta = (r.vec[5:6, :] * grad).astype(LOW)
        add(4, delta.astype(WIDE))
        r.d1t[:, rows] = delta.T
        r.dot[:, rows] = nt(r.wback[...], delta).astype(LOW)

    each(ROWS // DENSE, 1, step, points)
    for half in WIDE_HALVES:
        r.we[:, :, :, half] = as_block(nn(r.n2t[...], r.slope[:, half]).astype(LOW))
    points["expand"]()
    for half in WIDE_HALVES:
        r.wr[:, :, :, half] = as_block(nn(r.d2t[...], r.act[:, half]).astype(LOW))
    points["reduce"]()
    for j in range(PARTS):
        r.early[0, 6 + j : 7 + j, :] = r.offset[:, WIDTH * j : WIDTH * (j + 1)]
    r.gwout[...] = nt(r.d1t[...], r.attt[...])


def attend_back(r, points):
    r.dvt[...] = jnp.zeros((WIDTH, ROWS), WIDE)
    r.accp[...] = jnp.zeros((HEADS, HEADS, TILE), WIDE)
    r.accq[...] = jnp.zeros((HEADS, HEADS, TILE), WIDE)

    def step(t, at):
        at(0)
        rows = rows_at(t, TILE)
        grad = r.dot[:, rows].astype(WIDE)
        inverse = r.linv[t]
        place = iota((128, TILE), 0)
        for h in range(HEADS):
            part = slice(TILE * h, TILE * (h + 1))
            post = r.cols[:, 8 + h : 9 + h]
            w = grad * r.un[t, :, part].astype(WIDE)
            r.accp[h] += by_head(w)
            minus = -inverse[:, part] * total(post * w)
            high = minus.astype(LOW).astype(WIDE)
            r.qm[0:WIDTH, part] = (grad * post * inverse[:, part]).astype(LOW)
            extra = jnp.where(place == 0, high, jnp.where(place == 1, minus - high, 0.0))
            r.qm[WIDTH:, part] = extra.astype(LOW)
        q = r.qt[:, rows].astype(WIDE)
        for half in HALVES:
            gp = nn(r.vext[...], r.qm[:, half])
            r.et[t, :, half] = (r.et[t + 1, :, half].astype(WIDE) * gp).astype(LOW)
        r.dvt[...] += nt(r.qm[0:WIDTH, :], r.et[t + 1])
        at(1)
        dq = jnp.zeros((WIDTH, TILE), WIDE)
        for i, half in enumerate(HALVES):
            y = nn(r.kt[...], r.et[t, :, half])
            for k in range(HEADS // 2):
                g = HEADS // 2 * i + k
                part = y[:, TILE * k : TILE * (k + 1)]
                dq = dq + r.cols[:, g : g + 1] * part
                r.accq[g] += by_head(q * part)
        r.dtr[0:WIDTH, rows] = dq.astype(LOW)

    each(STEPS, TOGETHER, step, points)
    r.gsum[...] = nn(r.dot[...], r.hot[...])
    bias = r.cols[:, 16:17]
    for k in range(3):
        r.dvt[...] += (bias * r.gsum[:, k : k + 1]) * r.hott[k : k + 1, :]
    r.dtr[WIDTH : 2 * WIDTH, :] = r.dvt[...].astype(LOW)


def keys_back(r, points):
    for t in range(STEPS):
        if t in points:
            points[t]()
        q = r.qt[:, rows_at(t, TILE)].astype(WIDE)
        mixed = r.qn if t % 2 else r.qm
        for g in range(HEADS):
            mixed[0:WIDTH, TILE * g : TILE * (g + 1)] = (q * r.cols[:, g : g + 1]).astype(LOW)
        part = nt(mixed[0:WIDTH, :], r.et[t])
        r.dkt[...] = part if t == 0 else r.dkt[...] + part
    r.dtr[2 * WIDTH :, :] = r.dkt[...].astype(LOW)


def talking_back(r):
    lane = iota((HEADS, 128), 1)

    def lanes_sum(x):
        return jnp.sum(x, -1, keepdims=True)

    out = jnp.where(lane == 2 * HEADS, lanes_sum(by_head(r.gsum[...] * r.vsum[...])), 0.0)
    for h in range(HEADS):
        out = out + jnp.where(lane == h, lanes_sum(r.accq[h]) * DEPTH ** (-0.5), 0.0)
        out = out + jnp.where(lane == HEADS + h, lanes_sum(r.accp[h]), 0.0)
    r.mid[0, :, WIDTH:] = out


def store_grads(r, j, part, rows):
    lanes = rows.shape[0]
    block = rows.T.astype(LOW).reshape(DEPS, 2, SHARD, lanes)
    r.wa[j, :, :, :, 128 * part : 128 * part + lanes] = block


def weights_early(r):
    whole = nn(r.dtr[0 : 2 * WIDTH, :], r.n1[...])
    query, value = whole[0:WIDTH], whole[WIDTH:]
    gwout = r.gwout
    store_grads(r, 0, 0, jnp.concatenate([query[0:288], gwout[0:96, :]], 0))
    store_grads(r, 1, 0, jnp.concatenate([query[288:], gwout[96:128, :]], 0))
    store_grads(r, 2, 0, jnp.concatenate([value[0:96], gwout[192:224, :]], 0))
    store_grads(r, 3, 0, jnp.concatenate([value[96:], gwout[288:, :]], 0))


def weights_late(r):
    keys = nn(r.dtr[2 * WIDTH :, :], r.n1[...])
    store_grads(r, 1, 1, jnp.concatenate([r.gwout[128:192, :], keys[0:192]], 0))
    store_grads(r, 2, 1, jnp.concatenate([r.gwout[224:288, :], keys[192:]], 0))


def project_back_start(r):
    ones = jnp.ones((8, ROWS), LOW)
    r.mid[0, 0:1, 0:WIDTH] = nt(ones, r.dtr[0:WIDTH, :])[0:1]
    r.mid[0, 1:2, 0:WIDTH] = nt(ones, r.dtr[WIDTH : 2 * WIDTH, :])[0:1]
    r.dvt[...] = nn(r.wfull[:, 0 : 2 * WIDTH], r.dtr[0 : 2 * WIDTH, :])


def project_back(r):
    r.sums[...] = jnp.zeros((8, WIDTH), WIDE)

    def step(i, c):
        rows = rows_at(i, DENSE)
        back = (r.dvt[:, rows] + nn(r.wfull[:, 2 * WIDTH :], r.dtr[2 * WIDTH :, rows])).T
        unit, inverse = unit_of(r, 0, rows, r.patches[rows, :].astype(WIDE))
        r.sums[0:1, :] += total(back * unit)
        r.sums[1:2, :] += total(back)
        r.middle[rows, :] = r.middle[rows, :] + normalize_back(
            back, r.vec[0:1, :], unit, inverse
        )
        return c

    lax.fori_loop(0, ROWS // DENSE, step, 0)
    for k in range(2):
        for n in range(3):
            r.late[0, 3 * k + n : 3 * k + n + 1, :] = r.sums[k : k + 1, 128 * n : 128 * n + 128]


MESH = pl.DeviceIdType.MESH
CHUNKS = ("a", "e", "r", "ac", "ec", "rc")
SHAPE = (PARTS, DEPS, 2, SHARD, WIDTH)
JOINED = (DEPS, 2, SHARD, PARTS * WIDTH)


class Place:
    def __init__(self, inner):
        self.inner = inner
        dp, tensor = lax.axis_index("dp"), lax.axis_index("tensor")
        self.rest = (lax.rem(dp, inner[0]), lax.rem(tensor, inner[1]))
        dp, tensor = dp // inner[0], tensor // inner[1]
        self.z, self.y = dp // 2, lax.rem(dp, 2)
        self.x, self.core = tensor // 2, lax.rem(tensor, 2)
        self.a = self.x + self.core * (self.y - self.x)
        self.b = self.y + self.core * (self.x - self.y)

    def xy(self, a, b):
        return a + self.core * (b - a), b + self.core * (a - b)

    def device(self, z, y, x, core):
        return (
            (z * 2 + y) * self.inner[0] + self.rest[0],
            (x * 2 + core) * self.inner[1] + self.rest[1],
        )

    def around(self, d):
        return lax.rem(self.z + d, DEPS)

    def z_peer(self, d):
        return self.device(self.around(d), self.y, self.x, self.core)

    def a_peer(self):
        x, y = self.xy(1 - self.a, self.b)
        return self.device(self.z, y, x, self.core)

    def b_peer(self):
        x, y = self.xy(self.a, 1 - self.b)
        return self.device(self.z, y, x, self.core)

    def x_peer(self):
        return self.device(self.z, self.y, 1 - self.x, self.core)

    def y_peer(self):
        return self.device(self.z, 1 - self.y, self.x, self.core)

    def plane_peer(self, a, b):
        x, y = self.xy(self.a + a * (1 - 2 * self.a), self.b + b * (1 - 2 * self.b))
        return self.device(self.z, y, x, self.core)

    def near(self, k):
        x = 1 - self.x if k & 4 else self.x
        y = 1 - self.y if k & 2 else self.y
        return self.device(self.z, y, x, 1 - self.core if k & 1 else self.core)

    def core_peer(self):
        return self.device(self.z, self.y, self.x, 1 - self.core)


def remote(src, dst, sems, k, device):
    return pltpu.make_async_remote_copy(
        src_ref=src,
        dst_ref=dst,
        send_sem=sems[0].at[k],
        recv_sem=sems[1].at[k],
        device_id=device,
        device_id_type=MESH,
    )


def part_of(w, j, z=slice(None), y=slice(None)):
    if len(w.shape) == 5:
        return w.at[j, z, y]
    return w.at[z, y, :, pl.ds(pl.multiple_of(j * WIDTH, 128), WIDTH)]


class Gather:
    def __init__(self, place, w, sems, base):
        self.p, self.w, self.sems, self.base = place, w, sems, base

    def copy(self, k, where, device):
        ref = part_of(self.w, *where)
        return remote(ref, ref, self.sems, self.base + k, device)

    def z_copies(self, back):
        p = self.p
        out = []
        for d in (1, 2, 3):
            z = p.around(DEPS - d) if back else p.z
            out.append(self.copy(d - 1, (p.x * 2 + p.core, z, p.y), p.z_peer(d)))
        return out

    def b_copies(self, back):
        p = self.p
        x, y = p.xy(p.a, 1 - p.b) if back else (p.x, p.y)
        return [self.copy(3, (x * 2 + p.core, slice(None), y), p.b_peer())]

    def a_copies(self, back):
        p = self.p
        a = 1 - p.a if back else p.a
        out = []
        for k, b in enumerate((p.b, 1 - p.b)):
            x, y = p.xy(a, b)
            out.append(self.copy(4 + k, (x * 2 + p.core, slice(None), y), p.a_peer()))
        return out

    def core_copies(self, back):
        p = self.p
        core = 1 - p.core if back else p.core
        return [self.copy(6 + x, (x * 2 + core,), p.core_peer()) for x in (0, 1)]

    def start(self, name):
        for copy in getattr(self, name + "_copies")(False):
            copy.start()

    def wait(self, name):
        for copy in getattr(self, name + "_copies")(True):
            copy.wait_recv()

    def drain(self):
        for name in ("z", "b", "a", "core"):
            for copy in getattr(self, name + "_copies")(False):
                copy.wait_send()


class QuickGather(Gather):
    def piece(self, a, b, back):
        p = self.p
        if back:
            a, b = p.a + a * (1 - 2 * p.a), p.b + b * (1 - 2 * p.b)
        else:
            a, b = p.a, p.b
        return p.xy(a, b)

    def plane_copy(self, q, d, back):
        p = self.p
        a, b = ((0, 1), (1, 0), (1, 1))[q]
        x, y = self.piece(a, b, back)
        where = (x * 2 + p.core, p.around(DEPS - d), y)
        return self.copy(3 + 4 * q + d, where, p.plane_peer(a, b))

    def core_copy(self, q, back):
        p = self.p
        a, b = ((0, 0), (0, 1), (1, 0), (1, 1))[q]
        x, y = self.piece(a, b, True)
        core = 1 - p.core if back else p.core
        return self.copy(15 + q, (x * 2 + core, slice(None), y), p.core_peer())

    def begin(self):
        for copy in self.z_copies(False):
            copy.start()
        for q in range(3):
            self.plane_copy(q, 0, False).start()

    def forward(self):
        for d, copy in zip((1, 2, 3), self.z_copies(True), strict=True):
            copy.wait_recv()
            for q in range(3):
                self.plane_copy(q, d, False).start()
        self.core_copy(0, False).start()

    def across(self):
        for q in range(3):
            for d in range(4):
                self.plane_copy(q, d, True).wait_recv()
            self.core_copy(1 + q, False).start()

    def end(self):
        for q in range(4):
            self.core_copy(q, True).wait_recv()

    def drain(self):
        for copy in self.z_copies(False):
            copy.wait_send()
        for q in range(3):
            for d in range(4):
                self.plane_copy(q, d, False).wait_send()
        for q in range(4):
            self.core_copy(q, False).wait_send()


class Scatter:
    def __init__(self, place, g, ins, sems, base):
        self.p, self.g, self.sems, self.base = place, g, sems, base
        self.c_in, self.a_in, self.b_in, self.z_in = ins

    def copies(self, name):
        p = self.p
        if name == "core":
            return [
                remote(part_of(self.g, x * 2 + 1 - p.core), self.c_in.at[x], self.sems, self.base + x, p.core_peer())
                for x in (0, 1)
            ]
        if name == "a":
            out = []
            for b in (0, 1):
                x, y = p.xy(1 - p.a, b)
                out.append(
                    remote(self.c_in.at[x, :, y], self.a_in.at[b], self.sems, self.base + 2 + b, p.a_peer())
                )
            return out
        if name == "b":
            return [remote(self.a_in.at[1 - p.b], self.b_in, self.sems, self.base + 4, p.b_peer())]
        return [
            remote(self.b_in.at[p.around(d)], self.z_in.at[d - 1], self.sems, self.base + 4 + d, p.z_peer(d))
            for d in (1, 2, 3)
        ]

    def start(self, name):
        for copy in self.copies(name):
            copy.start()

    def finish(self, name):
        p = self.p
        for copy in self.copies(name):
            copy.wait_recv()
        if name == "core":
            for x in (0, 1):
                self.c_in[x] += part_of(self.g, x * 2 + p.core)[...]
        elif name == "a":
            for b in (0, 1):
                x, y = p.xy(p.a, b)
                self.a_in[b] += self.c_in[x, :, y]
        elif name == "b":
            self.b_in[...] += self.a_in[p.b]

    def result(self):
        out = self.b_in[self.p.z].astype(WIDE)
        for d in range(3):
            out = out + self.z_in[d].astype(WIDE)
        return out

    def drain(self):
        for name in ("core", "a", "b", "z"):
            for copy in self.copies(name):
                copy.wait_send()


class QuickScatter(Scatter):
    def __init__(self, place, g, ins, sems, base, lane):
        super().__init__(place, g, ins, sems, base)
        self.lanes = pl.ds(lane, 128)

    def copies(self, name):
        p, base, lanes = self.p, self.base, self.lanes
        every = slice(None)
        out = []
        if name == "core":
            for x in (0, 1):
                src = self.g.at[x * 2 + 1 - p.core, :, :, :, lanes]
                dst = self.c_in.at[x, :, :, :, lanes]
                out.append(remote(src, dst, self.sems, base + x, p.core_peer()))
        elif name == "a":
            for q, (a, b) in enumerate(((0, 1), (1, 0), (1, 1))):
                x, y = p.xy(p.a + a * (1 - 2 * p.a), p.b + b * (1 - 2 * p.b))
                src = self.c_in.at[x, :, y, :, lanes]
                dst = self.a_in.at[q, :, :, lanes]
                out.append(remote(src, dst, self.sems, base + 2 + q, p.plane_peer(a, b)))
        elif name == "z":
            for d in (1, 2, 3):
                src = self.b_in.at[p.around(d), :, lanes]
                dst = self.z_in.at[d - 1, :, lanes]
                out.append(remote(src, dst, self.sems, base + 4 + d, p.z_peer(d)))
        return out

    def finish(self, name):
        p, lanes = self.p, self.lanes
        for copy in self.copies(name):
            copy.wait_recv()
        if name == "core":
            for x in (0, 1):
                self.c_in[x, :, :, :, lanes] += self.g[x * 2 + p.core, :, :, :, lanes]
        elif name == "a":
            mine = self.c_in[p.x, :, p.y, :, lanes].astype(WIDE)
            for q in range(3):
                mine = mine + self.a_in[q, :, :, lanes].astype(WIDE)
            self.b_in[:, :, lanes] = mine.astype(LOW)

    def result(self):
        out = self.b_in[self.p.z, :, self.lanes].astype(WIDE)
        for d in range(3):
            out = out + self.z_in[d, :, self.lanes].astype(WIDE)
        return out


class PartScatter(QuickScatter):
    def __init__(self, place, g, ins, sems, base, owner):
        super().__init__(place, g, ins, sems, base, 128)
        self.lanes = pl.ds(128, 256)
        self.owner = owner

    def core_copy(self, back):
        p = self.p
        x = self.owner if back else 1 - self.owner
        src = self.g.at[x * 2 + 1 - p.core, :, :, :, self.lanes]
        return remote(src, self.c_in.at[x, :, :, :, self.lanes], self.sems, self.base, p.core_peer())

    def plane_copy(self, k):
        p = self.p
        y = 1 - p.y if k & 1 else p.y
        src = self.c_in.at[self.owner, :, y, :, self.lanes]
        dst = self.a_in.at[k - 1, :, :, self.lanes]
        peer = (None, p.y_peer, p.x_peer, lambda: p.plane_peer(1, 1))[k]()
        return remote(src, dst, self.sems, self.base + k, peer)

    def owned(self, todo):
        pl.when(self.p.x == self.owner)(todo)

    def others(self, todo):
        pl.when(self.p.x != self.owner)(todo)

    def start(self, name):
        if name == "core":
            self.core_copy(False).start()
        elif name == "a":
            self.owned(lambda: self.plane_copy(1).start())

            def both():
                self.plane_copy(2).start()
                self.plane_copy(3).start()

            self.others(both)
        else:
            self.owned(lambda: QuickScatter.start(self, name))

    def finish(self, name):
        p, lanes = self.p, self.lanes
        if name == "core":
            self.core_copy(True).wait_recv()
            self.c_in[self.owner, :, :, :, lanes] += self.g[self.owner * 2 + p.core, :, :, :, lanes]
            return

        def todo():
            if name == "z":
                QuickScatter.finish(self, name)
                return
            for k in (1, 2, 3):
                self.plane_copy(k).wait_recv()
            mine = self.c_in[self.owner, :, p.y, :, lanes].astype(WIDE)
            for q in range(3):
                mine = mine + self.a_in[q, :, :, lanes].astype(WIDE)
            self.b_in[:, :, lanes] = mine.astype(LOW)

        self.owned(todo)

    def drain(self):
        self.core_copy(False).wait_send()

        def owned():
            self.plane_copy(1).wait_send()
            for copy in self.copies("z"):
                copy.wait_send()

        def others():
            self.plane_copy(2).wait_send()
            self.plane_copy(3).wait_send()

        self.owned(owned)
        self.others(others)


class SlowTotal:
    def __init__(self, place, own, got, sems, base):
        self.p, self.own, self.got, self.sems, self.base = place, own, got, sems, base

    def copies(self, k):
        p = self.p
        if k < 3:
            device = (p.core_peer, p.x_peer, p.y_peer)[k]()
            return [remote(self.own.at[k], self.got.at[k], self.sems, self.base + k, device)]
        return [
            remote(self.own.at[3], self.got.at[3 + d], self.sems, self.base + 2 + d, p.z_peer(d))
            for d in (1, 2, 3)
        ]

    def start(self, k):
        for copy in self.copies(k):
            copy.start()

    def finish(self, k):
        p = self.p
        for copy in self.copies(k):
            copy.wait_recv()
        if k < 3:
            self.own[k + 1] = self.own[k] + self.got[k]
            return None
        self.got[3] = self.own[3]
        out = None
        for z in range(DEPS):
            part = self.got[3 + lax.rem(p.z - z + DEPS, DEPS)]
            out = part if z == 0 else out + part
        return out

    def drain(self):
        for k in range(4):
            for copy in self.copies(k):
                copy.wait_send()


class Total:
    def __init__(self, place, own, got, sems, base):
        self.p, self.own, self.got, self.sems, self.base = place, own, got, sems, base

    def copies(self, k):
        p = self.p
        if k == 0:
            return [
                remote(self.own.at[0], self.got.at[n], self.sems, self.base + n, p.near(n))
                for n in range(1, 8)
            ]
        return [
            remote(self.own.at[1], self.got.at[8 + d], self.sems, self.base + 7 + d, p.z_peer(d))
            for d in (1, 2, 3)
        ]

    def start(self, k):
        for copy in self.copies(k):
            copy.start()

    def finish(self, k):
        p = self.p
        for copy in self.copies(k):
            copy.wait_recv()
        self.got[8 * k] = self.own[k]
        out = None
        if k == 0:
            for n in range(8):
                x = 1 - p.x if n & 4 else p.x
                y = 1 - p.y if n & 2 else p.y
                core = 1 - p.core if n & 1 else p.core
                part = self.got[x * 4 + y * 2 + core]
                out = part if n == 0 else out + part
            self.own[1] = out
            return None
        for z in range(DEPS):
            part = self.got[8 + lax.rem(p.z - z + DEPS, DEPS)]
            out = part if z == 0 else out + part
        return out

    def drain(self):
        for k in range(2):
            for copy in self.copies(k):
                copy.wait_send()


INPUTS = ("size", "images", "patches_in", "cot_in", "classes", "class_cot")
INPUTS += ("entry", "exit", "expand", "reduce", "entry_c", "exit_c", "expand_c", "reduce_c")
INPUTS += ("vec", "talking", "off", "vec_c", "off_c")
OUTPUTS = dict(
    patch_result=((ROWS, WIDTH), LOW),
    patch_grad=((ROWS, WIDTH), WIDE),
    class_result=((3, WIDTH), LOW),
    class_grad=((3, WIDTH), WIDE),
    blocks=((6, SHARD, WIDTH), WIDE),
    rows_early=((24, WIDTH), WIDE),
    rows_mid=((8, 512), WIDE),
    rows_late=((8, 128), WIDE),
)
COMM = {n: (SHAPE, LOW) for n in ("wa", "wa_c")}
COMM |= {n: (JOINED, LOW) for n in ("we", "wr", "we_c", "wr_c")}
COMM |= dict(
    wf=((PARTS, DEPS, 2, 16, WIDTH), LOW),
    turned=((2, DEPS, 2, SHARD, 256), LOW),
    early=((4, 24, WIDTH), WIDE),
    early_in=((7, 24, WIDTH), WIDE),
    mid=((2, 8, 512), WIDE),
    mid_in=((12, 8, 512), WIDE),
    late=((2, 8, 128), WIDE),
    late_in=((12, 8, 128), WIDE),
)
for _k in ("a", "e", "r", "ac"):
    COMM["c_in_" + _k] = ((2, DEPS, 2, SHARD, WIDTH), LOW)
    COMM["a_in_" + _k] = ((3 if _k == "a" else 2, DEPS, SHARD, WIDTH), LOW)
    COMM["b_in_" + _k] = ((DEPS, SHARD, WIDTH), LOW)
    COMM["z_in_" + _k] = ((3, SHARD, WIDTH), LOW)
SEMS = dict(g_send=67, g_recv=67, s_send=64, s_recv=64, t_send=28, t_recv=28, out=2, into=2)


def greet(p):
    barrier = pltpu.get_barrier_semaphore()
    peers = [p.z_peer(d) for d in (1, 2, 3)] + [p.near(n) for n in range(1, 8)]
    for peer in peers:
        pl.semaphore_signal(barrier, inc=1, device_id=peer, device_id_type=MESH)
    return lambda: pl.semaphore_wait(barrier, len(peers))


def layer_kernel(inner, *refs):
    r = Refs(**dict(zip([*INPUTS, *OUTPUTS, *SCRATCH, *COMM, *SEMS], refs, strict=True)))
    p = Place(inner)
    mine = p.x * 2 + p.core
    weights = dict(a=r.wa, e=r.we, r=r.wr, ac=r.wa_c, ec=r.we_c, rc=r.wr_c)
    grads = weights
    first = QuickGather(p, r.wa, (r.g_send, r.g_recv), 40)
    gathers, scatters = {}, {}
    for i, k in enumerate(CHUNKS):
        if k != "a":
            gathers[k] = Gather(p, weights[k], (r.g_send, r.g_recv), 8 * (i - 1))
        if k in ("ec", "rc"):
            continue
        ins = [getattr(r, n + "_in_" + k) for n in ("c", "a", "b", "z")]
        if k == "a":
            sems = (r.s_send, r.s_recv)
            last = [
                QuickScatter(p, r.wa, ins, sems, 40, 0),
                PartScatter(p, r.wa, ins, sems, 48, p.core),
                PartScatter(p, r.wa, ins, sems, 56, 1 - p.core),
            ]
        else:
            scatters[k] = Scatter(p, grads[k], ins, (r.s_send, r.s_recv), 8 * (i - 1))
    gathers["cf"] = Gather(p, r.wf, (r.g_send, r.g_recv), 59)
    early = SlowTotal(p, r.early, r.early_in, (r.t_send, r.t_recv), 0)
    mid = Total(p, r.mid, r.mid_in, (r.t_send, r.t_recv), 6)
    late = Total(p, r.late, r.late_in, (r.t_send, r.t_recv), 17)

    def go(*moves):
        def todo():
            for k, old, new in moves:
                if old:
                    gathers[k].wait(old)
                if new:
                    gathers[k].start(new)

        return todo

    def back(*moves):
        def todo():
            for k, old, new in moves:
                if k == "cf":
                    go((k, old, new))()
                    continue
                what = scatters.get(k) or early
                if old is not None:
                    what.finish(old)
                if new is not None:
                    what.start(new)

        return todo

    enter = greet(p)
    r.wa[mine, p.z, p.y] = jnp.concatenate([r.entry[...], r.exit[...]], 1)
    load = [
        pltpu.make_async_copy(r.patches_in, r.patches, r.into.at[0]),
        pltpu.make_async_copy(r.cot_in, r.cot, r.into.at[1]),
    ]
    load[0].start()
    load[1].start()
    enter()
    first.begin()
    part_of(r.we, mine, p.z, p.y)[...] = r.expand[...]
    part_of(r.wr, mine, p.z, p.y)[...] = r.reduce[...]
    r.wa_c[mine, p.z, p.y] = jnp.concatenate([r.entry_c[...], r.exit_c[...]], 1)
    part_of(r.we_c, mine, p.z, p.y)[...] = r.expand_c[...]
    part_of(r.wr_c, mine, p.z, p.y)[...] = r.reduce_c[...]
    columns(r)
    first.forward()
    go(("e", None, "z"), ("r", None, "z"))()
    masks(r)
    load[0].wait()
    norm_first(r)
    r.early[0] = jnp.zeros((24, WIDTH), WIDE)
    r.mid[0] = jnp.zeros((8, 512), WIDE)
    r.late[0] = jnp.zeros((8, 128), WIDE)
    first.across()
    first.end()
    go(("e", "z", "b"), ("ac", None, "z"), ("ec", None, "z"), ("rc", None, "z"), ("r", "z", "b"))()
    project(r)
    attend(r, gather_points(go))
    gathers["e"].wait("core")
    gathers["r"].wait("core")
    feed(r, feed_points(go))
    out_result = pltpu.make_async_copy(r.result, r.patch_result, r.out.at[0])
    out_result.start()
    def begin_class():
        gathers["ac"].wait("core")
        load[1].wait()

    def begin_scores():
        gathers["rc"].wait("a")
        gathers["rc"].start("core")

    def begin_feed():
        gathers["ec"].wait("core")

    def begin_reduce():
        gathers["rc"].wait("core")
        for k in ("a", *CHUNKS[1:]):
            (first if k == "a" else gathers[k]).drain()

    def share(rows):
        r.wf[mine, p.z, p.y] = rows
        gathers["cf"].start("z")

    classes(r, (begin_class, begin_feed, share, begin_scores, begin_reduce))
    scatters["ac"].start("core")
    ready = {n: functools.partial(scatters[n[0]].start, "core") for n in ("expand", "reduce")}
    feed_back(r, feed_back_points(back) | ready)
    attend_back(r, attend_back_points(back))
    weights_early(r)
    last[0].start("core")
    last[1].start("core")
    talking_back(r)
    project_back_start(r)
    mid.start(0)
    keys_back(r, keys_points(last, mid, back))
    weights_late(r)
    last[2].start("core")
    project_back(r)
    last[2].finish("core")
    last[2].start("a")
    late.start(0)
    out_grad = pltpu.make_async_copy(r.middle, r.patch_grad, r.out.at[1])
    out_grad.start()
    for n in (0, 1):
        last[n].finish("a")
        last[n].start("z")
    gathers["cf"].wait("core")
    class_weights(r, p)
    for i, k in ((1, "e"), (2, "r"), (3, "ac")):
        scatters[k].finish("z")
        r.blocks[i] = scatters[k].result()
    r.rows_early[...] = early.finish(3)
    late.finish(0)
    late.start(1)
    r.rows_mid[...] = mid.finish(1)
    last[2].finish("a")
    last[2].start("z")
    r.rows_late[...] = late.finish(1)
    for n in range(3):
        last[n].finish("z")
    r.blocks[0, :, 0:128] = last[0].result()
    r.blocks[0, :, 128:] = last[1].result()
    out_result.wait()
    out_grad.wait()
    for k in ("e", "r", "ac"):
        scatters[k].drain()
    gathers["cf"].drain()
    for k in last:
        k.drain()
    early.drain()
    mid.drain()
    late.drain()


def gather_points(go):
    return {
        0: go(("e", "b", "a")),
        2: go(("ac", "z", "b")),
        3: go(("r", "b", "a")),
        5: go(("e", "a", "core"), ("ec", "z", "b")),
        6: go(("ac", "b", "a")),
        8: go(("r", "a", "core"), ("rc", "z", "b")),
        9: go(("ec", "b", "a")),
        11: go(("ac", "a", "core")),
    }


def feed_points(go):
    return {0: go(("rc", "b", "a")), 2: go(("ec", "a", "core"))}


def keys_points(last, mid, back):
    def core(n):
        def todo():
            last[n].finish("core")
            last[n].start("a")

        return todo

    def middle():
        mid.finish(0)
        mid.start(1)

    return {0: core(0), 1: core(1), 4: middle}


def feed_back_points(back):
    return {
        0: back(("cf", "z", "b")),
        2: back(("cf", "b", "a"), ("ac", "core", "a")),
    }


def attend_back_points(back):
    return {
        0: back(("cf", "a", "core")),
        2: back(("ac", "a", "b"), ("e", "core", "a")),
        4: back(("r", "core", "a"), ("ac", "b", "z"), ("early", None, 0)),
        6: back(("e", "a", "b"), ("early", 0, 1)),
        8: back(("r", "a", "b"), ("e", "b", "z"), ("early", 1, 2)),
        10: back(("r", "b", "z"), ("early", 2, 3)),
    }


def finish_kernel(inner, *refs):
    r = Refs(**dict(zip([*(n + "_in" for n in OUTPUTS), *FINAL], refs, strict=True)))
    r.patch_result[...] = r.patch_result_in[...]
    r.patch_grad[...] = r.patch_grad_in[...]
    r.class_result[...] = r.class_result_in[...]
    r.class_grad[...] = r.class_grad_in[...]
    r.g_entry_c[...] = r.blocks_in[3, :, 0:COLS]
    r.g_exit_c[...] = r.blocks_in[3, :, COLS:]
    part = lax.axis_index("tensor") // inner[1]
    block = r.blocks_in[0]
    one, two, three = block[:, 0:96], block[:, 96:192], block[:, 192:]
    outer = (part == 0) | (part == 3)
    inside = jnp.where(
        part == 1, jnp.concatenate([one, three], 1), jnp.concatenate([three, one], 1)
    )
    r.g_entry[...] = jnp.where(outer, block[:, 0:COLS], inside)
    r.g_exit[...] = jnp.where(outer, block[:, COLS:], two)
    for i, c in ((0, ""), (3, "_c")):
        getattr(r, "g_expand" + c)[...] = r.blocks_in[i + 1]
        getattr(r, "g_reduce" + c)[...] = r.blocks_in[i + 2]
    for k in range(2):
        for n in range(3):
            r.g_vec[k : k + 1, 128 * n : 128 * n + 128] = r.rows_late_in[3 * k + n : 3 * k + n + 1, :]
    r.g_vec[2:4, :] = r.rows_mid_in[0:2, 0:WIDTH]
    r.g_vec[4:10, :] = r.rows_early_in[0:6, :]
    r.g_vec_c[...] = r.rows_early_in[10:20, :]
    for j in range(PARTS):
        part = slice(WIDTH * j, WIDTH * (j + 1))
        r.g_off[part] = r.rows_early_in[6 + j : 7 + j, :].reshape(WIDTH)
        r.g_off_c[part] = r.rows_early_in[20 + j : 21 + j, :].reshape(WIDTH)
    talk = r.rows_mid_in[:, WIDTH:]
    turned = jnp.concatenate([talk, jnp.zeros((120, 128), WIDE)], 0).T
    lane = iota((8, 128), 1)
    moved = pltpu.roll(turned[8:16], 8, 1)
    r.g_talking[...] = jnp.where((lane >= 8) & (lane < 16), moved, talk)[:, 0:17]


FINAL = dict(
    patch_result=((ROWS, WIDTH), LOW),
    class_result=((3, WIDTH), LOW),
    patch_grad=((ROWS, WIDTH), WIDE),
    class_grad=((3, WIDTH), WIDE),
    g_entry=((SHARD, COLS), WIDE),
    g_exit=((SHARD, 96), WIDE),
    g_expand=((SHARD, WIDTH), WIDE),
    g_reduce=((SHARD, WIDTH), WIDE),
    g_vec=((10, WIDTH), WIDE),
    g_talking=((8, 17), WIDE),
    g_off=((FF,), WIDE),
    g_entry_c=((SHARD, COLS), WIDE),
    g_exit_c=((SHARD, 96), WIDE),
    g_expand_c=((SHARD, WIDTH), WIDE),
    g_reduce_c=((SHARD, WIDTH), WIDE),
    g_vec_c=((10, WIDTH), WIDE),
    g_off_c=((FF,), WIDE),
)


def layers(inner, *args):
    smem = pl.BlockSpec(memory_space=pltpu.SMEM)
    vmem = pl.BlockSpec(memory_space=pltpu.VMEM)
    hbm = pl.BlockSpec(memory_space=pl.ANY)
    sems = [pltpu.SemaphoreType.DMA((n,)) for n in SEMS.values()]
    mid = pl.pallas_call(
        functools.partial(layer_kernel, inner),
        out_shape=[jax.ShapeDtypeStruct(*s) for s in OUTPUTS.values()],
        in_specs=[smem, smem, hbm, hbm] + [vmem] * (len(INPUTS) - 4),
        out_specs=[hbm, hbm] + [vmem] * (len(OUTPUTS) - 2),
        scratch_shapes=[pltpu.VMEM(*s) for s in (SCRATCH | COMM).values()] + sems,
        compiler_params=pltpu.CompilerParams(
            vmem_limit_bytes=63 * 2**20, collective_id=0, has_side_effects=True
        ),
    )(*args)
    out = pl.pallas_call(
        functools.partial(finish_kernel, inner),
        out_shape=[jax.ShapeDtypeStruct(*s) for s in FINAL.values()],
        in_specs=[vmem] * len(OUTPUTS),
        out_specs=[vmem] * len(FINAL),
    )(*mid)
    return dict(zip(FINAL, out, strict=True))


def groups(axis, inner):
    return [[inner * k + i for i in range(inner)] for k in range(lax.axis_size(axis) // inner)]


def widen(x, inner, dims):
    for axis, n, dim in zip(("dp", "tensor"), inner, dims, strict=True):
        if n > 1:
            x = lax.all_gather(x, axis, axis=dim, tiled=True, axis_index_groups=groups(axis, n))
    return x


def narrow(x, inner, dims):
    for axis, n, dim in zip(("dp", "tensor"), inner, dims, strict=True):
        if n > 1:
            x = lax.psum_scatter(
                x, axis, scatter_dimension=dim, tiled=True, axis_index_groups=groups(axis, n)
            )
    return x


def whole(x, inner):
    for axis, n in zip(("dp", "tensor"), inner, strict=True):
        if n > 1:
            x = lax.psum(x, axis, axis_index_groups=groups(axis, n))
    return x


KINDS = ((0, 1),) * 4


def local(
    patches,
    classes,
    group_size,
    image_count,
    self_entry,
    self_exit,
    self_expand,
    self_reduce,
    self_vectors,
    self_talking,
    self_offset,
    class_entry,
    class_exit,
    class_expand,
    class_reduce,
    class_vectors,
    class_offset,
    patch_cotangent,
    class_cotangent,
):
    inner = (lax.axis_size("dp") // 8, lax.axis_size("tensor") // 4)
    weights = [
        widen(w, inner, dims)
        for w, dims in zip(
            (
                self_entry,
                self_exit,
                self_expand,
                self_reduce.T,
                class_entry,
                class_exit,
                class_expand,
                class_reduce.T,
            ),
            KINDS * 2,
            strict=True,
        )
    ]
    out = layers(
        inner,
        group_size,
        image_count,
        patches,
        patch_cotangent,
        classes,
        class_cotangent,
        *weights,
        self_vectors,
        self_talking.T,
        self_offset,
        class_vectors,
        class_offset,
    )
    names = ("entry", "exit", "expand", "reduce")
    own = [narrow(out["g_" + n], inner, dims) for n, dims in zip(names, KINDS, strict=True)]
    own_c = [narrow(out["g_" + n + "_c"], inner, dims) for n, dims in zip(names, KINDS, strict=True)]
    return (
        out["patch_result"],
        out["class_result"],
        out["patch_grad"],
        out["class_grad"],
        *own[:3],
        own[3].T,
        whole(out["g_vec"], inner),
        whole(out["g_talking"], inner).T,
        whole(out["g_off"], inner),
        *own_c[:3],
        own_c[3].T,
        whole(out["g_vec_c"], inner),
        whole(out["g_off_c"], inner),
    )


def solution(mesh):
    both = P(("dp", "tensor"), None)
    weights = (P("dp", "tensor"), P("dp", "tensor"), P("dp", "tensor"), P("tensor", "dp"))
    return jax.shard_map(
        local,
        mesh=mesh,
        in_specs=(
            both,
            both,
            P(("dp", "tensor")),
            P(("dp", "tensor")),
            *weights,
            P(),
            P(),
            P(),
            *weights,
            P(),
            P(),
            both,
            both,
        ),
        out_specs=(both, both, both, both, *weights, P(), P(), P(), *weights, P(), P()),
        check_vma=False,
    )
```

```python
import functools

import jax
import jax.numpy as jnp
from jax import lax
from jax.experimental import pallas as pl
from jax.experimental.pallas import tpu as pltpu
from jax.sharding import PartitionSpec as P

HEADS = 8
EPSILON = 1e-06
NEGATIVE = -1e30
ROOT_HALF = 0.7071067811865476
ROOT_TWO_PI = 2.5066282746310002
WIDE = jnp.float32
LOW = jnp.bfloat16

WIDTH = 384
DEPTH = WIDTH // HEADS
ROWS = 768
FF = 1536
PARTS = 4
COLS = 3 * WIDTH // PARTS
TILE = 128
SPAN = HEADS * TILE
HALVES = (slice(0, SPAN // 2), slice(SPAN // 2, SPAN))
WIDE_HALVES = (slice(0, FF // 2), slice(FF // 2, FF))
SHARD = 48
DEPS = 4
STEPS = ROWS // TILE
TOGETHER = 2
KEYS = ROWS + 128
DENSE = 384
PAIRS = HEADS * 8


def nn(a, b):
    return lax.dot_general(a, b, (((1,), (0,)), ((), ())), preferred_element_type=WIDE)


def nt(a, b):
    return lax.dot_general(a, b, (((1,), (1,)), ((), ())), preferred_element_type=WIDE)


def iota(shape, dim):
    return lax.broadcasted_iota(jnp.int32, shape, dim)


def rows_at(i, size):
    if isinstance(i, int):
        return slice(i * size, (i + 1) * size)
    return pl.ds(pl.multiple_of(i * size, size), size)


def normalize(x, gain, shift):
    mean = jnp.mean(x, -1, keepdims=True)
    centered = x - mean
    inverse = lax.rsqrt(jnp.mean(centered * centered, -1, keepdims=True) + EPSILON)
    unit = centered * inverse
    return unit * gain + shift, unit, inverse


def keep_stats(r, k, rows, x, inverse):
    r.stats[rows, 2 * k : 2 * k + 1] = jnp.mean(x, -1, keepdims=True)
    r.stats[rows, 2 * k + 1 : 2 * k + 2] = inverse


def unit_of(r, k, rows, x):
    inverse = r.stats[rows, 2 * k + 1 : 2 * k + 2]
    return (x - r.stats[rows, 2 * k : 2 * k + 1]) * inverse, inverse


def normalize_back(grad, gain, unit, inverse):
    scaled = grad * gain
    inner = jnp.mean(scaled * unit, -1, keepdims=True)
    return inverse * (scaled - jnp.mean(scaled, -1, keepdims=True) - unit * inner)


def by_head(x):
    return jnp.sum(x.reshape(HEADS, DEPTH, x.shape[-1]), 1)


def total(x):
    return jnp.sum(x, 0, keepdims=True)


def smooth(hidden):
    cdf = 0.5 * (1.0 + lax.erf(hidden * ROOT_HALF))
    slope = cdf + hidden * jnp.exp(-0.5 * hidden * hidden) * (1.0 / ROOT_TWO_PI)
    return (hidden * cdf).astype(LOW), slope.astype(LOW)


def each(count, together, step, points):
    def some(i, c):
        for k in range(together):

            def at(where):
                for key, todo in points.items():
                    if isinstance(key, str):
                        continue
                    t, place = divmod(key, 2)
                    if place == where and t % together == k:
                        pl.when(i == t // together)(todo)

            step(i * together + k, at)
        return c

    lax.fori_loop(0, count // together, some, 0)


class Refs:
    def __init__(self, **refs):
        self.__dict__.update(refs)


SCRATCH = dict(
    cols=((WIDTH, 128), WIDE),
    pad=((128, 128), WIDE),
    patches=((ROWS, WIDTH), LOW),
    cot=((ROWS, WIDTH), LOW),
    result=((ROWS, WIDTH), LOW),
    n1=((ROWS, WIDTH), LOW),
    stats=((ROWS, 128), WIDE),
    went=((3 * WIDTH, WIDTH), LOW),
    wout=((WIDTH, WIDTH), LOW),
    wback=((WIDTH, WIDTH), LOW),
    wfull=((WIDTH, 3 * WIDTH), LOW),
    qt=((WIDTH, ROWS), LOW),
    kext=((ROWS, 512), LOW),
    kt=((WIDTH, ROWS), LOW),
    vext=((ROWS, 512), LOW),
    vt=((WIDTH, ROWS), LOW),
    hot=((ROWS, 128), LOW),
    hott=((8, ROWS), WIDE),
    vsum=((WIDTH, 128), WIDE),
    gsum=((WIDTH, 128), WIDE),
    qm=((512, SPAN), LOW),
    qn=((WIDTH, SPAN), LOW),
    et=((STEPS + 1, ROWS, SPAN), LOW),
    un=((STEPS, WIDTH, SPAN), LOW),
    linv=((STEPS, 1, SPAN), WIDE),
    attt=((WIDTH, ROWS), LOW),
    middle=((ROWS, WIDTH), WIDE),
    branch1=((ROWS, WIDTH), LOW),
    branch2=((ROWS, WIDTH), WIDE),
    n2t=((WIDTH, ROWS), LOW),
    act=((ROWS, FF), LOW),
    slope=((ROWS, FF), LOW),
    next=((KEYS, WIDTH), LOW),
    wout_c=((WIDTH, WIDTH), LOW),
    small8=((8, WIDTH), WIDE),
    cot8=((8, WIDTH), WIDE),
    both=((KEYS, 128), LOW),
    qkwv=((128, WIDTH), LOW),
    d1t=((WIDTH, ROWS), LOW),
    d2t=((WIDTH, ROWS), LOW),
    dot=((WIDTH, ROWS), LOW),
    gwout=((WIDTH, WIDTH), WIDE),
    sums=((8, WIDTH), WIDE),
    offset=((1, FF), WIDE),
    dvt=((WIDTH, ROWS), WIDE),
    dkt=((WIDTH, ROWS), WIDE),
    accp=((HEADS, HEADS, TILE), WIDE),
    accq=((HEADS, HEADS, TILE), WIDE),
    dtr=((3 * WIDTH, ROWS), LOW),
)


def block_of(w, j):
    return w[j].reshape(WIDTH, w.shape[-1])


def whole_of(w):
    return w[...].reshape(WIDTH, FF)


def as_block(x):
    return x.reshape(DEPS, 2, SHARD, x.shape[-1])


def unpack_weights(wa, went, wout):
    for j in range(PARTS):
        block = block_of(wa, j).T
        went[COLS * j : COLS * (j + 1), :] = block[:COLS]
        wout[96 * j : 96 * (j + 1), :] = block[COLS:]

def columns(r):
    r.pad[...] = jnp.zeros((128, 128), WIDE)
    r.pad[0:8, 0:17] = r.talking[...]
    turned = r.pad[...]
    talk = turned.T
    turned = turned[0:8]
    moved = pltpu.roll(talk, 8, 1)[8:16]
    lane = iota((8, 128), 1)
    alone = jnp.sum(talk[8:16], 1, keepdims=True) + turned[:, 16:17]
    base = jnp.where(lane < 8, turned * DEPTH ** (-0.5), moved)
    base = jnp.where(lane == 16, turned, base)
    base = jnp.where(lane == 19, alone, base)
    turned = r.vec[0:8, :].T
    lane = iota((DEPTH, 128), 1)
    for h in range(HEADS):
        rows = slice(DEPTH * h, DEPTH * (h + 1))
        x = jnp.broadcast_to(base[h : h + 1], (DEPTH, 128))
        x = jnp.where(lane == 17, turned[rows, 2:3], x)
        r.cols[rows, :] = jnp.where(lane == 18, turned[rows, 3:4], x)


def masks(r):
    size, images = r.size[0], r.images[0]
    place = iota((ROWS, 128), 0)
    which = iota((ROWS, 128), 1)
    inside = (place >= which * size) & (place < which * size + size) & (which < images)
    r.hot[...] = jnp.where(inside, 1.0, 0.0).astype(LOW)
    r.kext[:, WIDTH:] = jnp.where(inside | (which >= 3), 0.0, NEGATIVE).astype(LOW)
    r.vext[:, WIDTH:] = jnp.where(which < 2, 1.0, 0.0).astype(LOW)
    place = iota((8, ROWS), 1)
    which = iota((8, ROWS), 0)
    inside = (place >= which * size) & (place < which * size + size) & (which < images)
    r.hott[...] = jnp.where(inside, 1.0, 0.0)


def norm_first(r):
    gain, shift = r.vec[0:1, :], r.vec[1:2, :]

    def norm_step(i, c):
        rows = rows_at(i, DENSE)
        x = r.patches[rows, :].astype(WIDE)
        normed, unit, inverse = normalize(x, gain, shift)
        r.n1[rows, :] = normed.astype(LOW)
        keep_stats(r, 0, rows, x, inverse)
        return c

    lax.fori_loop(0, ROWS // DENSE, norm_step, 0)


def project(r):
    unpack_weights(r.wa, r.went, r.wout)

    def step(i, c):
        rows = rows_at(i, DENSE)
        normed = r.n1[rows, :]
        turned = nt(r.went[...], normed)
        r.qt[:, rows] = (turned[0:WIDTH] + r.cols[:, 17:18]).astype(LOW)
        r.kt[:, rows] = turned[WIDTH : 2 * WIDTH].astype(LOW)
        r.vt[:, rows] = (turned[2 * WIDTH :] + r.cols[:, 18:19]).astype(LOW)
        both = nt(normed, r.went[WIDTH:, :])
        r.kext[rows, 0:WIDTH] = both[:, 0:WIDTH].astype(LOW)
        r.vext[rows, 0:WIDTH] = (both[:, WIDTH:] + r.vec[3:4, :]).astype(LOW)
        return c

    lax.fori_loop(0, ROWS // DENSE, step, 0)
    r.vsum[...] = nn(r.vt[...], r.hot[...])
    r.wback[...] = r.wout[...].T
    r.wfull[:, 0:WIDTH] = r.went[0:WIDTH, :].T
    r.wfull[:, WIDTH : 2 * WIDTH] = r.went[2 * WIDTH :, :].T
    r.wfull[:, 2 * WIDTH :] = r.went[WIDTH : 2 * WIDTH, :].T


def attend(r, points):
    def step(t, at):
        at(0)
        rows = rows_at(t, TILE)
        q = r.qt[:, rows].astype(WIDE)
        hot = r.hott[:, rows]
        hot_rows = jnp.concatenate([hot, jnp.zeros((120, TILE), WIDE)], 0).astype(LOW)
        for g in range(HEADS):
            r.qm[0:WIDTH, TILE * g : TILE * (g + 1)] = (q * r.cols[:, g : g + 1]).astype(LOW)
            r.qm[WIDTH:, TILE * g : TILE * (g + 1)] = hot_rows
        own = r.vt[:, rows].astype(WIDE)
        att = r.cols[:, 16:17] * (
            r.vsum[:, 0:1] * hot[0:1] + r.vsum[:, 1:2] * hot[1:2] + r.vsum[:, 2:3] * hot[2:3]
        )
        for half in HALVES:
            scores = nn(r.kext[...], r.qm[:, half])
            raised = jnp.exp(scores - jnp.max(scores, 0, keepdims=True))
            r.linv[t, :, half] = 1.0 / jnp.sum(raised, 0, keepdims=True)
            r.et[t + 1, :, half] = raised.astype(LOW)
        at(1)
        for i, half in enumerate(HALVES):
            mean = nn(r.vt[...], r.et[t + 1, :, half]) * r.linv[t, :, half]
            r.un[t, :, half] = mean.astype(LOW)
            for k in range(HEADS // 2):
                h = HEADS // 2 * i + k
                att = att + r.cols[:, 8 + h : 9 + h] * mean[:, TILE * k : TILE * (k + 1)]
        live = (hot[0:1] + hot[1:2] + hot[2:3]) > 0.5
        att = jnp.where(live, att, r.cols[:, 19:20] * own).astype(LOW)
        r.attt[:, rows] = att
        branch = nt(att.T, r.wout[...]) + r.vec[4:5, :]
        r.branch1[rows, :] = branch.astype(LOW)
        r.middle[rows, :] = r.patches[rows, :].astype(WIDE) + r.vec[5:6, :] * branch

    each(STEPS, TOGETHER, step, points)


def feed(r, points):
    def step(i, at):
        at(0)
        rows = rows_at(i, DENSE)
        middle = r.middle[rows, :]
        normed, unit, inverse = normalize(middle, r.vec[6:7, :], r.vec[7:8, :])
        keep_stats(r, 1, rows, middle, inverse)
        normed = normed.astype(LOW)
        r.n2t[:, rows] = normed.T
        hidden = [nn(normed, whole_of(r.we)[:, half]) + r.off[half].reshape(1, FF // 2) for half in WIDE_HALVES]
        for half, part in zip(WIDE_HALVES, hidden, strict=True):
            active, slope = smooth(part)
            r.act[rows, half] = active
            r.slope[rows, half] = slope
        at(1)
        lifted = nt(whole_of(r.wr), r.act[rows, :]).T
        branch = lifted + r.vec[8:9, :]
        r.branch2[rows, :] = branch
        first = middle + r.vec[9:10, :] * branch
        r.result[rows, :] = first.astype(LOW)
        normed, unit, inverse = normalize(first, r.vec_c[0:1, :], r.vec_c[1:2, :])
        r.next[rows, :] = normed.astype(LOW)
        keep_stats(r, 2, rows, first, inverse)

    each(ROWS // DENSE, 1, step, points)


def classes(r, points):
    v = lambda k: r.vec_c[k : k + 1, :]
    scale = DEPTH ** (-0.5)
    points[0]()
    unpack_weights(r.wa_c, r.went, r.wout_c)
    wq, wk, wv = (r.went[WIDTH * k : WIDTH * (k + 1), :] for k in range(3))
    r.small8[...] = jnp.zeros((8, WIDTH), WIDE)
    r.cot8[...] = jnp.zeros((8, WIDTH), WIDE)
    r.small8[0:3, :] = r.classes[...].astype(WIDE)
    r.cot8[0:3, :] = r.class_cot[...].astype(WIDE)
    tokens = r.small8[...]
    normed, unit, inverse = normalize(tokens, v(0), v(1))
    low = normed.astype(LOW)
    valid = iota((128, WIDTH), 0) < 3
    r.next[ROWS:, :] = jnp.where(
        valid, jnp.concatenate([normed, jnp.zeros((120, WIDTH), WIDE)], 0), 0.0
    ).astype(LOW)
    head_of = iota((PAIRS, WIDTH), 1) // DEPTH
    own_head = head_of == iota((PAIRS, WIDTH), 0) // 8

    def spread(x):
        return jnp.where(own_head, jnp.concatenate([x] * HEADS, 0), 0.0)

    def gather_heads(x):
        x = jnp.where(own_head, x, 0.0)
        out = x[0:8]
        for h in range(1, HEADS):
            out = out + x[8 * h : 8 * (h + 1)]
        return out

    queries = (nt(low, wq) + v(2)).astype(LOW)
    qexp = spread(queries.astype(WIDE))
    qk = (nn(qexp.astype(LOW), wk) * scale).astype(LOW)
    keys = r.next[...]
    points[3]()
    scores = nt(qk, keys)
    size, images = r.size[0], r.images[0]
    slot = iota((PAIRS, KEYS), 0) & 7
    place = iota((PAIRS, KEYS), 1)
    allowed = (place >= slot * size) & (place < slot * size + size) & (slot < images)
    allowed = allowed | (place == slot + ROWS)
    scores = jnp.where(allowed, scores, NEGATIVE)
    raised = jnp.exp(scores - jnp.max(scores, -1, keepdims=True))
    probs = raised / jnp.sum(raised, -1, keepdims=True)
    probs_low = probs.astype(LOW)
    mass = jnp.sum(probs_low.astype(WIDE), -1, keepdims=True)
    z = nn(probs_low, keys).astype(LOW)
    attended = gather_heads(nt(z, wv) + mass * v(3)).astype(LOW)
    branch = nt(attended, r.wout_c[...]) + v(4)
    middle = tokens + v(5) * branch
    normed2, unit2, inverse2 = normalize(middle, v(6), v(7))
    low2 = normed2.astype(LOW)
    grad = r.cot8[...]
    delta2 = (v(9) * grad).astype(LOW)
    points[2](jnp.concatenate([low2.astype(WIDE), delta2.astype(WIDE)], 0).astype(LOW))
    points[1]()
    expand = whole_of(r.we_c)
    hidden = nn(low2, expand) + r.off_c[...].reshape(1, FF)
    active, slope = smooth(hidden)
    points[4]()
    reduce = whole_of(r.wr_c)
    lifted = nt(active, reduce)
    branch2 = lifted + v(8)
    second = middle + v(9) * branch2
    r.class_result[...] = second[0:3].astype(LOW)
    grad_scale2 = total(grad * branch2)
    grad_bias2 = total(delta2.astype(WIDE))
    grad_hidden = (nn(delta2, reduce) * slope.astype(WIDE)).astype(LOW)
    off = total(grad_hidden.astype(WIDE))
    for j in range(PARTS):
        r.early[0, 20 + j : 21 + j, :] = off[:, WIDTH * j : WIDTH * (j + 1)]
    back = nt(grad_hidden, expand)
    grad_gain2, grad_shift2 = total(back * unit2), total(back)
    grad = grad + normalize_back(back, v(6), unit2, inverse2)
    grad_scale = total(grad * branch)
    delta = (v(5) * grad).astype(LOW)
    grad_bias = total(delta.astype(WIDE))
    gatt = nn(delta, r.wout_c[...]).astype(LOW)
    dexp = spread(gatt.astype(WIDE))
    wide_v = nn(dexp.astype(LOW), wv).astype(LOW)
    gp = nt(wide_v, keys)
    ds = (probs * (gp - jnp.sum(gp * probs, -1, keepdims=True))).astype(LOW)
    y = nn(ds, keys).astype(LOW)
    gq = (gather_heads(nt(y, wk)) * scale).astype(LOW)
    both = jnp.concatenate([ds.astype(WIDE), probs_low.astype(WIDE)], 0).T.astype(LOW)
    r.both[...] = both
    r.qkwv[...] = jnp.concatenate([qk, wide_v], 0)
    grad_normed = nn(both[ROWS:, :], r.qkwv[...])[0:8] + nn(gq, wq)
    r.class_grad[...] = (grad + normalize_back(grad_normed, v(0), unit, inverse))[0:3]
    valid8 = iota((8, WIDTH), 0) < 3
    grad_normed = jnp.where(valid8, grad_normed, 0.0)
    gq_t = gq.astype(WIDE).T.astype(LOW)
    grad_q = nn(gq_t, low)
    grad_k = nn((qexp * scale).T.astype(LOW), y)
    grad_v = nn(dexp.T.astype(LOW), z)
    grad_out = nn(delta.astype(WIDE).T.astype(LOW), attended)
    whole = jnp.concatenate([grad_q, grad_k, grad_v], 0)
    for j in range(PARTS):
        block = jnp.concatenate(
            [whole[COLS * j : COLS * (j + 1)], grad_out[96 * j : 96 * (j + 1)]], 0
        )
        r.wa_c[j] = as_block(block.T.astype(LOW))
    grad_vb = total(jnp.where(own_head, mass * dexp, 0.0))
    r.early[0, 10:20, :] = jnp.concatenate(
        [
            total(grad_normed * unit),
            total(grad_normed),
            total(gq.astype(WIDE)),
            grad_vb,
            grad_bias,
            grad_scale,
            grad_gain2,
            grad_shift2,
            grad_bias2,
            grad_scale2,
        ],
        0,
    )


def class_weights(r, p):
    rows = r.wf[...].astype(WIDE).reshape(32, 16, WIDTH)
    normed, delta = (rows[:, k : k + 8].reshape(256, WIDTH) for k in (0, 8))
    for k, x in enumerate((normed, delta)):
        r.turned[k] = x.T.astype(LOW).reshape(DEPS, 2, SHARD, 256)
    part = p.x * 2 + p.core
    offset = r.off_c[0:WIDTH]
    for j in range(1, PARTS):
        offset = jnp.where(part == j, r.off_c[WIDTH * j : WIDTH * (j + 1)], offset)
    expand = part_of(r.we_c, part)[...].reshape(WIDTH, WIDTH)
    reduce = part_of(r.wr_c, part)[...].reshape(WIDTH, WIDTH)
    hidden = nn(normed.astype(LOW), expand) + offset.reshape(1, WIDTH)
    active, slope = smooth(hidden)
    grad_hidden = (nn(delta.astype(LOW), reduce) * slope.astype(WIDE)).astype(LOW)
    r.blocks[4] = nn(r.turned[0, p.z, p.y], grad_hidden)
    r.blocks[5] = nn(r.turned[1, p.z, p.y], active)


def feed_back(r, points):
    size, images = r.size[0], r.images[0]
    r.early[0, 0:10, :] = jnp.zeros((10, WIDTH), WIDE)
    r.offset[...] = jnp.zeros((1, FF), WIDE)

    def add(k, x):
        r.early[0, k - 4 : k - 3, :] += total(x)

    def step(i, at):
        at(0)
        rows = rows_at(i, DENSE)
        branch2 = r.branch2[rows, :]
        unitc, inversec = unit_of(r, 2, rows, r.middle[rows, :] + r.vec[9:10, :] * branch2)
        dn = nn(r.both[rows, :], r.qkwv[...])
        add(14, dn * unitc)
        add(15, dn)
        grad = normalize_back(dn, r.vec_c[0:1, :], unitc, inversec)
        place = iota((DENSE, WIDTH), 0) + i * DENSE
        grad = grad + jnp.where(place < size * images, r.cot[rows, :].astype(WIDE), 0.0)
        add(9, grad * branch2)
        delta = (r.vec[9:10, :] * grad).astype(LOW)
        add(8, delta.astype(WIDE))
        r.d2t[:, rows] = delta.T
        grad_hidden = [
            (nn(delta, whole_of(r.wr)[:, half]) * r.slope[rows, half].astype(WIDE)).astype(LOW)
            for half in WIDE_HALVES
        ]
        for half, part in zip(WIDE_HALVES, grad_hidden, strict=True):
            r.slope[rows, half] = part
            r.offset[:, half] += total(part.astype(WIDE))
        at(1)
        back = nt(whole_of(r.we), r.slope[rows, :]).T
        unit, inverse = unit_of(r, 1, rows, r.middle[rows, :])
        add(6, back * unit)
        add(7, back)
        grad = grad + normalize_back(back, r.vec[6:7, :], unit, inverse)
        r.middle[rows, :] = grad
        add(5, grad * r.branch1[rows, :].astype(WIDE))
        delta = (r.vec[5:6, :] * grad).astype(LOW)
        add(4, delta.astype(WIDE))
        r.d1t[:, rows] = delta.T
        r.dot[:, rows] = nt(r.wback[...], delta).astype(LOW)

    each(ROWS // DENSE, 1, step, points)
    for half in WIDE_HALVES:
        r.we[:, :, :, half] = as_block(nn(r.n2t[...], r.slope[:, half]).astype(LOW))
    points["expand"]()
    for half in WIDE_HALVES:
        r.wr[:, :, :, half] = as_block(nn(r.d2t[...], r.act[:, half]).astype(LOW))
    points["reduce"]()
    for j in range(PARTS):
        r.early[0, 6 + j : 7 + j, :] = r.offset[:, WIDTH * j : WIDTH * (j + 1)]
    r.gwout[...] = nt(r.d1t[...], r.attt[...])


def attend_back(r, points):
    r.dvt[...] = jnp.zeros((WIDTH, ROWS), WIDE)
    r.accp[...] = jnp.zeros((HEADS, HEADS, TILE), WIDE)
    r.accq[...] = jnp.zeros((HEADS, HEADS, TILE), WIDE)

    def step(t, at):
        at(0)
        rows = rows_at(t, TILE)
        grad = r.dot[:, rows].astype(WIDE)
        inverse = r.linv[t]
        place = iota((128, TILE), 0)
        for h in range(HEADS):
            part = slice(TILE * h, TILE * (h + 1))
            post = r.cols[:, 8 + h : 9 + h]
            w = grad * r.un[t, :, part].astype(WIDE)
            r.accp[h] += by_head(w)
            minus = -inverse[:, part] * total(post * w)
            high = minus.astype(LOW).astype(WIDE)
            r.qm[0:WIDTH, part] = (grad * post * inverse[:, part]).astype(LOW)
            extra = jnp.where(place == 0, high, jnp.where(place == 1, minus - high, 0.0))
            r.qm[WIDTH:, part] = extra.astype(LOW)
        q = r.qt[:, rows].astype(WIDE)
        for half in HALVES:
            gp = nn(r.vext[...], r.qm[:, half])
            r.et[t, :, half] = (r.et[t + 1, :, half].astype(WIDE) * gp).astype(LOW)
        r.dvt[...] += nt(r.qm[0:WIDTH, :], r.et[t + 1])
        at(1)
        dq = jnp.zeros((WIDTH, TILE), WIDE)
        for i, half in enumerate(HALVES):
            y = nn(r.kt[...], r.et[t, :, half])
            for k in range(HEADS // 2):
                g = HEADS // 2 * i + k
                part = y[:, TILE * k : TILE * (k + 1)]
                dq = dq + r.cols[:, g : g + 1] * part
                r.accq[g] += by_head(q * part)
        r.dtr[0:WIDTH, rows] = dq.astype(LOW)

    each(STEPS, TOGETHER, step, points)
    r.gsum[...] = nn(r.dot[...], r.hot[...])
    bias = r.cols[:, 16:17]
    for k in range(3):
        r.dvt[...] += (bias * r.gsum[:, k : k + 1]) * r.hott[k : k + 1, :]
    r.dtr[WIDTH : 2 * WIDTH, :] = r.dvt[...].astype(LOW)


def keys_back(r, points):
    for t in range(STEPS):
        if t in points:
            points[t]()
        q = r.qt[:, rows_at(t, TILE)].astype(WIDE)
        mixed = r.qn if t % 2 else r.qm
        for g in range(HEADS):
            mixed[0:WIDTH, TILE * g : TILE * (g + 1)] = (q * r.cols[:, g : g + 1]).astype(LOW)
        part = nt(mixed[0:WIDTH, :], r.et[t])
        r.dkt[...] = part if t == 0 else r.dkt[...] + part
    r.dtr[2 * WIDTH :, :] = r.dkt[...].astype(LOW)


def talking_back(r):
    lane = iota((HEADS, 128), 1)

    def lanes_sum(x):
        return jnp.sum(x, -1, keepdims=True)

    out = jnp.where(lane == 2 * HEADS, lanes_sum(by_head(r.gsum[...] * r.vsum[...])), 0.0)
    for h in range(HEADS):
        out = out + jnp.where(lane == h, lanes_sum(r.accq[h]) * DEPTH ** (-0.5), 0.0)
        out = out + jnp.where(lane == HEADS + h, lanes_sum(r.accp[h]), 0.0)
    r.mid[0, :, WIDTH:] = out


def store_grads(r, j, part, rows):
    lanes = rows.shape[0]
    block = rows.T.astype(LOW).reshape(DEPS, 2, SHARD, lanes)
    r.wa[j, :, :, :, 128 * part : 128 * part + lanes] = block


def weights_early(r):
    whole = nn(r.dtr[0 : 2 * WIDTH, :], r.n1[...])
    query, value = whole[0:WIDTH], whole[WIDTH:]
    gwout = r.gwout
    store_grads(r, 0, 0, jnp.concatenate([query[0:288], gwout[0:96, :]], 0))
    store_grads(r, 1, 0, jnp.concatenate([query[288:], gwout[96:128, :]], 0))
    store_grads(r, 2, 0, jnp.concatenate([value[0:96], gwout[192:224, :]], 0))
    store_grads(r, 3, 0, jnp.concatenate([value[96:], gwout[288:, :]], 0))


def weights_late(r):
    keys = nn(r.dtr[2 * WIDTH :, :], r.n1[...])
    store_grads(r, 1, 1, jnp.concatenate([r.gwout[128:192, :], keys[0:192]], 0))
    store_grads(r, 2, 1, jnp.concatenate([r.gwout[224:288, :], keys[192:]], 0))


def project_back_start(r):
    ones = jnp.ones((8, ROWS), LOW)
    r.mid[0, 0:1, 0:WIDTH] = nt(ones, r.dtr[0:WIDTH, :])[0:1]
    r.mid[0, 1:2, 0:WIDTH] = nt(ones, r.dtr[WIDTH : 2 * WIDTH, :])[0:1]
    r.dvt[...] = nn(r.wfull[:, 0 : 2 * WIDTH], r.dtr[0 : 2 * WIDTH, :])


def project_back(r):
    r.sums[...] = jnp.zeros((8, WIDTH), WIDE)

    def step(i, c):
        rows = rows_at(i, DENSE)
        back = (r.dvt[:, rows] + nn(r.wfull[:, 2 * WIDTH :], r.dtr[2 * WIDTH :, rows])).T
        unit, inverse = unit_of(r, 0, rows, r.patches[rows, :].astype(WIDE))
        r.sums[0:1, :] += total(back * unit)
        r.sums[1:2, :] += total(back)
        r.middle[rows, :] = r.middle[rows, :] + normalize_back(
            back, r.vec[0:1, :], unit, inverse
        )
        return c

    lax.fori_loop(0, ROWS // DENSE, step, 0)
    for k in range(2):
        for n in range(3):
            r.late[0, 3 * k + n : 3 * k + n + 1, :] = r.sums[k : k + 1, 128 * n : 128 * n + 128]


MESH = pl.DeviceIdType.MESH
CHUNKS = ("a", "e", "r", "ac", "ec", "rc")
SHAPE = (PARTS, DEPS, 2, SHARD, WIDTH)
JOINED = (DEPS, 2, SHARD, PARTS * WIDTH)


class Place:
    def __init__(self, inner):
        self.inner = inner
        dp, tensor = lax.axis_index("dp"), lax.axis_index("tensor")
        self.rest = (lax.rem(dp, inner[0]), lax.rem(tensor, inner[1]))
        dp, tensor = dp // inner[0], tensor // inner[1]
        self.z, self.y = dp // 2, lax.rem(dp, 2)
        self.x, self.core = tensor // 2, lax.rem(tensor, 2)
        self.a = self.x + self.core * (self.y - self.x)
        self.b = self.y + self.core * (self.x - self.y)

    def xy(self, a, b):
        return a + self.core * (b - a), b + self.core * (a - b)

    def device(self, z, y, x, core):
        return (
            (z * 2 + y) * self.inner[0] + self.rest[0],
            (x * 2 + core) * self.inner[1] + self.rest[1],
        )

    def around(self, d):
        return lax.rem(self.z + d, DEPS)

    def z_peer(self, d):
        return self.device(self.around(d), self.y, self.x, self.core)

    def a_peer(self):
        x, y = self.xy(1 - self.a, self.b)
        return self.device(self.z, y, x, self.core)

    def b_peer(self):
        x, y = self.xy(self.a, 1 - self.b)
        return self.device(self.z, y, x, self.core)

    def x_peer(self):
        return self.device(self.z, self.y, 1 - self.x, self.core)

    def y_peer(self):
        return self.device(self.z, 1 - self.y, self.x, self.core)

    def plane_peer(self, a, b):
        x, y = self.xy(self.a + a * (1 - 2 * self.a), self.b + b * (1 - 2 * self.b))
        return self.device(self.z, y, x, self.core)

    def near(self, k):
        x = 1 - self.x if k & 4 else self.x
        y = 1 - self.y if k & 2 else self.y
        return self.device(self.z, y, x, 1 - self.core if k & 1 else self.core)

    def core_peer(self):
        return self.device(self.z, self.y, self.x, 1 - self.core)


def remote(src, dst, sems, k, device):
    return pltpu.make_async_remote_copy(
        src_ref=src,
        dst_ref=dst,
        send_sem=sems[0].at[k],
        recv_sem=sems[1].at[k],
        device_id=device,
        device_id_type=MESH,
    )


def part_of(w, j, z=slice(None), y=slice(None)):
    if len(w.shape) == 5:
        return w.at[j, z, y]
    return w.at[z, y, :, pl.ds(pl.multiple_of(j * WIDTH, 128), WIDTH)]


class Gather:
    def __init__(self, place, w, sems, base):
        self.p, self.w, self.sems, self.base = place, w, sems, base

    def copy(self, k, where, device):
        ref = part_of(self.w, *where)
        return remote(ref, ref, self.sems, self.base + k, device)

    def z_copies(self, back):
        p = self.p
        out = []
        for d in (1, 2, 3):
            z = p.around(DEPS - d) if back else p.z
            out.append(self.copy(d - 1, (p.x * 2 + p.core, z, p.y), p.z_peer(d)))
        return out

    def b_copies(self, back):
        p = self.p
        x, y = p.xy(p.a, 1 - p.b) if back else (p.x, p.y)
        return [self.copy(3, (x * 2 + p.core, slice(None), y), p.b_peer())]

    def a_copies(self, back):
        p = self.p
        a = 1 - p.a if back else p.a
        out = []
        for k, b in enumerate((p.b, 1 - p.b)):
            x, y = p.xy(a, b)
            out.append(self.copy(4 + k, (x * 2 + p.core, slice(None), y), p.a_peer()))
        return out

    def core_copies(self, back):
        p = self.p
        core = 1 - p.core if back else p.core
        return [self.copy(6 + x, (x * 2 + core,), p.core_peer()) for x in (0, 1)]

    def start(self, name):
        for copy in getattr(self, name + "_copies")(False):
            copy.start()

    def wait(self, name):
        for copy in getattr(self, name + "_copies")(True):
            copy.wait_recv()

    def drain(self):
        for name in ("z", "b", "a", "core"):
            for copy in getattr(self, name + "_copies")(False):
                copy.wait_send()


class QuickGather(Gather):
    def piece(self, a, b, back):
        p = self.p
        if back:
            a, b = p.a + a * (1 - 2 * p.a), p.b + b * (1 - 2 * p.b)
        else:
            a, b = p.a, p.b
        return p.xy(a, b)

    def plane_copy(self, q, d, back):
        p = self.p
        a, b = ((0, 1), (1, 0), (1, 1))[q]
        x, y = self.piece(a, b, back)
        where = (x * 2 + p.core, p.around(DEPS - d), y)
        return self.copy(3 + 4 * q + d, where, p.plane_peer(a, b))

    def core_copy(self, q, back):
        p = self.p
        a, b = ((0, 0), (0, 1), (1, 0), (1, 1))[q]
        x, y = self.piece(a, b, True)
        core = 1 - p.core if back else p.core
        return self.copy(15 + q, (x * 2 + core, slice(None), y), p.core_peer())

    def begin(self):
        for copy in self.z_copies(False):
            copy.start()
        for q in range(3):
            self.plane_copy(q, 0, False).start()

    def forward(self):
        for d, copy in zip((1, 2, 3), self.z_copies(True), strict=True):
            copy.wait_recv()
            for q in range(3):
                self.plane_copy(q, d, False).start()
        self.core_copy(0, False).start()

    def across(self):
        for q in range(3):
            for d in range(4):
                self.plane_copy(q, d, True).wait_recv()
            self.core_copy(1 + q, False).start()

    def end(self):
        for q in range(4):
            self.core_copy(q, True).wait_recv()

    def drain(self):
        for copy in self.z_copies(False):
            copy.wait_send()
        for q in range(3):
            for d in range(4):
                self.plane_copy(q, d, False).wait_send()
        for q in range(4):
            self.core_copy(q, False).wait_send()


class Scatter:
    def __init__(self, place, g, ins, sems, base):
        self.p, self.g, self.sems, self.base = place, g, sems, base
        self.c_in, self.a_in, self.b_in, self.z_in = ins

    def copies(self, name):
        p = self.p
        if name == "core":
            return [
                remote(part_of(self.g, x * 2 + 1 - p.core), self.c_in.at[x], self.sems, self.base + x, p.core_peer())
                for x in (0, 1)
            ]
        if name == "a":
            out = []
            for b in (0, 1):
                x, y = p.xy(1 - p.a, b)
                out.append(
                    remote(self.c_in.at[x, :, y], self.a_in.at[b], self.sems, self.base + 2 + b, p.a_peer())
                )
            return out
        if name == "b":
            return [remote(self.a_in.at[1 - p.b], self.b_in, self.sems, self.base + 4, p.b_peer())]
        return [
            remote(self.b_in.at[p.around(d)], self.z_in.at[d - 1], self.sems, self.base + 4 + d, p.z_peer(d))
            for d in (1, 2, 3)
        ]

    def start(self, name):
        for copy in self.copies(name):
            copy.start()

    def finish(self, name):
        p = self.p
        for copy in self.copies(name):
            copy.wait_recv()
        if name == "core":
            for x in (0, 1):
                self.c_in[x] += part_of(self.g, x * 2 + p.core)[...]
        elif name == "a":
            for b in (0, 1):
                x, y = p.xy(p.a, b)
                self.a_in[b] += self.c_in[x, :, y]
        elif name == "b":
            self.b_in[...] += self.a_in[p.b]

    def result(self):
        out = self.b_in[self.p.z].astype(WIDE)
        for d in range(3):
            out = out + self.z_in[d].astype(WIDE)
        return out

    def drain(self):
        for name in ("core", "a", "b", "z"):
            for copy in self.copies(name):
                copy.wait_send()


class QuickScatter(Scatter):
    def __init__(self, place, g, ins, sems, base, lane):
        super().__init__(place, g, ins, sems, base)
        self.lanes = pl.ds(lane, 128)

    def copies(self, name):
        p, base, lanes = self.p, self.base, self.lanes
        every = slice(None)
        out = []
        if name == "core":
            for x in (0, 1):
                src = self.g.at[x * 2 + 1 - p.core, :, :, :, lanes]
                dst = self.c_in.at[x, :, :, :, lanes]
                out.append(remote(src, dst, self.sems, base + x, p.core_peer()))
        elif name == "a":
            for q, (a, b) in enumerate(((0, 1), (1, 0), (1, 1))):
                x, y = p.xy(p.a + a * (1 - 2 * p.a), p.b + b * (1 - 2 * p.b))
                src = self.c_in.at[x, :, y, :, lanes]
                dst = self.a_in.at[q, :, :, lanes]
                out.append(remote(src, dst, self.sems, base + 2 + q, p.plane_peer(a, b)))
        elif name == "z":
            for d in (1, 2, 3):
                src = self.b_in.at[p.around(d), :, lanes]
                dst = self.z_in.at[d - 1, :, lanes]
                out.append(remote(src, dst, self.sems, base + 4 + d, p.z_peer(d)))
        return out

    def finish(self, name):
        p, lanes = self.p, self.lanes
        for copy in self.copies(name):
            copy.wait_recv()
        if name == "core":
            for x in (0, 1):
                self.c_in[x, :, :, :, lanes] += self.g[x * 2 + p.core, :, :, :, lanes]
        elif name == "a":
            mine = self.c_in[p.x, :, p.y, :, lanes].astype(WIDE)
            for q in range(3):
                mine = mine + self.a_in[q, :, :, lanes].astype(WIDE)
            self.b_in[:, :, lanes] = mine.astype(LOW)

    def result(self):
        out = self.b_in[self.p.z, :, self.lanes].astype(WIDE)
        for d in range(3):
            out = out + self.z_in[d, :, self.lanes].astype(WIDE)
        return out


class PartScatter(QuickScatter):
    def __init__(self, place, g, ins, sems, base, owner):
        super().__init__(place, g, ins, sems, base, 128)
        self.lanes = pl.ds(128, 256)
        self.owner = owner

    def core_copy(self, back):
        p = self.p
        x = self.owner if back else 1 - self.owner
        src = self.g.at[x * 2 + 1 - p.core, :, :, :, self.lanes]
        return remote(src, self.c_in.at[x, :, :, :, self.lanes], self.sems, self.base, p.core_peer())

    def plane_copy(self, k):
        p = self.p
        y = 1 - p.y if k & 1 else p.y
        src = self.c_in.at[self.owner, :, y, :, self.lanes]
        dst = self.a_in.at[k - 1, :, :, self.lanes]
        peer = (None, p.y_peer, p.x_peer, lambda: p.plane_peer(1, 1))[k]()
        return remote(src, dst, self.sems, self.base + k, peer)

    def owned(self, todo):
        pl.when(self.p.x == self.owner)(todo)

    def others(self, todo):
        pl.when(self.p.x != self.owner)(todo)

    def start(self, name):
        if name == "core":
            self.core_copy(False).start()
        elif name == "a":
            self.owned(lambda: self.plane_copy(1).start())

            def both():
                self.plane_copy(2).start()
                self.plane_copy(3).start()

            self.others(both)
        else:
            self.owned(lambda: QuickScatter.start(self, name))

    def finish(self, name):
        p, lanes = self.p, self.lanes
        if name == "core":
            self.core_copy(True).wait_recv()
            self.c_in[self.owner, :, :, :, lanes] += self.g[self.owner * 2 + p.core, :, :, :, lanes]
            return

        def todo():
            if name == "z":
                QuickScatter.finish(self, name)
                return
            for k in (1, 2, 3):
                self.plane_copy(k).wait_recv()
            mine = self.c_in[self.owner, :, p.y, :, lanes].astype(WIDE)
            for q in range(3):
                mine = mine + self.a_in[q, :, :, lanes].astype(WIDE)
            self.b_in[:, :, lanes] = mine.astype(LOW)

        self.owned(todo)

    def drain(self):
        self.core_copy(False).wait_send()

        def owned():
            self.plane_copy(1).wait_send()
            for copy in self.copies("z"):
                copy.wait_send()

        def others():
            self.plane_copy(2).wait_send()
            self.plane_copy(3).wait_send()

        self.owned(owned)
        self.others(others)


class SlowTotal:
    def __init__(self, place, own, got, sems, base):
        self.p, self.own, self.got, self.sems, self.base = place, own, got, sems, base

    def copies(self, k):
        p = self.p
        if k < 3:
            device = (p.core_peer, p.x_peer, p.y_peer)[k]()
            return [remote(self.own.at[k], self.got.at[k], self.sems, self.base + k, device)]
        return [
            remote(self.own.at[3], self.got.at[3 + d], self.sems, self.base + 2 + d, p.z_peer(d))
            for d in (1, 2, 3)
        ]

    def start(self, k):
        for copy in self.copies(k):
            copy.start()

    def finish(self, k):
        p = self.p
        for copy in self.copies(k):
            copy.wait_recv()
        if k < 3:
            self.own[k + 1] = self.own[k] + self.got[k]
            return None
        self.got[3] = self.own[3]
        out = None
        for z in range(DEPS):
            part = self.got[3 + lax.rem(p.z - z + DEPS, DEPS)]
            out = part if z == 0 else out + part
        return out

    def drain(self):
        for k in range(4):
            for copy in self.copies(k):
                copy.wait_send()


class Total:
    def __init__(self, place, own, got, sems, base):
        self.p, self.own, self.got, self.sems, self.base = place, own, got, sems, base

    def copies(self, k):
        p = self.p
        if k == 0:
            return [
                remote(self.own.at[0], self.got.at[n], self.sems, self.base + n, p.near(n))
                for n in range(1, 8)
            ]
        return [
            remote(self.own.at[1], self.got.at[8 + d], self.sems, self.base + 7 + d, p.z_peer(d))
            for d in (1, 2, 3)
        ]

    def start(self, k):
        for copy in self.copies(k):
            copy.start()

    def finish(self, k):
        p = self.p
        for copy in self.copies(k):
            copy.wait_recv()
        self.got[8 * k] = self.own[k]
        out = None
        if k == 0:
            for n in range(8):
                x = 1 - p.x if n & 4 else p.x
                y = 1 - p.y if n & 2 else p.y
                core = 1 - p.core if n & 1 else p.core
                part = self.got[x * 4 + y * 2 + core]
                out = part if n == 0 else out + part
            self.own[1] = out
            return None
        for z in range(DEPS):
            part = self.got[8 + lax.rem(p.z - z + DEPS, DEPS)]
            out = part if z == 0 else out + part
        return out

    def drain(self):
        for k in range(2):
            for copy in self.copies(k):
                copy.wait_send()


INPUTS = ("size", "images", "patches_in", "cot_in", "classes", "class_cot")
INPUTS += ("entry", "exit", "expand", "reduce", "entry_c", "exit_c", "expand_c", "reduce_c")
INPUTS += ("vec", "talking", "off", "vec_c", "off_c")
DIRECT = ("patches_in", "cot_in", "expand", "reduce", "expand_c", "reduce_c")
OUTPUTS = dict(
    patch_result=((ROWS, WIDTH), LOW),
    patch_grad=((ROWS, WIDTH), WIDE),
    class_result=((3, WIDTH), LOW),
    class_grad=((3, WIDTH), WIDE),
    blocks=((6, SHARD, WIDTH), WIDE),
    rows_early=((24, WIDTH), WIDE),
    rows_mid=((8, 512), WIDE),
    rows_late=((8, 128), WIDE),
)
COMM = {n: (SHAPE, LOW) for n in ("wa", "wa_c")}
COMM |= {n: (JOINED, LOW) for n in ("we", "wr", "we_c", "wr_c")}
COMM |= dict(
    wf=((PARTS, DEPS, 2, 16, WIDTH), LOW),
    turned=((2, DEPS, 2, SHARD, 256), LOW),
    early=((4, 24, WIDTH), WIDE),
    early_in=((7, 24, WIDTH), WIDE),
    mid=((2, 8, 512), WIDE),
    mid_in=((12, 8, 512), WIDE),
    late=((2, 8, 128), WIDE),
    late_in=((12, 8, 128), WIDE),
)
for _k in ("a", "e", "r", "ac"):
    COMM["c_in_" + _k] = ((2, DEPS, 2, SHARD, WIDTH), LOW)
    COMM["a_in_" + _k] = ((3 if _k == "a" else 2, DEPS, SHARD, WIDTH), LOW)
    COMM["b_in_" + _k] = ((DEPS, SHARD, WIDTH), LOW)
    COMM["z_in_" + _k] = ((3, SHARD, WIDTH), LOW)
SEMS = dict(g_send=67, g_recv=67, s_send=64, s_recv=64, t_send=28, t_recv=28, out=2, into=6)


def greet(p):
    barrier = pltpu.get_barrier_semaphore()
    peers = [p.z_peer(d) for d in (1, 2, 3)] + [p.near(n) for n in range(1, 8)]
    for peer in peers:
        pl.semaphore_signal(barrier, inc=1, device_id=peer, device_id_type=MESH)
    return lambda: pl.semaphore_wait(barrier, len(peers))


def layer_kernel(inner, *refs):
    r = Refs(**dict(zip([*INPUTS, *OUTPUTS, *SCRATCH, *COMM, *SEMS], refs, strict=True)))
    p = Place(inner)
    mine = p.x * 2 + p.core
    weights = dict(a=r.wa, e=r.we, r=r.wr, ac=r.wa_c, ec=r.we_c, rc=r.wr_c)
    grads = weights
    first = QuickGather(p, r.wa, (r.g_send, r.g_recv), 40)
    gathers, scatters = {}, {}
    for i, k in enumerate(CHUNKS):
        if k != "a":
            gathers[k] = Gather(p, weights[k], (r.g_send, r.g_recv), 8 * (i - 1))
        if k in ("ec", "rc"):
            continue
        ins = [getattr(r, n + "_in_" + k) for n in ("c", "a", "b", "z")]
        if k == "a":
            sems = (r.s_send, r.s_recv)
            last = [
                QuickScatter(p, r.wa, ins, sems, 40, 0),
                PartScatter(p, r.wa, ins, sems, 48, p.core),
                PartScatter(p, r.wa, ins, sems, 56, 1 - p.core),
            ]
        else:
            scatters[k] = Scatter(p, grads[k], ins, (r.s_send, r.s_recv), 8 * (i - 1))
    gathers["cf"] = Gather(p, r.wf, (r.g_send, r.g_recv), 59)
    early = SlowTotal(p, r.early, r.early_in, (r.t_send, r.t_recv), 0)
    mid = Total(p, r.mid, r.mid_in, (r.t_send, r.t_recv), 6)
    late = Total(p, r.late, r.late_in, (r.t_send, r.t_recv), 17)

    def go(*moves):
        def todo():
            for k, old, new in moves:
                if old:
                    gathers[k].wait(old)
                if new:
                    gathers[k].start(new)

        return todo

    def back(*moves):
        def todo():
            for k, old, new in moves:
                if k == "cf":
                    go((k, old, new))()
                    continue
                what = scatters.get(k) or early
                if old is not None:
                    what.finish(old)
                if new is not None:
                    what.start(new)

        return todo

    enter = greet(p)
    r.wa[mine, p.z, p.y] = jnp.concatenate([r.entry[...], r.exit[...]], 1)
    load = [
        pltpu.make_async_copy(r.patches_in, r.patches, r.into.at[0]),
        pltpu.make_async_copy(r.cot_in, r.cot, r.into.at[1]),
    ]
    for k, (w, src) in enumerate(
        ((r.we, r.expand), (r.wr, r.reduce), (r.we_c, r.expand_c), (r.wr_c, r.reduce_c))
    ):
        load.append(pltpu.make_async_copy(src, part_of(w, mine, p.z, p.y), r.into.at[2 + k]))
    for copy in load:
        copy.start()
    enter()
    first.begin()
    r.wa_c[mine, p.z, p.y] = jnp.concatenate([r.entry_c[...], r.exit_c[...]], 1)
    columns(r)
    for copy in load[2:]:
        copy.wait()
    first.forward()
    go(("e", None, "z"), ("r", None, "z"))()
    masks(r)
    load[0].wait()
    norm_first(r)
    r.early[0] = jnp.zeros((24, WIDTH), WIDE)
    r.mid[0] = jnp.zeros((8, 512), WIDE)
    r.late[0] = jnp.zeros((8, 128), WIDE)
    first.across()
    first.end()
    go(("e", "z", "b"), ("ac", None, "z"), ("ec", None, "z"), ("rc", None, "z"), ("r", "z", "b"))()
    project(r)
    attend(r, gather_points(go))
    gathers["e"].wait("core")
    gathers["r"].wait("core")
    feed(r, feed_points(go))
    out_result = pltpu.make_async_copy(r.result, r.patch_result, r.out.at[0])
    out_result.start()
    def begin_class():
        gathers["ac"].wait("core")
        load[1].wait()

    def begin_scores():
        gathers["rc"].wait("a")
        gathers["rc"].start("core")

    def begin_feed():
        gathers["ec"].wait("core")

    def begin_reduce():
        gathers["rc"].wait("core")
        for k in ("a", *CHUNKS[1:]):
            (first if k == "a" else gathers[k]).drain()

    def share(rows):
        r.wf[mine, p.z, p.y] = rows
        gathers["cf"].start("z")

    classes(r, (begin_class, begin_feed, share, begin_scores, begin_reduce))
    scatters["ac"].start("core")
    ready = {n: functools.partial(scatters[n[0]].start, "core") for n in ("expand", "reduce")}
    feed_back(r, feed_back_points(back) | ready)
    attend_back(r, attend_back_points(back))
    weights_early(r)
    last[0].start("core")
    last[1].start("core")
    talking_back(r)
    project_back_start(r)
    mid.start(0)
    keys_back(r, keys_points(last, mid, back))
    weights_late(r)
    last[2].start("core")
    project_back(r)
    last[2].finish("core")
    last[2].start("a")
    late.start(0)
    out_grad = pltpu.make_async_copy(r.middle, r.patch_grad, r.out.at[1])
    out_grad.start()
    for n in (0, 1):
        last[n].finish("a")
        last[n].start("z")
    gathers["cf"].wait("core")
    class_weights(r, p)
    for i, k in ((1, "e"), (2, "r"), (3, "ac")):
        scatters[k].finish("z")
        r.blocks[i] = scatters[k].result()
    r.rows_early[...] = early.finish(3)
    late.finish(0)
    late.start(1)
    r.rows_mid[...] = mid.finish(1)
    last[2].finish("a")
    last[2].start("z")
    r.rows_late[...] = late.finish(1)
    for n in range(3):
        last[n].finish("z")
    r.blocks[0, :, 0:128] = last[0].result()
    r.blocks[0, :, 128:] = last[1].result()
    out_result.wait()
    out_grad.wait()
    for k in ("e", "r", "ac"):
        scatters[k].drain()
    gathers["cf"].drain()
    for k in last:
        k.drain()
    early.drain()
    mid.drain()
    late.drain()


def gather_points(go):
    return {
        0: go(("e", "b", "a")),
        2: go(("ac", "z", "b")),
        3: go(("r", "b", "a")),
        5: go(("e", "a", "core"), ("ec", "z", "b")),
        6: go(("ac", "b", "a")),
        8: go(("r", "a", "core"), ("rc", "z", "b")),
        9: go(("ec", "b", "a")),
        11: go(("ac", "a", "core")),
    }


def feed_points(go):
    return {0: go(("rc", "b", "a")), 2: go(("ec", "a", "core"))}


def keys_points(last, mid, back):
    def core(n):
        def todo():
            last[n].finish("core")
            last[n].start("a")

        return todo

    def middle():
        mid.finish(0)
        mid.start(1)

    return {0: core(0), 1: core(1), 4: middle}


def feed_back_points(back):
    return {
        0: back(("cf", "z", "b")),
        2: back(("cf", "b", "a"), ("ac", "core", "a")),
    }


def attend_back_points(back):
    return {
        0: back(("cf", "a", "core")),
        2: back(("ac", "a", "b"), ("e", "core", "a")),
        4: back(("r", "core", "a"), ("ac", "b", "z"), ("early", None, 0)),
        6: back(("e", "a", "b"), ("early", 0, 1)),
        8: back(("r", "a", "b"), ("e", "b", "z"), ("early", 1, 2)),
        10: back(("r", "b", "z"), ("early", 2, 3)),
    }


def finish_kernel(inner, *refs):
    r = Refs(**dict(zip([*(n + "_in" for n in OUTPUTS), *FINAL], refs, strict=True)))
    r.patch_result[...] = r.patch_result_in[...]
    r.patch_grad[...] = r.patch_grad_in[...]
    r.class_result[...] = r.class_result_in[...]
    r.class_grad[...] = r.class_grad_in[...]
    r.g_entry_c[...] = r.blocks_in[3, :, 0:COLS]
    r.g_exit_c[...] = r.blocks_in[3, :, COLS:]
    part = lax.axis_index("tensor") // inner[1]
    block = r.blocks_in[0]
    one, two, three = block[:, 0:96], block[:, 96:192], block[:, 192:]
    outer = (part == 0) | (part == 3)
    inside = jnp.where(
        part == 1, jnp.concatenate([one, three], 1), jnp.concatenate([three, one], 1)
    )
    r.g_entry[...] = jnp.where(outer, block[:, 0:COLS], inside)
    r.g_exit[...] = jnp.where(outer, block[:, COLS:], two)
    for i, c in ((0, ""), (3, "_c")):
        getattr(r, "g_expand" + c)[...] = r.blocks_in[i + 1]
        getattr(r, "g_reduce" + c)[...] = r.blocks_in[i + 2]
    for k in range(2):
        for n in range(3):
            r.g_vec[k : k + 1, 128 * n : 128 * n + 128] = r.rows_late_in[3 * k + n : 3 * k + n + 1, :]
    r.g_vec[2:4, :] = r.rows_mid_in[0:2, 0:WIDTH]
    r.g_vec[4:10, :] = r.rows_early_in[0:6, :]
    r.g_vec_c[...] = r.rows_early_in[10:20, :]
    for j in range(PARTS):
        part = slice(WIDTH * j, WIDTH * (j + 1))
        r.g_off[part] = r.rows_early_in[6 + j : 7 + j, :].reshape(WIDTH)
        r.g_off_c[part] = r.rows_early_in[20 + j : 21 + j, :].reshape(WIDTH)
    talk = r.rows_mid_in[:, WIDTH:]
    turned = jnp.concatenate([talk, jnp.zeros((120, 128), WIDE)], 0).T
    lane = iota((8, 128), 1)
    moved = pltpu.roll(turned[8:16], 8, 1)
    r.g_talking[...] = jnp.where((lane >= 8) & (lane < 16), moved, talk)[:, 0:17]


FINAL = dict(
    patch_result=((ROWS, WIDTH), LOW),
    class_result=((3, WIDTH), LOW),
    patch_grad=((ROWS, WIDTH), WIDE),
    class_grad=((3, WIDTH), WIDE),
    g_entry=((SHARD, COLS), WIDE),
    g_exit=((SHARD, 96), WIDE),
    g_expand=((SHARD, WIDTH), WIDE),
    g_reduce=((SHARD, WIDTH), WIDE),
    g_vec=((10, WIDTH), WIDE),
    g_talking=((8, 17), WIDE),
    g_off=((FF,), WIDE),
    g_entry_c=((SHARD, COLS), WIDE),
    g_exit_c=((SHARD, 96), WIDE),
    g_expand_c=((SHARD, WIDTH), WIDE),
    g_reduce_c=((SHARD, WIDTH), WIDE),
    g_vec_c=((10, WIDTH), WIDE),
    g_off_c=((FF,), WIDE),
)


def layers(inner, *args):
    smem = pl.BlockSpec(memory_space=pltpu.SMEM)
    vmem = pl.BlockSpec(memory_space=pltpu.VMEM)
    hbm = pl.BlockSpec(memory_space=pl.ANY)
    sems = [pltpu.SemaphoreType.DMA((n,)) for n in SEMS.values()]
    mid = pl.pallas_call(
        functools.partial(layer_kernel, inner),
        out_shape=[jax.ShapeDtypeStruct(*s) for s in OUTPUTS.values()],
        in_specs=[smem, smem] + [hbm if n in DIRECT else vmem for n in INPUTS[2:]],
        out_specs=[hbm, hbm] + [vmem] * (len(OUTPUTS) - 2),
        scratch_shapes=[pltpu.VMEM(*s) for s in (SCRATCH | COMM).values()] + sems,
        compiler_params=pltpu.CompilerParams(
            vmem_limit_bytes=63 * 2**20, collective_id=0, has_side_effects=True
        ),
    )(*args)
    out = pl.pallas_call(
        functools.partial(finish_kernel, inner),
        out_shape=[jax.ShapeDtypeStruct(*s) for s in FINAL.values()],
        in_specs=[vmem] * len(OUTPUTS),
        out_specs=[vmem] * len(FINAL),
    )(*mid)
    return dict(zip(FINAL, out, strict=True))


def groups(axis, inner):
    return [[inner * k + i for i in range(inner)] for k in range(lax.axis_size(axis) // inner)]


def widen(x, inner, dims):
    for axis, n, dim in zip(("dp", "tensor"), inner, dims, strict=True):
        if n > 1:
            x = lax.all_gather(x, axis, axis=dim, tiled=True, axis_index_groups=groups(axis, n))
    return x


def narrow(x, inner, dims):
    for axis, n, dim in zip(("dp", "tensor"), inner, dims, strict=True):
        if n > 1:
            x = lax.psum_scatter(
                x, axis, scatter_dimension=dim, tiled=True, axis_index_groups=groups(axis, n)
            )
    return x


def whole(x, inner):
    for axis, n in zip(("dp", "tensor"), inner, strict=True):
        if n > 1:
            x = lax.psum(x, axis, axis_index_groups=groups(axis, n))
    return x


KINDS = ((0, 1),) * 4


def local(
    patches,
    classes,
    group_size,
    image_count,
    self_entry,
    self_exit,
    self_expand,
    self_reduce,
    self_vectors,
    self_talking,
    self_offset,
    class_entry,
    class_exit,
    class_expand,
    class_reduce,
    class_vectors,
    class_offset,
    patch_cotangent,
    class_cotangent,
):
    inner = (lax.axis_size("dp") // 8, lax.axis_size("tensor") // 4)
    weights = [
        widen(w, inner, dims)
        for w, dims in zip(
            (
                self_entry,
                self_exit,
                self_expand,
                self_reduce.T,
                class_entry,
                class_exit,
                class_expand,
                class_reduce.T,
            ),
            KINDS * 2,
            strict=True,
        )
    ]
    out = layers(
        inner,
        group_size,
        image_count,
        patches,
        patch_cotangent,
        classes,
        class_cotangent,
        *weights,
        self_vectors,
        self_talking.T,
        self_offset,
        class_vectors,
        class_offset,
    )
    names = ("entry", "exit", "expand", "reduce")
    own = [narrow(out["g_" + n], inner, dims) for n, dims in zip(names, KINDS, strict=True)]
    own_c = [narrow(out["g_" + n + "_c"], inner, dims) for n, dims in zip(names, KINDS, strict=True)]
    return (
        out["patch_result"],
        out["class_result"],
        out["patch_grad"],
        out["class_grad"],
        *own[:3],
        own[3].T,
        whole(out["g_vec"], inner),
        whole(out["g_talking"], inner).T,
        whole(out["g_off"], inner),
        *own_c[:3],
        own_c[3].T,
        whole(out["g_vec_c"], inner),
        whole(out["g_off_c"], inner),
    )


def solution(mesh):
    both = P(("dp", "tensor"), None)
    weights = (P("dp", "tensor"), P("dp", "tensor"), P("dp", "tensor"), P("tensor", "dp"))
    return jax.shard_map(
        local,
        mesh=mesh,
        in_specs=(
            both,
            both,
            P(("dp", "tensor")),
            P(("dp", "tensor")),
            *weights,
            P(),
            P(),
            P(),
            *weights,
            P(),
            P(),
            both,
            both,
        ),
        out_specs=(both, both, both, both, *weights, P(), P(), P(), *weights, P(), P()),
        check_vma=False,
    )
```
